32 devices in a mesh: alpha: 2 (over y), beta: 16 (over z, x, core).
Axes of the slice: x: 2, y: 2, z: 4, core: 2. Of those that a mesh axis runs over, the one named last changes fastest.
Arguments:
- ci_vectors: bfloat16 [8, 4096, 4096], P(None, 'alpha', 'beta'), may hold values from -6 to 6
- alpha_blocks: bfloat16 [32, 16, 128, 128], P('alpha'), may hold values from -0.125 to 0.125
- alpha_cols: int32 [32, 16], P('alpha'), may hold values from 0 to 31, all different within a row
- beta_blocks: bfloat16 [32, 16, 128, 128], P('beta'), may hold values from -0.125 to 0.125
- beta_cols: int32 [32, 16], P('beta'), may hold values from 0 to 31, all different within a row
- diagonal: float32 [4096, 4096], P('alpha', 'beta'), may hold values from -1 to 3
Outputs:
- sigma_vectors: bfloat16 [8, 4096, 4096], P(None, 'alpha', 'beta')
The draws below stay inside these ranges and needn't reach their ends.
Inputs may be any that keep to these rules, and one draw needn't show every extreme that they name: `alpha_cols`: each block-row names 16 different block-columns. `beta_cols`: each block-row names 16 different block-columns.
All inputs are finite; a program needn't handle non-finite values.
Results may differ from the reference program's by a relative error of at most 0.001.
Values may be sent and summed in bfloat16 or wider, within the bound.
No kernel may reach another device: no remote copies, remote signals or barrier semaphores. Data moves between devices by JAX's collectives and lax.ppermute only.
A program may use at most 320 MiB of HBM per device.

```python
import jax
import jax.numpy as jnp
from jax import lax

NA = 4096
NB = 4096
BLK = 128
KB = 16
NV = 8
NBLK_A = 32
NBLK_B = 32


def level_of(stream_key, extent, split, smallest, high):
    def one(position, shards_of):
        heights = jax.random.uniform(jax.random.fold_in(jax.random.fold_in(stream_key, 6), position), (shards_of,), jnp.float32, smallest / len(split), high / len(split))
        return jnp.repeat(jnp.exp(heights), extent[position] // shards_of).reshape((-1,) + (1,) * (len(extent) - position - 1))

    factor_of = one(*split[0])
    for cut in split[1:]:
        factor_of = factor_of * one(*cut)
    return factor_of


def choose_distinct(key, rows, count, top, lift):
    sequence = jax.random.permutation(jax.random.fold_in(key, 1), count)
    pull = sequence
    for power in range(3):
        pull = pull * pull // count
    pull = pull * lift // count
    tickets = jax.random.randint(jax.random.fold_in(key, 2), (rows, count), 0, 4096) + pull
    holders = jax.random.permutation(jax.random.fold_in(key, 3), rows)[jnp.arange(count) % rows]
    tickets = jnp.where(jnp.arange(rows)[:, None] == holders[None, :], 1 << 14, tickets)
    score = tickets * count + jnp.arange(count)
    return lax.top_k(score.astype(jnp.int32), top)[1].astype(jnp.int32)


def scatter_about(stream_key, extent, width, most, split=(), kind=jnp.bfloat16):
    entries = jax.random.normal(stream_key, extent, jnp.float32) * width
    if len(split) > 0:
        entries = level_of(stream_key, extent, split, -0.22, 0.18) * entries
    return jnp.clip(entries, min=-most, max=most).astype(kind)


def setup_inputs(seed: int = 0) -> dict:
    seeds = jax.random.split(jax.random.key(seed), 7)
    ci_vectors = scatter_about(seeds[0], (NV, NA, NB), 1.0, 6.0, ((1, 2), (2, 16)))
    alpha_blocks = scatter_about(seeds[1], (NBLK_A, KB, BLK, BLK), (KB * BLK) ** -0.5, 0.125, ((0, 2),))
    alpha_cols = choose_distinct(seeds[2], NBLK_A, NBLK_A, KB, 0)
    beta_blocks = scatter_about(seeds[3], (NBLK_B, KB, BLK, BLK), (KB * BLK) ** -0.5, 0.125, ((0, 16),))
    beta_cols = choose_distinct(seeds[4], NBLK_B, NBLK_B, KB, 0)
    diagonal = jnp.clip(-1.0 + 4.0 * jax.random.uniform(seeds[5], (NA, NB), jnp.float32) ** level_of(seeds[5], (NA, NB), ((0, 2), (1, 16)), -0.2, 0.2), -1.0, 3.0)
    return {"ci_vectors": ci_vectors, "alpha_blocks": alpha_blocks, "alpha_cols": alpha_cols, "beta_blocks": beta_blocks, "beta_cols": beta_cols, "diagonal": diagonal}


def alpha_term(ci_vectors, alpha_blocks, alpha_cols):
    grid = ci_vectors.reshape(NV, NBLK_A, BLK, NB)

    def one_row(pair):
        blocks, columns = pair
        picked = grid[:, columns].astype(jnp.float32)
        return jnp.einsum('kij,vkjb->vib', blocks.astype(jnp.float32), picked)

    stacked = lax.map(one_row, (alpha_blocks, alpha_cols))
    return stacked.transpose(1, 0, 2, 3).reshape(NV, NA, NB)


def beta_term(ci_vectors, beta_blocks, beta_cols):
    grid = ci_vectors.reshape(NV, NA, NBLK_B, BLK)

    def one_row(pair):
        blocks, columns = pair
        picked = grid[:, :, columns].astype(jnp.float32)
        return jnp.einsum('vakj,kij->vai', picked, blocks.astype(jnp.float32))

    stacked = lax.map(one_row, (beta_blocks, beta_cols))
    return stacked.transpose(1, 2, 0, 3).reshape(NV, NA, NB)


def reference(ci_vectors, alpha_blocks, alpha_cols, beta_blocks, beta_cols, diagonal):
    alpha_part = alpha_term(ci_vectors, alpha_blocks, alpha_cols)
    beta_part = beta_term(ci_vectors, beta_blocks, beta_cols)
    total = alpha_part + beta_part + diagonal[None, :, :] * ci_vectors.astype(jnp.float32)
    return total.astype(jnp.bfloat16)
```

```python
import functools

import jax
import jax.numpy as jnp
from jax import lax
from jax.experimental import pallas as pl
from jax.experimental.pallas import tpu as pltpu
from jax.sharding import PartitionSpec as P

MIB = 1 << 20
STEPS_PER_OCTAVE = 8
SHIFT = 1000
CODE_BITS = 11
LARGEST = 32767.0


def row_scale(code):
    return jnp.exp2((code - SHIFT).astype(jnp.float32) * (1.0 / STEPS_PER_OCTAVE))


def to_words(values):
    top = jnp.maximum(jnp.max(jnp.abs(values), axis=1, keepdims=True), 2.0 ** -100)
    code = jnp.ceil(jnp.log2(top) * STEPS_PER_OCTAVE + 0.01).astype(jnp.int32) + SHIFT
    words = jnp.round(values * (LARGEST / row_scale(code)))
    words = jnp.clip(words, -LARGEST, LARGEST).astype(jnp.int32)
    lane = lax.broadcasted_iota(jnp.int32, words.shape, 1)
    bit = lax.shift_right_logical(jnp.broadcast_to(code, words.shape), jnp.minimum(lane, CODE_BITS)) & 1
    return jnp.where(lane < CODE_BITS, (words & -2) | bit, words).astype(jnp.int16)


def from_words(words):
    words = words.astype(jnp.int32)
    head = words[:, :128]
    lane = lax.broadcasted_iota(jnp.int32, head.shape, 1)
    bits = jnp.where(lane < CODE_BITS, lax.shift_left(head & 1, jnp.minimum(lane, CODE_BITS)), 0)
    code = jnp.sum(bits.astype(jnp.float32), axis=1, keepdims=True).astype(jnp.int32)
    return words.astype(jnp.float32) * (row_scale(code) * (1.0 / LARGEST))


def beta_kernel(slots, cols_ref, turned_ref, blocks_ref, out_ref):
    dest = pl.program_id(0)
    sources, vectors, few_rows, strip = turned_ref.shape
    block = blocks_ref.shape[-1]
    per_strip = strip // block
    owned = per_strip
    parts = []
    for n in range(owned):
        picked = []
        for k in range(slots):
            c = cols_ref[(dest * owned + n) * slots + k]
            src = c // per_strip
            at = pl.multiple_of((c % per_strip) * block, block)
            tile = turned_ref[src, :, :, pl.ds(at, block)]
            picked.append(tile.reshape(vectors * few_rows, block))
        wide = jnp.concatenate(picked, axis=1)
        tall = blocks_ref[0, 0, n * slots * block : (n + 1) * slots * block, :]
        parts.append(jnp.dot(wide, tall, preferred_element_type=jnp.float32))
    term = jnp.concatenate(parts, axis=1) if owned > 1 else parts[0]
    out_ref[0] = to_words(term).reshape(vectors, few_rows, strip)


def beta_chunk(slots, columns, turned, blocks, first, count):
    sources, _, few_rows, strip = turned.shape
    inner, outer, depth, block = blocks.shape
    dests = inner * outer
    rows = count * few_rows
    return pl.pallas_call(
        functools.partial(beta_kernel, slots),
        grid_spec=pltpu.PrefetchScalarGridSpec(
            num_scalar_prefetch=1,
            grid=(dests,),
            in_specs=[
                pl.BlockSpec((sources, count, few_rows, strip), lambda p, _: (0, first // count, 0, 0)),
                pl.BlockSpec((1, 1, depth, block), lambda p, _: (p % inner, p // inner, 0, 0)),
            ],
            out_specs=pl.BlockSpec((1, count, few_rows, strip), lambda p, _: (p, 0, 0, 0)),
        ),
        out_shape=jax.ShapeDtypeStruct((dests, count, few_rows, strip), jnp.int16),
        compiler_params=pltpu.CompilerParams(vmem_limit_bytes=40 * MIB),
        cost_estimate=pl.CostEstimate(
            flops=4 * dests * rows * strip * slots * block,
            bytes_accessed=blocks.size * 2 + 2 * dests * rows * strip * 2,
            transcendentals=0,
        ),
        name="beta_term",
    )(columns, turned, blocks)


def alpha_kernel(cols_ref, whole_ref, own_ref, blocks_ref, diag_ref, out_ref):
    owned, slots, block, _ = blocks_ref.shape

    @pl.loop(0, owned)
    def _(r):
        picked = []
        for k in range(slots):
            at = pl.multiple_of(cols_ref[r * slots + k] * block, block)
            picked.append(whole_ref[0, pl.ds(at, block), :])
        tall = jnp.concatenate(picked, axis=0)
        wide = jnp.concatenate([blocks_ref[r, k] for k in range(slots)], axis=1)
        term = jnp.dot(wide, tall, preferred_element_type=jnp.float32)
        here = pl.ds(pl.multiple_of(r * block, block), block)
        out_ref[0, here, :] = term + diag_ref[here, :] * own_ref[0, here, :].astype(jnp.float32)


def alpha_term(columns, whole, own, blocks, diagonal):
    vectors, rows, strip = own.shape
    owned, slots, block, _ = blocks.shape
    once = pl.Buffered(1)
    return pl.pallas_call(
        alpha_kernel,
        grid_spec=pltpu.PrefetchScalarGridSpec(
            num_scalar_prefetch=1,
            grid=(vectors,),
            in_specs=[
                pl.BlockSpec((1, whole.shape[1], strip), lambda v, _: (v, 0, 0)),
                pl.BlockSpec((1, rows, strip), lambda v, _: (v, 0, 0)),
                pl.BlockSpec(blocks.shape, lambda v, _: (0, 0, 0, 0), pipeline_mode=once),
                pl.BlockSpec(diagonal.shape, lambda v, _: (0, 0), pipeline_mode=once),
            ],
            out_specs=pl.BlockSpec((1, rows, strip), lambda v, _: (v, 0, 0)),
        ),
        out_shape=jax.ShapeDtypeStruct((vectors, rows, strip), jnp.float32),
        compiler_params=pltpu.CompilerParams(vmem_limit_bytes=44 * MIB),
        cost_estimate=pl.CostEstimate(
            flops=6 * vectors * rows * strip * slots * block,
            bytes_accessed=whole.size * 2 + own.size * 6 + blocks.size * 2 + diagonal.size * 4,
            transcendentals=0,
        ),
        name="alpha_term",
    )(columns, whole, own, blocks, diagonal)


def join_kernel(acc_ref, words_ref, *rest):
    out_ref = rest[-1]
    sources, _, few_rows, strip = words_ref.shape
    for p in range(sources):
        here = pl.ds(p * few_rows, few_rows)
        out_ref[0, here, :] = (acc_ref[0, here, :] + from_words(words_ref[p, 0])).astype(jnp.bfloat16)


def join(acc, words, first, before):
    vectors, rows, strip = acc.shape
    sources, count, few_rows, _ = words.shape
    in_specs = [
        pl.BlockSpec((1, rows, strip), lambda v: (first + v, 0, 0)),
        pl.BlockSpec((sources, 1, few_rows, strip), lambda v: (0, v, 0, 0)),
    ]
    args = [acc, words]
    aliases = {}
    if before is not None:
        in_specs.append(pl.BlockSpec(memory_space=pl.ANY))
        args.append(before)
        aliases = {2: 0}
    return pl.pallas_call(
        join_kernel,
        grid=(count,),
        in_specs=in_specs,
        out_specs=pl.BlockSpec((1, rows, strip), lambda v: (first + v, 0, 0)),
        out_shape=jax.ShapeDtypeStruct((vectors, rows, strip), jnp.bfloat16),
        input_output_aliases=aliases,
        compiler_params=pltpu.CompilerParams(vmem_limit_bytes=32 * MIB),
        cost_estimate=pl.CostEstimate(
            flops=8 * count * rows * strip, bytes_accessed=8 * count * rows * strip, transcendentals=0
        ),
        name="join_terms",
    )(*args)


def gather_beta(beta_blocks, beta_cols, ring):
    owned, slots, block, _ = beta_blocks.shape
    outer = 4 if ring % 4 == 0 else 1
    inner = ring // outer
    turned = beta_blocks.transpose(0, 1, 3, 2).reshape(owned * slots * block, block)
    heads = jnp.pad(beta_cols.reshape(1, owned * slots).astype(jnp.bfloat16), ((0, 15), (0, block - owned * slots)))
    message = jnp.concatenate([turned, heads], axis=0)
    far = [[o * inner + i for o in range(outer)] for i in range(inner)]
    near = [[o * inner + i for i in range(inner)] for o in range(outer)]
    message = lax.all_gather(message, "beta", axis=0, tiled=False, axis_index_groups=far)
    message = lax.all_gather(message, "beta", axis=0, tiled=False, axis_index_groups=near)
    return message, inner, outer


def shards(ring, ci_vectors, alpha_blocks, alpha_cols, beta_blocks, beta_cols, diagonal):
    vectors, rows, strip = ci_vectors.shape
    few_rows = rows // ring
    owned, slots, block, _ = beta_blocks.shape
    count = 2
    half = vectors // 2

    message, inner, outer = gather_beta(beta_blocks, beta_cols, ring)
    body = owned * slots * block
    columns = message[:, :, body, : owned * slots].transpose(1, 0, 2).reshape(-1).astype(jnp.int32)

    turned = []
    for h in range(0, vectors, half):
        piece = ci_vectors[h : h + half].reshape(half, ring, few_rows, strip).transpose(1, 0, 2, 3)
        turned.append(lax.all_to_all(piece, "beta", split_axis=0, concat_axis=0, tiled=True))

    whole = lax.all_gather(ci_vectors, "alpha", axis=1, tiled=True)

    words = []
    for first in range(0, vectors, count):
        term = beta_chunk(slots, columns, turned[first // half], message, first % half, count)
        words.append(lax.all_to_all(term, "beta", split_axis=0, concat_axis=0, tiled=True))

    acc = alpha_term(alpha_cols.reshape(-1), whole, ci_vectors, alpha_blocks, diagonal)
    total = None
    for i, first in enumerate(range(0, vectors, count)):
        total = join(acc, words[i], first, total)
    return total


def solution(mesh):
    placed = (
        P(None, "alpha", "beta"),
        P("alpha", None, None, None),
        P("alpha", None),
        P("beta", None, None, None),
        P("beta", None),
        P("alpha", "beta"),
    )
    return jax.shard_map(
        functools.partial(shards, mesh.shape["beta"]),
        mesh=mesh,
        in_specs=placed,
        out_specs=P(None, "alpha", "beta"),
        check_vma=False,
    )
```

```python
import functools
import math

import jax
import jax.numpy as jnp
from jax import lax
from jax.experimental import pallas as pl
from jax.experimental.pallas import tpu as pltpu
from jax.sharding import PartitionSpec as P

MIB = 1 << 20
STEPS_PER_OCTAVE = 8
SHIFT = 1000
CODE_BITS = 11
LARGEST = 32767.0
TILE = 16
CORES = 2
ANYWHERE = pl.BlockSpec(memory_space=pl.ANY)


def row_scale(code):
    return jnp.exp2((code - SHIFT).astype(jnp.float32) * (1.0 / STEPS_PER_OCTAVE))


def to_words(values):
    top = jnp.maximum(jnp.max(jnp.abs(values), axis=1, keepdims=True), 2.0 ** -100)
    code = jnp.ceil(jnp.log2(top) * STEPS_PER_OCTAVE + 0.01).astype(jnp.int32) + SHIFT
    words = jnp.round(values * (LARGEST / row_scale(code))).astype(jnp.int32)
    head = words[:, :128]
    lane = lax.broadcasted_iota(jnp.int32, head.shape, 1)
    bit = lax.shift_right_logical(jnp.broadcast_to(code, head.shape), jnp.minimum(lane, CODE_BITS)) & 1
    head = jnp.where(lane < CODE_BITS, (head & -2) | bit, head)
    if words.shape[1] > 128:
        head = jnp.concatenate([head, words[:, 128:]], axis=1)
    return head.astype(jnp.int16)


def from_words(words):
    words = words.astype(jnp.int32)
    head = words[:, :128]
    lane = lax.broadcasted_iota(jnp.int32, head.shape, 1)
    bits = jnp.where(lane < CODE_BITS, lax.shift_left(head & 1, jnp.minimum(lane, CODE_BITS)), 0)
    code = jnp.sum(bits.astype(jnp.float32), axis=1, keepdims=True).astype(jnp.int32)
    return words.astype(jnp.float32) * (row_scale(code) * (1.0 / LARGEST))


def pack_kernel(first, count, few_rows, *refs):
    source_ref, out_ref, sem = refs[0], refs[-2], refs[-1]
    dests = out_ref.shape[0]

    def copy(d, v):
        return pltpu.make_async_copy(
            source_ref.at[first + v, pl.ds(d * few_rows, few_rows)],
            out_ref.at[d, pl.ds(v * few_rows, few_rows)],
            sem.at[d, v],
        )

    def head(d):
        return pltpu.make_async_copy(refs[1], out_ref.at[d, pl.ds(count * few_rows, TILE)], sem.at[d, count])

    def all_of(act):
        for d in range(dests):
            for v in range(count):
                act(copy(d, v))
            if len(refs) == 4:
                act(head(d))

    all_of(lambda c: c.start())
    all_of(lambda c: c.wait())


def pack(ci_vectors, heads, first, count, ring):
    _, rows, strip = ci_vectors.shape
    few_rows = rows // ring
    depth = count * few_rows + (0 if heads is None else TILE)
    args = (ci_vectors,) if heads is None else (ci_vectors, heads)
    return pl.pallas_call(
        functools.partial(pack_kernel, first, count, few_rows),
        in_specs=[ANYWHERE] * len(args),
        out_specs=ANYWHERE,
        out_shape=jax.ShapeDtypeStruct((ring, depth, strip), jnp.bfloat16),
        scratch_shapes=[pltpu.SemaphoreType.DMA((ring, count + 1))],
        cost_estimate=pl.CostEstimate(flops=0, bytes_accessed=4 * ring * depth * strip, transcendentals=0),
        name="pack_pieces",
    )(*args)


def beta_kernel(slots, xs, cols_ref, place_ref, *refs):
    own_ref, twin_ref = refs[:2]
    message_refs = refs[2:-5]
    out_ref, picked_ref, blocks_ref, picked_sem, blocks_sem = refs[-5:]
    block = blocks_ref.shape[-1]
    sources = own_ref.shape[0]
    per_strip = own_ref.shape[2] // block
    _, both_rows, _ = picked_ref.shape
    rows = both_rows // CORES
    half = blocks_ref.shape[1] // 2
    outer = message_refs[0].shape[0]
    dest, tile = pl.program_id(0), pl.program_id(1)
    core, x_here, parity = place_ref[0], place_ref[1], place_ref[2]

    @pl.when((dest == 0) & (tile == 0))
    def _():
        for which, ref in enumerate((own_ref, twin_ref)):
            at = pl.multiple_of((core ^ which) * rows, rows)
            for src in range(sources):
                for s in range(per_strip):
                    pltpu.make_async_copy(
                        ref.at[src, pl.ds(0, rows), pl.ds(s * block, block)],
                        picked_ref.at[src * per_strip + s, pl.ds(at, rows)],
                        picked_sem,
                    ).start()
        for z in range(outer):
            for q in range(xs):
                for r in range(2):
                    d = z * xs + (x_here ^ q)
                    at = pl.multiple_of((parity ^ r) * half, half)
                    pltpu.make_async_copy(
                        message_refs[q * 2 + r].at[z], blocks_ref.at[d, pl.ds(at, half)], blocks_sem.at[d]
                    ).start()
        pltpu.make_async_copy(picked_ref, picked_ref, picked_sem).wait()

    @pl.when(tile == 0)
    def _():
        pltpu.make_async_copy(blocks_ref.at[dest], blocks_ref.at[dest], blocks_sem.at[dest]).wait()

    size = out_ref.shape[1]
    here = pl.ds(pl.multiple_of(tile * size, size), size)
    strip = dest * CORES + core
    parts = []
    for n in range(per_strip):
        wide = jnp.concatenate(
            [picked_ref[cols_ref[(strip * per_strip + n) * slots + k], here, :] for k in range(slots)], axis=1
        )
        tall = blocks_ref[dest, n * slots * block : (n + 1) * slots * block, :]
        parts.append(jnp.dot(wide, tall, preferred_element_type=jnp.float32))
    term = jnp.concatenate(parts, axis=1) if per_strip > 1 else parts[0]
    out_ref[0] = to_words(term)


def beta_term(slots, xs, columns, place, own, twin, messages, rows):
    sources, _, strip = own.shape
    outer, half, block = messages[0].shape
    dests = outer * xs
    both = rows * CORES
    size = math.gcd(both, 512)
    count = sources * strip // block
    return pl.pallas_call(
        functools.partial(beta_kernel, slots, xs),
        grid_spec=pltpu.PrefetchScalarGridSpec(
            num_scalar_prefetch=2,
            grid=(dests, both // size),
            in_specs=[ANYWHERE] * (2 + len(messages)),
            out_specs=pl.BlockSpec((1, size, strip), lambda d, m, *_: (d, m, 0)),
            scratch_shapes=[
                pltpu.VMEM((count, both, block), jnp.bfloat16),
                pltpu.VMEM((dests, 2 * half, block), jnp.bfloat16),
                pltpu.SemaphoreType.DMA,
                pltpu.SemaphoreType.DMA((dests,)),
            ],
        ),
        out_shape=jax.ShapeDtypeStruct((dests, both, strip), jnp.int16),
        compiler_params=pltpu.CompilerParams(vmem_limit_bytes=44 * MIB),
        cost_estimate=pl.CostEstimate(
            flops=4 * dests * both * strip * slots * block,
            bytes_accessed=8 * half * block * dests + 4 * count * both * block,
            transcendentals=0,
        ),
        name="beta_term",
    )(columns, place, own, twin, *messages)


def alpha_kernel(pieces, cols_ref, place_ref, *refs):
    blocks_ref, diag_ref, out_ref, whole_ref = refs[pieces:]
    own_ref = refs[0]
    owned, slots, block, _ = blocks_ref.shape
    rows = own_ref.shape[1]
    for s in range(pieces):
        at = pl.multiple_of(lax.rem(place_ref[3] + s, pieces) * rows, rows)
        whole_ref[pl.ds(at, rows), :] = refs[s][0]

    @pl.loop(0, owned)
    def _(r):
        picked = []
        for k in range(slots):
            at = pl.multiple_of(cols_ref[r * slots + k] * block, block)
            picked.append(whole_ref[pl.ds(at, block), :])
        tall = jnp.concatenate(picked, axis=0)
        wide = jnp.concatenate([blocks_ref[r, k] for k in range(slots)], axis=1)
        term = jnp.dot(wide, tall, preferred_element_type=jnp.float32)
        here = pl.ds(pl.multiple_of(r * block, block), block)
        out_ref[0, here, :] = term + diag_ref[here, :] * own_ref[0, here, :].astype(jnp.float32)


def alpha_term(columns, place, own, others, blocks, diagonal, first):
    count, rows, strip = others[0].shape if others else own.shape
    owned, slots, block, _ = blocks.shape
    pieces = 1 + len(others)
    once = pl.Buffered(1)
    return pl.pallas_call(
        functools.partial(alpha_kernel, pieces),
        grid_spec=pltpu.PrefetchScalarGridSpec(
            num_scalar_prefetch=2,
            grid=(count,),
            in_specs=[pl.BlockSpec((1, rows, strip), lambda v, *_: (first + v, 0, 0))]
            + [pl.BlockSpec((1, rows, strip), lambda v, *_: (v, 0, 0))] * len(others)
            + [
                pl.BlockSpec(blocks.shape, lambda v, *_: (0, 0, 0, 0), pipeline_mode=once),
                pl.BlockSpec(diagonal.shape, lambda v, *_: (0, 0), pipeline_mode=once),
            ],
            out_specs=pl.BlockSpec((1, rows, strip), lambda v, *_: (v, 0, 0)),
            scratch_shapes=[pltpu.VMEM((pieces * rows, strip), jnp.bfloat16)],
        ),
        out_shape=jax.ShapeDtypeStruct((count, rows, strip), jnp.float32),
        compiler_params=pltpu.CompilerParams(vmem_limit_bytes=44 * MIB),
        cost_estimate=pl.CostEstimate(
            flops=6 * count * rows * strip * slots * block,
            bytes_accessed=count * rows * strip * (2 * pieces + 4) + blocks.size * 2 + diagonal.size * 4,
            transcendentals=0,
        ),
        name="alpha_term",
    )(columns, place, own, *others, blocks, diagonal)


def join_kernel(few_rows, acc_ref, words_ref, *rest):
    out_ref = rest[-1]
    for j in range(words_ref.shape[0]):
        for c in range(CORES):
            here = pl.ds((j * CORES + c) * few_rows, few_rows)
            out_ref[0, here, :] = (acc_ref[0, here, :] + from_words(words_ref[j, c, 0])).astype(jnp.bfloat16)


def join(acc, words, first, vectors, before):
    count, rows, strip = acc.shape
    sources = words.shape[0]
    few_rows = rows // (sources * CORES)
    words = words.reshape(sources, CORES, count, few_rows, strip)
    in_specs = [
        pl.BlockSpec((1, rows, strip), lambda v: (v, 0, 0)),
        pl.BlockSpec((sources, CORES, 1, few_rows, strip), lambda v: (0, 0, v, 0, 0)),
    ]
    args = [acc, words]
    aliases = {}
    if before is not None:
        in_specs.append(ANYWHERE)
        args.append(before)
        aliases = {2: 0}
    return pl.pallas_call(
        functools.partial(join_kernel, few_rows),
        grid=(count,),
        in_specs=in_specs,
        out_specs=pl.BlockSpec((1, rows, strip), lambda v: (first + v, 0, 0)),
        out_shape=jax.ShapeDtypeStruct((vectors, rows, strip), jnp.bfloat16),
        input_output_aliases=aliases,
        compiler_params=pltpu.CompilerParams(vmem_limit_bytes=32 * MIB),
        cost_estimate=pl.CostEstimate(
            flops=8 * count * rows * strip, bytes_accessed=8 * count * rows * strip, transcendentals=0
        ),
        name="join_terms",
    )(*args)


def after(value, earlier):
    return lax.optimization_barrier((value, earlier))[0]


def shards(ring, ring_a, ci_vectors, alpha_blocks, alpha_cols, beta_blocks, beta_cols, diagonal):
    vectors, rows, strip = ci_vectors.shape
    few_rows = rows // ring
    owned, slots, block, _ = beta_blocks.shape
    outer = 4
    inner = ring // outer
    xs = inner // CORES
    at_a, at_b = lax.axis_index("alpha"), lax.axis_index("beta")
    parity = lax.rem(at_a, 2)
    place = jnp.stack([lax.rem(at_b, CORES), lax.rem(lax.div(at_b, CORES), xs), parity, at_a]).astype(jnp.int32)
    cuts = [(0, 6), (6, 2)]

    def swap(value, bit):
        return lax.ppermute(value, "beta", [(i, i ^ bit) for i in range(ring)])

    def across(value):
        return lax.ppermute(value, "alpha", [(i, i ^ 1) for i in range(ring_a)])

    def exchange(value):
        return [
            lax.ppermute(value, "alpha", [((i + s) % ring_a, i) for i in range(ring_a)]) for s in range(1, ring_a)
        ]

    stored = beta_blocks.reshape(2, owned * slots // 2, block, block)
    mine = lax.dynamic_index_in_dim(stored, parity, 0, keepdims=False)
    mine = mine.transpose(0, 2, 1).reshape(-1, block)
    far = [[o * inner + i for o in range(outer)] for i in range(inner)]
    carried = [lax.all_gather(mine, "beta", axis=0, tiled=False, axis_index_groups=far)]
    bit = CORES
    while bit < inner:
        carried = carried + [swap(m, bit) for m in carried]
        bit *= 2
    messages = []
    for m in carried:
        messages += [m, across(m)]

    heads = jnp.pad(beta_cols.reshape(1, -1).astype(jnp.bfloat16), ((0, TILE - 1), (0, strip - owned * slots)))
    turned = []
    for i, (first, count) in enumerate(cuts):
        piece = pack(ci_vectors, heads if i == 0 else None, first, count, ring)
        if i > 0:
            piece = after(piece, turned[i - 1])
        turned.append(lax.all_to_all(piece, "beta", split_axis=0, concat_axis=0, tiled=True))
    columns = turned[0][:, cuts[0][1] * few_rows, : owned * slots].reshape(-1).astype(jnp.int32)

    twins = [swap(t, 1) for t in turned]

    own_late = ci_vectors[cuts[0][0] : cuts[0][0] + cuts[0][1]]
    own_early = ci_vectors[cuts[1][0] : cuts[1][0] + cuts[1][1]]
    acc_late = alpha_term(
        alpha_cols.reshape(-1), place, ci_vectors, exchange(after(own_late, messages[-1])), alpha_blocks, diagonal, 0
    )
    acc_early = alpha_term(
        alpha_cols.reshape(-1), place, ci_vectors, exchange(own_early), alpha_blocks, diagonal, cuts[1][0]
    )

    near = [[j * CORES + c for j in range(ring // CORES)] for c in range(CORES)]
    total = None
    last = turned[-1]
    for i, (first, count) in enumerate(cuts):
        term = beta_term(slots, xs, columns, place, turned[i], twins[i], messages, count * few_rows)
        term = after(term, last)
        words = lax.all_to_all(term, "beta", split_axis=0, concat_axis=0, tiled=True, axis_index_groups=near)
        last = words
        total = join((acc_late, acc_early)[i], words, first, vectors, total)
    return total


def solution(mesh):
    placed = (
        P(None, "alpha", "beta"),
        P("alpha", None, None, None),
        P("alpha", None),
        P("beta", None, None, None),
        P("beta", None),
        P("alpha", "beta"),
    )
    return jax.shard_map(
        functools.partial(shards, mesh.shape["beta"], mesh.shape["alpha"]),
        mesh=mesh,
        in_specs=placed,
        out_specs=P(None, "alpha", "beta"),
        check_vma=False,
    )
```

```python
import functools
import math

import jax
import jax.numpy as jnp
from jax import lax
from jax.experimental import pallas as pl
from jax.experimental.pallas import tpu as pltpu
from jax.sharding import PartitionSpec as P

MIB = 1 << 20
STEPS_PER_OCTAVE = 8
SHIFT = 1000
CODE_BITS = 11
LARGEST = 32767.0
TILE = 16
CORES = 2
ANYWHERE = pl.BlockSpec(memory_space=pl.ANY)


def row_scale(code):
    return jnp.exp2((code - SHIFT).astype(jnp.float32) * (1.0 / STEPS_PER_OCTAVE))


def to_words(values):
    top = jnp.maximum(jnp.max(jnp.abs(values), axis=1, keepdims=True), 2.0 ** -100)
    code = jnp.ceil(jnp.log2(top) * STEPS_PER_OCTAVE + 0.01).astype(jnp.int32) + SHIFT
    words = jnp.round(values * (LARGEST / row_scale(code))).astype(jnp.int32)
    head = words[:, :128]
    lane = lax.broadcasted_iota(jnp.int32, head.shape, 1)
    bit = lax.shift_right_logical(jnp.broadcast_to(code, head.shape), jnp.minimum(lane, CODE_BITS)) & 1
    head = jnp.where(lane < CODE_BITS, (head & -2) | bit, head)
    if words.shape[1] > 128:
        head = jnp.concatenate([head, words[:, 128:]], axis=1)
    return head.astype(jnp.int16)


def from_words(words):
    words = words.astype(jnp.int32)
    head = words[:, :128]
    lane = lax.broadcasted_iota(jnp.int32, head.shape, 1)
    bits = jnp.where(lane < CODE_BITS, lax.shift_left(head & 1, jnp.minimum(lane, CODE_BITS)), 0)
    code = jnp.sum(bits.astype(jnp.float32), axis=1, keepdims=True).astype(jnp.int32)
    return words.astype(jnp.float32) * (row_scale(code) * (1.0 / LARGEST))


def pack_kernel(source_ref, *refs):
    out_ref = refs[-1]
    count, wide, _ = source_ref.shape
    dests = out_ref.shape[0]
    few_rows = wide // dests
    for d in range(dests):
        for v in range(count):
            out_ref[d, v * few_rows : (v + 1) * few_rows, :] = source_ref[v, d * few_rows : (d + 1) * few_rows, :]
        if len(refs) == 2:
            out_ref[d, count * few_rows :, :] = refs[0][...]


def pack(ci_vectors, heads, first, count, ring):
    _, rows, strip = ci_vectors.shape
    few_rows = rows // ring
    depth = count * few_rows + (0 if heads is None else TILE)
    each = 4
    in_specs = [pl.BlockSpec((count, each * few_rows, strip), lambda d: (first // count, d, 0))]
    args = [ci_vectors]
    if heads is not None:
        in_specs.append(pl.BlockSpec((TILE, strip), lambda d: (0, 0)))
        args.append(heads)
    return pl.pallas_call(
        pack_kernel,
        grid=(ring // each,),
        in_specs=in_specs,
        out_specs=pl.BlockSpec((each, depth, strip), lambda d: (d, 0, 0)),
        out_shape=jax.ShapeDtypeStruct((ring, depth, strip), jnp.bfloat16),
        compiler_params=pltpu.CompilerParams(vmem_limit_bytes=24 * MIB),
        cost_estimate=pl.CostEstimate(flops=0, bytes_accessed=4 * ring * depth * strip, transcendentals=0),
        name="pack_pieces",
    )(*args)


def beta_kernel(slots, xs, cols_ref, place_ref, *refs):
    own_ref, twin_ref = refs[:2]
    message_refs = refs[2:-5]
    out_ref, picked_ref, blocks_ref, picked_sem, blocks_sem = refs[-5:]
    block = blocks_ref.shape[-1]
    sources = own_ref.shape[0]
    per_strip = own_ref.shape[2] // block
    _, both_rows, _ = picked_ref.shape
    rows = both_rows // CORES
    half = blocks_ref.shape[1] // 2
    outer = message_refs[0].shape[0]
    dest, tile = pl.program_id(0), pl.program_id(1)
    core, x_here, parity = place_ref[0], place_ref[1], place_ref[2]

    @pl.when((dest == 0) & (tile == 0))
    def _():
        for which, ref in enumerate((own_ref, twin_ref)):
            at = pl.multiple_of((core ^ which) * rows, rows)
            for src in range(sources):
                for s in range(per_strip):
                    pltpu.make_async_copy(
                        ref.at[src, pl.ds(0, rows), pl.ds(s * block, block)],
                        picked_ref.at[src * per_strip + s, pl.ds(at, rows)],
                        picked_sem,
                    ).start()
        for z in range(outer):
            for q in range(xs):
                for r in range(2):
                    d = z * xs + (x_here ^ q)
                    at = pl.multiple_of((parity ^ r) * half, half)
                    pltpu.make_async_copy(
                        message_refs[q * 2 + r].at[z], blocks_ref.at[d, pl.ds(at, half)], blocks_sem.at[d]
                    ).start()
        pltpu.make_async_copy(picked_ref, picked_ref, picked_sem).wait()

    @pl.when(tile == 0)
    def _():
        pltpu.make_async_copy(blocks_ref.at[dest], blocks_ref.at[dest], blocks_sem.at[dest]).wait()

    size = out_ref.shape[1]
    here = pl.ds(pl.multiple_of(tile * size, size), size)
    strip = dest * CORES + core
    parts = []
    for n in range(per_strip):
        wide = jnp.concatenate(
            [picked_ref[cols_ref[(strip * per_strip + n) * slots + k], here, :] for k in range(slots)], axis=1
        )
        tall = blocks_ref[dest, n * slots * block : (n + 1) * slots * block, :]
        parts.append(jnp.dot(wide, tall, preferred_element_type=jnp.float32))
    term = jnp.concatenate(parts, axis=1) if per_strip > 1 else parts[0]
    out_ref[0] = to_words(term)


def beta_term(slots, xs, columns, place, own, twin, messages, rows):
    sources, _, strip = own.shape
    outer, half, block = messages[0].shape
    dests = outer * xs
    both = rows * CORES
    size = math.gcd(both, 512)
    count = sources * strip // block
    return pl.pallas_call(
        functools.partial(beta_kernel, slots, xs),
        grid_spec=pltpu.PrefetchScalarGridSpec(
            num_scalar_prefetch=2,
            grid=(dests, both // size),
            in_specs=[ANYWHERE] * (2 + len(messages)),
            out_specs=pl.BlockSpec((1, size, strip), lambda d, m, *_: (d, m, 0)),
            scratch_shapes=[
                pltpu.VMEM((count, both, block), jnp.bfloat16),
                pltpu.VMEM((dests, 2 * half, block), jnp.bfloat16),
                pltpu.SemaphoreType.DMA,
                pltpu.SemaphoreType.DMA((dests,)),
            ],
        ),
        out_shape=jax.ShapeDtypeStruct((dests, both, strip), jnp.int16),
        compiler_params=pltpu.CompilerParams(vmem_limit_bytes=44 * MIB),
        cost_estimate=pl.CostEstimate(
            flops=4 * dests * both * strip * slots * block,
            bytes_accessed=8 * half * block * dests + 4 * count * both * block,
            transcendentals=0,
        ),
        name="beta_term",
    )(columns, place, own, twin, *messages)


def alpha_kernel(pieces, cols_ref, place_ref, *refs):
    blocks_ref, diag_ref = refs[pieces : pieces + 2]
    out_ref, whole_ref = refs[-2:]
    own_ref = refs[0]
    owned, slots, block, _ = blocks_ref.shape
    rows = own_ref.shape[1]
    for s in range(pieces):
        at = pl.multiple_of(lax.rem(place_ref[3] + s, pieces) * rows, rows)
        whole_ref[pl.ds(at, rows), :] = refs[s][0]

    @pl.loop(0, owned)
    def _(r):
        picked = []
        for k in range(slots):
            at = pl.multiple_of(cols_ref[r * slots + k] * block, block)
            picked.append(whole_ref[pl.ds(at, block), :])
        tall = jnp.concatenate(picked, axis=0)
        wide = jnp.concatenate([blocks_ref[r, k] for k in range(slots)], axis=1)
        term = jnp.dot(wide, tall, preferred_element_type=jnp.float32)
        here = pl.ds(pl.multiple_of(r * block, block), block)
        out_ref[0, here, :] = term + diag_ref[here, :] * own_ref[0, here, :].astype(jnp.float32)


def alpha_term(columns, place, own, others, blocks, diagonal, first, count, before):
    vectors, rows, strip = own.shape
    owned, slots, block, _ = blocks.shape
    pieces = 1 + len(others)
    once = pl.Buffered(1)
    mine = pl.BlockSpec((1, rows, strip), lambda v, *_: (first + v, 0, 0))
    in_specs = (
        [mine]
        + [pl.BlockSpec((1, rows, strip), lambda v, *_: (v, 0, 0))] * len(others)
        + [
            pl.BlockSpec(blocks.shape, lambda v, *_: (0, 0, 0, 0), pipeline_mode=once),
            pl.BlockSpec(diagonal.shape, lambda v, *_: (0, 0), pipeline_mode=once),
        ]
    )
    args = [columns, place, own, *others, blocks, diagonal]
    aliases = {}
    if before is not None:
        aliases = {len(args): 0}
        args.append(before)
        in_specs.append(ANYWHERE)
    return pl.pallas_call(
        functools.partial(alpha_kernel, pieces),
        grid_spec=pltpu.PrefetchScalarGridSpec(
            num_scalar_prefetch=2,
            grid=(count,),
            in_specs=in_specs,
            out_specs=mine,
            scratch_shapes=[pltpu.VMEM((pieces * rows, strip), jnp.bfloat16)],
        ),
        out_shape=jax.ShapeDtypeStruct((vectors, rows, strip), jnp.float32),
        input_output_aliases=aliases,
        compiler_params=pltpu.CompilerParams(vmem_limit_bytes=44 * MIB),
        cost_estimate=pl.CostEstimate(
            flops=6 * count * rows * strip * slots * block,
            bytes_accessed=count * rows * strip * (2 * pieces + 4) + blocks.size * 2 + diagonal.size * 4,
            transcendentals=0,
        ),
        name="alpha_term",
    )(*args)


def join_kernel(few_rows, acc_ref, words_ref, *rest):
    out_ref = rest[-1]
    for j in range(words_ref.shape[0]):
        for c in range(CORES):
            here = pl.ds((j * CORES + c) * few_rows, few_rows)
            out_ref[0, here, :] = (acc_ref[0, here, :] + from_words(words_ref[j, c, 0])).astype(jnp.bfloat16)


def join(acc, words, first, vectors, before):
    _, rows, strip = acc.shape
    sources = words.shape[0]
    few_rows = rows // (sources * CORES)
    words = words.reshape(sources, CORES, -1, few_rows, strip)
    count = words.shape[2]
    in_specs = [
        pl.BlockSpec((1, rows, strip), lambda v: (first + v, 0, 0)),
        pl.BlockSpec((sources, CORES, 1, few_rows, strip), lambda v: (0, 0, v, 0, 0)),
    ]
    args = [acc, words]
    aliases = {}
    if before is not None:
        in_specs.append(ANYWHERE)
        args.append(before)
        aliases = {2: 0}
    return pl.pallas_call(
        functools.partial(join_kernel, few_rows),
        grid=(count,),
        in_specs=in_specs,
        out_specs=pl.BlockSpec((1, rows, strip), lambda v: (first + v, 0, 0)),
        out_shape=jax.ShapeDtypeStruct((vectors, rows, strip), jnp.bfloat16),
        input_output_aliases=aliases,
        compiler_params=pltpu.CompilerParams(vmem_limit_bytes=32 * MIB),
        cost_estimate=pl.CostEstimate(
            flops=8 * count * rows * strip, bytes_accessed=8 * count * rows * strip, transcendentals=0
        ),
        name="join_terms",
    )(*args)


def after(value, earlier):
    return lax.optimization_barrier((value, earlier))[0]


def shards(ring, ring_a, ci_vectors, alpha_blocks, alpha_cols, beta_blocks, beta_cols, diagonal):
    vectors, rows, strip = ci_vectors.shape
    few_rows = rows // ring
    owned, slots, block, _ = beta_blocks.shape
    outer = 4
    inner = ring // outer
    xs = inner // CORES
    at_a, at_b = lax.axis_index("alpha"), lax.axis_index("beta")
    parity = lax.rem(at_a, 2)
    place = jnp.stack([lax.rem(at_b, CORES), lax.rem(lax.div(at_b, CORES), xs), parity, at_a]).astype(jnp.int32)
    cuts = [(6, 2), (0, 6)]
    halves = [(0, vectors // 2), (vectors // 2, vectors // 2)]

    def swap(value, bit):
        return lax.ppermute(value, "beta", [(i, i ^ bit) for i in range(ring)])

    def across(value):
        return lax.ppermute(value, "alpha", [(i, i ^ 1) for i in range(ring_a)])

    def exchange(value):
        return [
            lax.ppermute(value, "alpha", [((i + s) % ring_a, i) for i in range(ring_a)]) for s in range(1, ring_a)
        ]

    others = [exchange(ci_vectors[: halves[0][1]])]

    stored = beta_blocks.reshape(2, owned * slots // 2, block, block)
    mine = lax.dynamic_index_in_dim(stored, parity, 0, keepdims=False)
    mine = mine.transpose(0, 2, 1).reshape(-1, block)
    far = [[o * inner + i for o in range(outer)] for i in range(inner)]
    carried = lax.all_gather(mine, "beta", axis=0, tiled=False, axis_index_groups=far)
    carried = [after(carried, others[0][-1])]
    bit = CORES
    while bit < inner:
        carried = carried + [swap(m, bit) for m in carried]
        bit *= 2
    messages = []
    for m in carried:
        messages += [m, across(m)]
    others.append(exchange(after(ci_vectors[halves[1][0] :], messages[-1])))

    heads = jnp.pad(beta_cols.reshape(1, -1).astype(jnp.bfloat16), ((0, TILE - 1), (0, strip - owned * slots)))
    turned = []
    for i, (first, count) in enumerate(cuts):
        piece = pack(ci_vectors, heads if i == 0 else None, first, count, ring)
        if i > 0:
            piece = after(piece, turned[i - 1])
        turned.append(lax.all_to_all(piece, "beta", split_axis=0, concat_axis=0, tiled=True))
    columns = turned[0][:, cuts[0][1] * few_rows, : owned * slots].reshape(-1).astype(jnp.int32)
    twins = [swap(t, 1) for t in turned]

    acc = None
    for (first, count), others_now in zip(halves, others):
        acc = alpha_term(
            alpha_cols.reshape(-1), place, ci_vectors, others_now, alpha_blocks, diagonal, first, count, acc
        )

    near = [[j * CORES + c for j in range(ring // CORES)] for c in range(CORES)]
    total = None
    last = turned[-1]
    for i, (first, count) in enumerate(cuts):
        term = beta_term(slots, xs, columns, place, turned[i], twins[i], messages, count * few_rows)
        term = after(term, last)
        words = lax.all_to_all(term, "beta", split_axis=0, concat_axis=0, tiled=True, axis_index_groups=near)
        last = words
        total = join(acc, words, first, vectors, total)
    return total


def solution(mesh):
    placed = (
        P(None, "alpha", "beta"),
        P("alpha", None, None, None),
        P("alpha", None),
        P("beta", None, None, None),
        P("beta", None),
        P("alpha", "beta"),
    )
    return jax.shard_map(
        functools.partial(shards, mesh.shape["beta"], mesh.shape["alpha"]),
        mesh=mesh,
        in_specs=placed,
        out_specs=P(None, "alpha", "beta"),
        check_vma=False,
    )
```

```python
import functools
import math

import jax
import jax.numpy as jnp
from jax import lax
from jax.experimental import pallas as pl
from jax.experimental.pallas import tpu as pltpu
from jax.sharding import PartitionSpec as P

MIB = 1 << 20
STEPS_PER_OCTAVE = 8
SHIFT = 1000
CODE_BITS = 11
LARGEST = 32767.0
TILE = 16
CORES = 2
ANYWHERE = pl.BlockSpec(memory_space=pl.ANY)


def row_scale(code):
    return jnp.exp2((code - SHIFT).astype(jnp.float32) * (1.0 / STEPS_PER_OCTAVE))


def to_words(values):
    top = jnp.maximum(jnp.max(jnp.abs(values), axis=1, keepdims=True), 2.0 ** -100)
    code = jnp.ceil(jnp.log2(top) * STEPS_PER_OCTAVE + 0.01).astype(jnp.int32) + SHIFT
    words = jnp.round(values * (LARGEST / row_scale(code))).astype(jnp.int32)
    head = words[:, :128]
    lane = lax.broadcasted_iota(jnp.int32, head.shape, 1)
    bit = lax.shift_right_logical(jnp.broadcast_to(code, head.shape), jnp.minimum(lane, CODE_BITS)) & 1
    head = jnp.where(lane < CODE_BITS, (head & -2) | bit, head)
    if words.shape[1] > 128:
        head = jnp.concatenate([head, words[:, 128:]], axis=1)
    return head.astype(jnp.int16)


def from_words(words):
    words = words.astype(jnp.int32)
    head = words[:, :128]
    lane = lax.broadcasted_iota(jnp.int32, head.shape, 1)
    bits = jnp.where(lane < CODE_BITS, lax.shift_left(head & 1, jnp.minimum(lane, CODE_BITS)), 0)
    code = jnp.sum(bits.astype(jnp.float32), axis=1, keepdims=True).astype(jnp.int32)
    return words.astype(jnp.float32) * (row_scale(code) * (1.0 / LARGEST))


def pack_kernel(source_ref, *refs):
    out_ref = refs[-1]
    count, wide, _ = source_ref.shape
    dests = out_ref.shape[0]
    few_rows = wide // dests
    for d in range(dests):
        for v in range(count):
            out_ref[d, v * few_rows : (v + 1) * few_rows, :] = source_ref[v, d * few_rows : (d + 1) * few_rows, :]
        if len(refs) == 2:
            out_ref[d, count * few_rows :, :] = refs[0][...]


def pack(ci_vectors, heads, first, count, ring):
    _, rows, strip = ci_vectors.shape
    few_rows = rows // ring
    depth = count * few_rows + (0 if heads is None else TILE)
    each = 4
    in_specs = [pl.BlockSpec((count, each * few_rows, strip), lambda d: (first // count, d, 0))]
    args = [ci_vectors]
    if heads is not None:
        in_specs.append(pl.BlockSpec((TILE, strip), lambda d: (0, 0)))
        args.append(heads)
    return pl.pallas_call(
        pack_kernel,
        grid=(ring // each,),
        in_specs=in_specs,
        out_specs=pl.BlockSpec((each, depth, strip), lambda d: (d, 0, 0)),
        out_shape=jax.ShapeDtypeStruct((ring, depth, strip), jnp.bfloat16),
        compiler_params=pltpu.CompilerParams(vmem_limit_bytes=24 * MIB),
        cost_estimate=pl.CostEstimate(flops=0, bytes_accessed=4 * ring * depth * strip, transcendentals=0),
        name="pack_pieces",
    )(*args)


def beta_kernel(slots, xs, cols_ref, place_ref, *refs):
    own_ref, twin_ref = refs[:2]
    message_refs = refs[2:-5]
    out_ref, picked_ref, blocks_ref, picked_sem, blocks_sem = refs[-5:]
    block = blocks_ref.shape[-1]
    sources = own_ref.shape[0]
    per_strip = own_ref.shape[2] // block
    _, both_rows, _ = picked_ref.shape
    rows = both_rows // CORES
    half = blocks_ref.shape[1] // 2
    outer = message_refs[0].shape[0]
    dest, tile = pl.program_id(0), pl.program_id(1)
    core, x_here, parity = place_ref[0], place_ref[1], place_ref[2]

    @pl.when((dest == 0) & (tile == 0))
    def _():
        for which, ref in enumerate((own_ref, twin_ref)):
            at = pl.multiple_of((core ^ which) * rows, rows)
            for src in range(sources):
                for s in range(per_strip):
                    pltpu.make_async_copy(
                        ref.at[src, pl.ds(0, rows), pl.ds(s * block, block)],
                        picked_ref.at[src * per_strip + s, pl.ds(at, rows)],
                        picked_sem,
                    ).start()
        for z in range(outer):
            for q in range(xs):
                for r in range(2):
                    d = z * xs + (x_here ^ q)
                    at = pl.multiple_of((parity ^ r) * half, half)
                    pltpu.make_async_copy(
                        message_refs[q * 2 + r].at[z], blocks_ref.at[d, pl.ds(at, half)], blocks_sem.at[d]
                    ).start()
        pltpu.make_async_copy(picked_ref, picked_ref, picked_sem).wait()

    @pl.when(tile == 0)
    def _():
        pltpu.make_async_copy(blocks_ref.at[dest], blocks_ref.at[dest], blocks_sem.at[dest]).wait()

    size = out_ref.shape[1]
    here = pl.ds(pl.multiple_of(tile * size, size), size)
    strip = dest * CORES + core
    parts = []
    for n in range(per_strip):
        wide = jnp.concatenate(
            [picked_ref[cols_ref[(strip * per_strip + n) * slots + k], here, :] for k in range(slots)], axis=1
        )
        tall = blocks_ref[dest, n * slots * block : (n + 1) * slots * block, :]
        parts.append(jnp.dot(wide, tall, preferred_element_type=jnp.float32))
    term = jnp.concatenate(parts, axis=1) if per_strip > 1 else parts[0]
    out_ref[0] = to_words(term)


def beta_term(slots, xs, columns, place, own, twin, messages, rows):
    sources, _, strip = own.shape
    outer, half, block = messages[0].shape
    dests = outer * xs
    both = rows * CORES
    size = math.gcd(both, 512)
    count = sources * strip // block
    return pl.pallas_call(
        functools.partial(beta_kernel, slots, xs),
        grid_spec=pltpu.PrefetchScalarGridSpec(
            num_scalar_prefetch=2,
            grid=(dests, both // size),
            in_specs=[ANYWHERE] * (2 + len(messages)),
            out_specs=pl.BlockSpec((1, size, strip), lambda d, m, *_: (d, m, 0)),
            scratch_shapes=[
                pltpu.VMEM((count, both, block), jnp.bfloat16),
                pltpu.VMEM((dests, 2 * half, block), jnp.bfloat16),
                pltpu.SemaphoreType.DMA,
                pltpu.SemaphoreType.DMA((dests,)),
            ],
        ),
        out_shape=jax.ShapeDtypeStruct((dests, both, strip), jnp.int16),
        compiler_params=pltpu.CompilerParams(vmem_limit_bytes=44 * MIB),
        cost_estimate=pl.CostEstimate(
            flops=4 * dests * both * strip * slots * block,
            bytes_accessed=8 * half * block * dests + 4 * count * both * block,
            transcendentals=0,
        ),
        name="beta_term",
    )(columns, place, own, twin, *messages)


def alpha_kernel(pieces, cols_ref, place_ref, *refs):
    blocks_ref, diag_ref = refs[pieces : pieces + 2]
    out_ref, whole_ref = refs[-2:]
    own_ref = refs[0]
    owned, slots, block, _ = blocks_ref.shape
    rows = own_ref.shape[1]
    for s in range(pieces):
        at = pl.multiple_of(lax.rem(place_ref[3] + s, pieces) * rows, rows)
        whole_ref[pl.ds(at, rows), :] = refs[s][0]

    @pl.loop(0, owned)
    def _(r):
        picked = []
        for k in range(slots):
            at = pl.multiple_of(cols_ref[r * slots + k] * block, block)
            picked.append(whole_ref[pl.ds(at, block), :])
        tall = jnp.concatenate(picked, axis=0)
        wide = jnp.concatenate([blocks_ref[r, k] for k in range(slots)], axis=1)
        term = jnp.dot(wide, tall, preferred_element_type=jnp.float32)
        here = pl.ds(pl.multiple_of(r * block, block), block)
        out_ref[0, here, :] = term + diag_ref[here, :] * own_ref[0, here, :].astype(jnp.float32)


def alpha_term(columns, place, own, others, blocks, diagonal, first, count, before):
    vectors, rows, strip = own.shape
    owned, slots, block, _ = blocks.shape
    pieces = 1 + len(others)
    once = pl.Buffered(1)
    mine = pl.BlockSpec((1, rows, strip), lambda v, *_: (first + v, 0, 0))
    in_specs = (
        [mine]
        + [pl.BlockSpec((1, rows, strip), lambda v, *_: (v, 0, 0))] * len(others)
        + [
            pl.BlockSpec(blocks.shape, lambda v, *_: (0, 0, 0, 0), pipeline_mode=once),
            pl.BlockSpec(diagonal.shape, lambda v, *_: (0, 0), pipeline_mode=once),
        ]
    )
    args = [columns, place, own, *others, blocks, diagonal]
    aliases = {}
    if before is not None:
        aliases = {len(args): 0}
        args.append(before)
        in_specs.append(ANYWHERE)
    return pl.pallas_call(
        functools.partial(alpha_kernel, pieces),
        grid_spec=pltpu.PrefetchScalarGridSpec(
            num_scalar_prefetch=2,
            grid=(count,),
            in_specs=in_specs,
            out_specs=mine,
            scratch_shapes=[pltpu.VMEM((pieces * rows, strip), jnp.bfloat16)],
        ),
        out_shape=jax.ShapeDtypeStruct((vectors, rows, strip), jnp.float32),
        input_output_aliases=aliases,
        compiler_params=pltpu.CompilerParams(vmem_limit_bytes=44 * MIB),
        cost_estimate=pl.CostEstimate(
            flops=6 * count * rows * strip * slots * block,
            bytes_accessed=count * rows * strip * (2 * pieces + 4) + blocks.size * 2 + diagonal.size * 4,
            transcendentals=0,
        ),
        name="alpha_term",
    )(*args)


def join_kernel(few_rows, acc_ref, words_ref, *rest):
    out_ref = rest[-1]
    for j in range(words_ref.shape[0]):
        for c in range(CORES):
            here = pl.ds((j * CORES + c) * few_rows, few_rows)
            out_ref[0, here, :] = (acc_ref[0, here, :] + from_words(words_ref[j, c, 0])).astype(jnp.bfloat16)


def join(acc, words, first, vectors, before):
    _, rows, strip = acc.shape
    sources = words.shape[0]
    few_rows = rows // (sources * CORES)
    words = words.reshape(sources, CORES, -1, few_rows, strip)
    count = words.shape[2]
    in_specs = [
        pl.BlockSpec((1, rows, strip), lambda v: (first + v, 0, 0)),
        pl.BlockSpec((sources, CORES, 1, few_rows, strip), lambda v: (0, 0, v, 0, 0)),
    ]
    args = [acc, words]
    aliases = {}
    if before is not None:
        in_specs.append(ANYWHERE)
        args.append(before)
        aliases = {2: 0}
    return pl.pallas_call(
        functools.partial(join_kernel, few_rows),
        grid=(count,),
        in_specs=in_specs,
        out_specs=pl.BlockSpec((1, rows, strip), lambda v: (first + v, 0, 0)),
        out_shape=jax.ShapeDtypeStruct((vectors, rows, strip), jnp.bfloat16),
        input_output_aliases=aliases,
        compiler_params=pltpu.CompilerParams(vmem_limit_bytes=32 * MIB),
        cost_estimate=pl.CostEstimate(
            flops=8 * count * rows * strip, bytes_accessed=8 * count * rows * strip, transcendentals=0
        ),
        name="join_terms",
    )(*args)


def after(value, earlier):
    return lax.optimization_barrier((value, earlier))[0]


def shards(ring, ring_a, ci_vectors, alpha_blocks, alpha_cols, beta_blocks, beta_cols, diagonal):
    vectors, rows, strip = ci_vectors.shape
    few_rows = rows // ring
    owned, slots, block, _ = beta_blocks.shape
    outer = 4
    inner = ring // outer
    xs = inner // CORES
    at_a, at_b = lax.axis_index("alpha"), lax.axis_index("beta")
    parity = lax.rem(at_a, 2)
    place = jnp.stack([lax.rem(at_b, CORES), lax.rem(lax.div(at_b, CORES), xs), parity, at_a]).astype(jnp.int32)
    few = vectors // 4
    cuts = [(vectors - few, few), (0, vectors - few)]
    shares = [(0, few), (few, few), (2 * few, vectors - 2 * few)]
    sent = [ci_vectors[first : first + count] for first, count in shares]

    def swap(value, bit):
        return lax.ppermute(value, "beta", [(i, i ^ bit) for i in range(ring)])

    def across(value):
        return lax.ppermute(value, "alpha", [(i, i ^ 1) for i in range(ring_a)])

    def exchange(value):
        return [
            lax.ppermute(value, "alpha", [((i + s) % ring_a, i) for i in range(ring_a)]) for s in range(1, ring_a)
        ]

    others = [exchange(sent[0])]

    stored = beta_blocks.reshape(2, owned * slots // 2, block, block)
    mine = lax.dynamic_index_in_dim(stored, parity, 0, keepdims=False)
    mine = mine.transpose(0, 2, 1).reshape(-1, block)
    far = [[o * inner + i for o in range(outer)] for i in range(inner)]
    carried = lax.all_gather(mine, "beta", axis=0, tiled=False, axis_index_groups=far)
    gathered = carried
    carried = [after(carried, tuple(sent[1:]))]
    bit = CORES
    while bit < inner:
        carried = carried + [swap(m, bit) for m in carried]
        bit *= 2

    heads = jnp.pad(beta_cols.reshape(1, -1).astype(jnp.bfloat16), ((0, TILE - 1), (0, strip - owned * slots)))
    turned = []
    for i, (first, count) in enumerate(cuts):
        piece = pack(ci_vectors, heads if i == 0 else None, first, count, ring)
        if i > 0:
            piece = after(piece, (turned[i - 1], gathered, others[0][-1]))
        turned.append(lax.all_to_all(piece, "beta", split_axis=0, concat_axis=0, tiled=True))
    columns = turned[0][:, cuts[0][1] * few_rows, : owned * slots].reshape(-1).astype(jnp.int32)
    twins = [swap(turned[0], 1)]

    messages = []
    for m in carried:
        if messages:
            m = after(m, (messages[-1], twins[0]))
        messages += [m, across(m)]
    for value in sent[1:]:
        others.append(exchange(after(value, messages[-1])))

    acc = None
    for (first, count), others_now in zip(shares, others):
        acc = alpha_term(
            alpha_cols.reshape(-1), place, ci_vectors, others_now, alpha_blocks, diagonal, first, count, acc
        )

    near = [[j * CORES + c for j in range(ring // CORES)] for c in range(CORES)]
    total = None
    last = turned[-1]
    for i, (first, count) in enumerate(cuts):
        if i > 0:
            twins.append(swap(after(turned[i], term), 1))
        term = beta_term(slots, xs, columns, place, turned[i], twins[i], messages, count * few_rows)
        term = after(term, last if i == 0 else (last, others[1][-1]))
        words = lax.all_to_all(term, "beta", split_axis=0, concat_axis=0, tiled=True, axis_index_groups=near)
        last = words
        total = join(acc, words, first, vectors, total)
    return total


def solution(mesh):
    placed = (
        P(None, "alpha", "beta"),
        P("alpha", None, None, None),
        P("alpha", None),
        P("beta", None, None, None),
        P("beta", None),
        P("alpha", "beta"),
    )
    return jax.shard_map(
        functools.partial(shards, mesh.shape["beta"], mesh.shape["alpha"]),
        mesh=mesh,
        in_specs=placed,
        out_specs=P(None, "alpha", "beta"),
        check_vma=False,
    )
```

```python
import functools
import math

import jax
import jax.numpy as jnp
from jax import lax
from jax.experimental import pallas as pl
from jax.experimental.pallas import tpu as pltpu
from jax.sharding import PartitionSpec as P

MIB = 1 << 20
STEPS_PER_OCTAVE = 8
SHIFT = 1000
CODE_BITS = 11
LARGEST = 32767.0
TILE = 16
HINTS = (42, 4)
CORES = 2
ANYWHERE = pl.BlockSpec(memory_space=pl.ANY)


def row_scale(code):
    return jnp.exp2((code - SHIFT).astype(jnp.float32) * (1.0 / STEPS_PER_OCTAVE))


def to_words(values):
    top = jnp.maximum(jnp.max(jnp.abs(values), axis=1, keepdims=True), 2.0 ** -100)
    code = jnp.ceil(jnp.log2(top) * STEPS_PER_OCTAVE + 0.01).astype(jnp.int32) + SHIFT
    words = jnp.round(values * (LARGEST / row_scale(code))).astype(jnp.int32)
    head = words[:, :128]
    lane = lax.broadcasted_iota(jnp.int32, head.shape, 1)
    bit = lax.shift_right_logical(jnp.broadcast_to(code, head.shape), jnp.minimum(lane, CODE_BITS)) & 1
    head = jnp.where(lane < CODE_BITS, (head & -2) | bit, head)
    if words.shape[1] > 128:
        head = jnp.concatenate([head, words[:, 128:]], axis=1)
    return head.astype(jnp.int16)


def bit_weights():
    lane = lax.broadcasted_iota(jnp.int32, (128, 128), 0)
    weight = jnp.where(lane < CODE_BITS, lax.shift_left(jnp.ones_like(lane), jnp.minimum(lane, CODE_BITS)), 0)
    return weight.astype(jnp.float32).astype(jnp.bfloat16)


def from_words(words, weights):
    words = words.astype(jnp.int32)
    bits = (words[:, :128] & 1).astype(jnp.float32).astype(jnp.bfloat16)
    code = jnp.dot(bits, weights, preferred_element_type=jnp.float32)
    scale = jnp.exp2((code - SHIFT) * (1.0 / STEPS_PER_OCTAVE)) * (1.0 / LARGEST)
    if words.shape[1] > 128:
        scale = jnp.concatenate([scale] * (words.shape[1] // 128), axis=1)
    return words.astype(jnp.float32) * scale


def pack_kernel(source_ref, *refs):
    out_ref = refs[-1]
    count, wide, _ = source_ref.shape
    dests = out_ref.shape[0]
    few_rows = wide // dests
    for d in range(dests):
        for v in range(count):
            out_ref[d, v * few_rows : (v + 1) * few_rows, :] = source_ref[v, d * few_rows : (d + 1) * few_rows, :]
        if len(refs) == 2:
            out_ref[d, count * few_rows :, :] = refs[0][...]


def pack(ci_vectors, heads, first, count, ring):
    _, rows, strip = ci_vectors.shape
    few_rows = rows // ring
    depth = count * few_rows + (0 if heads is None else TILE)
    each = 4
    in_specs = [pl.BlockSpec((count, each * few_rows, strip), lambda d: (first // count, d, 0))]
    args = [ci_vectors]
    if heads is not None:
        in_specs.append(pl.BlockSpec((TILE, strip), lambda d: (0, 0)))
        args.append(heads)
    return pl.pallas_call(
        pack_kernel,
        grid=(ring // each,),
        in_specs=in_specs,
        out_specs=pl.BlockSpec((each, depth, strip), lambda d: (d, 0, 0)),
        out_shape=jax.ShapeDtypeStruct((ring, depth, strip), jnp.bfloat16),
        compiler_params=pltpu.CompilerParams(vmem_limit_bytes=24 * MIB),
        cost_estimate=pl.CostEstimate(flops=0, bytes_accessed=4 * ring * depth * strip, transcendentals=0),
        name="pack_pieces",
    )(*args)


def beta_kernel(slots, xs, cols_ref, place_ref, *refs):
    own_ref, twin_ref = refs[:2]
    message_refs = refs[2:-5]
    out_ref, picked_ref, blocks_ref, picked_sem, blocks_sem = refs[-5:]
    block = blocks_ref.shape[-1]
    sources = own_ref.shape[0]
    per_strip = own_ref.shape[2] // block
    _, both_rows, _ = picked_ref.shape
    rows = both_rows // CORES
    half = blocks_ref.shape[1] // 2
    outer = message_refs[0].shape[0]
    dest, tile = pl.program_id(0), pl.program_id(1)
    core, x_here, parity = place_ref[0], place_ref[1], place_ref[2]

    @pl.when((dest == 0) & (tile == 0))
    def _():
        for which, ref in enumerate((own_ref, twin_ref)):
            at = pl.multiple_of((core ^ which) * rows, rows)
            for src in range(sources):
                for s in range(per_strip):
                    pltpu.make_async_copy(
                        ref.at[src, pl.ds(0, rows), pl.ds(s * block, block)],
                        picked_ref.at[src * per_strip + s, pl.ds(at, rows)],
                        picked_sem,
                    ).start()
        for z in range(outer):
            for q in range(xs):
                for r in range(2):
                    d = z * xs + (x_here ^ q)
                    at = pl.multiple_of((parity ^ r) * half, half)
                    pltpu.make_async_copy(
                        message_refs[q * 2 + r].at[z], blocks_ref.at[d, pl.ds(at, half)], blocks_sem.at[d]
                    ).start()
        pltpu.make_async_copy(picked_ref, picked_ref, picked_sem).wait()

    @pl.when(tile == 0)
    def _():
        pltpu.make_async_copy(blocks_ref.at[dest], blocks_ref.at[dest], blocks_sem.at[dest]).wait()

    size = out_ref.shape[1]
    here = pl.ds(pl.multiple_of(tile * size, size), size)
    strip = dest * CORES + core
    parts = []
    for n in range(per_strip):
        wide = jnp.concatenate(
            [picked_ref[cols_ref[(strip * per_strip + n) * slots + k], here, :] for k in range(slots)], axis=1
        )
        tall = blocks_ref[dest, n * slots * block : (n + 1) * slots * block, :]
        parts.append(jnp.dot(wide, tall, preferred_element_type=jnp.float32))
    term = jnp.concatenate(parts, axis=1) if per_strip > 1 else parts[0]
    out_ref[0] = to_words(term)


def beta_term(slots, xs, columns, place, own, twin, messages, rows, hint):
    sources, _, strip = own.shape
    outer, half, block = messages[0].shape
    dests = outer * xs
    both = rows * CORES
    size = math.gcd(both, 512)
    count = sources * strip // block
    return pl.pallas_call(
        functools.partial(beta_kernel, slots, xs),
        grid_spec=pltpu.PrefetchScalarGridSpec(
            num_scalar_prefetch=2,
            grid=(dests, both // size),
            in_specs=[ANYWHERE] * (2 + len(messages)),
            out_specs=pl.BlockSpec((1, size, strip), lambda d, m, *_: (d, m, 0)),
            scratch_shapes=[
                pltpu.VMEM((count, both, block), jnp.bfloat16),
                pltpu.VMEM((dests, 2 * half, block), jnp.bfloat16),
                pltpu.SemaphoreType.DMA,
                pltpu.SemaphoreType.DMA((dests,)),
            ],
        ),
        out_shape=jax.ShapeDtypeStruct((dests, both, strip), jnp.int16),
        compiler_params=pltpu.CompilerParams(vmem_limit_bytes=44 * MIB),
        cost_estimate=pl.CostEstimate(
            flops=hint * dests * both * strip * slots * block,
            bytes_accessed=8 * half * block * dests + 4 * count * both * block,
            transcendentals=0,
        ),
        name="beta_term",
    )(columns, place, own, twin, *messages)


def alpha_kernel(pieces, cols_ref, place_ref, *refs):
    blocks_ref, diag_ref = refs[pieces : pieces + 2]
    out_ref, whole_ref = refs[-2:]
    own_ref = refs[0]
    owned, slots, block, _ = blocks_ref.shape
    rows = own_ref.shape[1]
    for s in range(pieces):
        at = pl.multiple_of(lax.rem(place_ref[3] + s, pieces) * rows, rows)
        whole_ref[pl.ds(at, rows), :] = refs[s][0]

    @pl.loop(0, owned)
    def _(r):
        picked = []
        for k in range(slots):
            at = pl.multiple_of(cols_ref[r * slots + k] * block, block)
            picked.append(whole_ref[pl.ds(at, block), :])
        tall = jnp.concatenate(picked, axis=0)
        wide = jnp.concatenate([blocks_ref[r, k] for k in range(slots)], axis=1)
        term = jnp.dot(wide, tall, preferred_element_type=jnp.float32)
        here = pl.ds(pl.multiple_of(r * block, block), block)
        out_ref[0, here, :] = term + diag_ref[here, :] * own_ref[0, here, :].astype(jnp.float32)


def alpha_term(columns, place, own, others, blocks, diagonal, first, count, before):
    vectors, rows, strip = own.shape
    owned, slots, block, _ = blocks.shape
    pieces = 1 + len(others)
    once = pl.Buffered(1)
    mine = pl.BlockSpec((1, rows, strip), lambda v, *_: (first + v, 0, 0))
    in_specs = (
        [mine]
        + [pl.BlockSpec((1, rows, strip), lambda v, *_: (v, 0, 0))] * len(others)
        + [
            pl.BlockSpec(blocks.shape, lambda v, *_: (0, 0, 0, 0), pipeline_mode=once),
            pl.BlockSpec(diagonal.shape, lambda v, *_: (0, 0), pipeline_mode=once),
        ]
    )
    args = [columns, place, own, *others, blocks, diagonal]
    aliases = {}
    if before is not None:
        aliases = {len(args): 0}
        args.append(before)
        in_specs.append(ANYWHERE)
    return pl.pallas_call(
        functools.partial(alpha_kernel, pieces),
        grid_spec=pltpu.PrefetchScalarGridSpec(
            num_scalar_prefetch=2,
            grid=(count,),
            in_specs=in_specs,
            out_specs=mine,
            scratch_shapes=[pltpu.VMEM((pieces * rows, strip), jnp.bfloat16)],
        ),
        out_shape=jax.ShapeDtypeStruct((vectors, rows, strip), jnp.float32),
        input_output_aliases=aliases,
        compiler_params=pltpu.CompilerParams(vmem_limit_bytes=44 * MIB),
        cost_estimate=pl.CostEstimate(
            flops=6 * count * rows * strip * slots * block,
            bytes_accessed=count * rows * strip * (2 * pieces + 4) + blocks.size * 2 + diagonal.size * 4,
            transcendentals=0,
        ),
        name="alpha_term",
    )(*args)


def join_kernel(few_rows, acc_ref, words_ref, *rest):
    out_ref = rest[-1]
    weights = bit_weights()
    for j in range(words_ref.shape[0]):
        for c in range(CORES):
            here = pl.ds((j * CORES + c) * few_rows, few_rows)
            out_ref[0, here, :] = (acc_ref[0, here, :] + from_words(words_ref[j, c, 0], weights)).astype(jnp.bfloat16)


def join(acc, words, first, vectors, before):
    _, rows, strip = acc.shape
    sources = words.shape[0]
    few_rows = rows // (sources * CORES)
    words = words.reshape(sources, CORES, -1, few_rows, strip)
    count = words.shape[2]
    in_specs = [
        pl.BlockSpec((1, rows, strip), lambda v: (first + v, 0, 0)),
        pl.BlockSpec((sources, CORES, 1, few_rows, strip), lambda v: (0, 0, v, 0, 0)),
    ]
    args = [acc, words]
    aliases = {}
    if before is not None:
        in_specs.append(ANYWHERE)
        args.append(before)
        aliases = {2: 0}
    return pl.pallas_call(
        functools.partial(join_kernel, few_rows),
        grid=(count,),
        in_specs=in_specs,
        out_specs=pl.BlockSpec((1, rows, strip), lambda v: (first + v, 0, 0)),
        out_shape=jax.ShapeDtypeStruct((vectors, rows, strip), jnp.bfloat16),
        input_output_aliases=aliases,
        compiler_params=pltpu.CompilerParams(vmem_limit_bytes=32 * MIB),
        cost_estimate=pl.CostEstimate(
            flops=8 * count * rows * strip, bytes_accessed=8 * count * rows * strip, transcendentals=0
        ),
        name="join_terms",
    )(*args)


def after(value, earlier):
    return lax.optimization_barrier((value, earlier))[0]


def shards(ring, ring_a, ci_vectors, alpha_blocks, alpha_cols, beta_blocks, beta_cols, diagonal):
    vectors, rows, strip = ci_vectors.shape
    few_rows = rows // ring
    owned, slots, block, _ = beta_blocks.shape
    outer = 4
    inner = ring // outer
    xs = inner // CORES
    at_a, at_b = lax.axis_index("alpha"), lax.axis_index("beta")
    parity = lax.rem(at_a, 2)
    place = jnp.stack([lax.rem(at_b, CORES), lax.rem(lax.div(at_b, CORES), xs), parity, at_a]).astype(jnp.int32)
    few = vectors // 4
    cuts = [(vectors - few, few), (0, vectors - few)]
    shares = [(0, few), (few, few), (2 * few, vectors - 2 * few)]
    sent = [ci_vectors[first : first + count] for first, count in shares]

    def swap(value, bit):
        return lax.ppermute(value, "beta", [(i, i ^ bit) for i in range(ring)])

    def across(value):
        return lax.ppermute(value, "alpha", [(i, i ^ 1) for i in range(ring_a)])

    def exchange(value):
        return [
            lax.ppermute(value, "alpha", [((i + s) % ring_a, i) for i in range(ring_a)]) for s in range(1, ring_a)
        ]

    others = [exchange(sent[0])]

    stored = beta_blocks.reshape(2, owned * slots // 2, block, block)
    mine = lax.dynamic_index_in_dim(stored, parity, 0, keepdims=False)
    mine = mine.transpose(0, 2, 1).reshape(-1, block)
    far = [[o * inner + i for o in range(outer)] for i in range(inner)]
    carried = lax.all_gather(mine, "beta", axis=0, tiled=False, axis_index_groups=far)
    gathered = carried
    carried = [after(carried, tuple(sent[1:]))]
    bit = CORES
    while bit < inner:
        carried = carried + [swap(m, bit) for m in carried]
        bit *= 2

    heads = jnp.pad(beta_cols.reshape(1, -1).astype(jnp.bfloat16), ((0, TILE - 1), (0, strip - owned * slots)))
    turned = []
    for i, (first, count) in enumerate(cuts):
        piece = pack(ci_vectors, heads if i == 0 else None, first, count, ring)
        piece = after(piece, (turned[i - 1], gathered, others[0][-1]) if i > 0 else mine)
        turned.append(lax.all_to_all(piece, "beta", split_axis=0, concat_axis=0, tiled=True))
    columns = turned[0][:, cuts[0][1] * few_rows, : owned * slots].reshape(-1).astype(jnp.int32)
    twins = [swap(turned[0], 1)]

    messages = []
    for m in carried:
        if messages:
            m = after(m, (messages[-1], twins[0]))
        messages += [m, across(m)]
    for value in sent[1:]:
        others.append(exchange(after(value, messages[-1])))

    acc = None
    for (first, count), others_now in zip(shares, others):
        acc = alpha_term(
            alpha_cols.reshape(-1), place, ci_vectors, others_now, alpha_blocks, diagonal, first, count, acc
        )

    near = [[j * CORES + c for j in range(ring // CORES)] for c in range(CORES)]
    total = None
    last = turned[-1]
    for i, (first, count) in enumerate(cuts):
        if i > 0:
            twins.append(swap(after(turned[i], term), 1))
        term = beta_term(slots, xs, columns, place, turned[i], twins[i], messages, count * few_rows, HINTS[i])
        term = after(term, last if i == 0 else (last, others[1][-1]))
        words = lax.all_to_all(term, "beta", split_axis=0, concat_axis=0, tiled=True, axis_index_groups=near)
        last = words
        total = join(acc, words, first, vectors, total)
    return total


def solution(mesh):
    placed = (
        P(None, "alpha", "beta"),
        P("alpha", None, None, None),
        P("alpha", None),
        P("beta", None, None, None),
        P("beta", None),
        P("alpha", "beta"),
    )
    return jax.shard_map(
        functools.partial(shards, mesh.shape["beta"], mesh.shape["alpha"]),
        mesh=mesh,
        in_specs=placed,
        out_specs=P(None, "alpha", "beta"),
        check_vma=False,
    )
```

```python
import functools
import math

import jax
import jax.numpy as jnp
from jax import lax
from jax.experimental import pallas as pl
from jax.experimental.pallas import tpu as pltpu
from jax.sharding import PartitionSpec as P

MIB = 1 << 20
STEPS_PER_OCTAVE = 8
SHIFT = 1000
CODE_BITS = 11
LARGEST = 32767.0
TILE = 16
HINTS = (42, 4)
VMEM = 60 * MIB
CORES = 2
ANYWHERE = pl.BlockSpec(memory_space=pl.ANY)


def row_scale(code):
    return jnp.exp2((code - SHIFT).astype(jnp.float32) * (1.0 / STEPS_PER_OCTAVE))


def to_words(values):
    top = jnp.maximum(jnp.max(jnp.abs(values), axis=1, keepdims=True), 2.0 ** -100)
    code = jnp.ceil(jnp.log2(top) * STEPS_PER_OCTAVE + 0.01).astype(jnp.int32) + SHIFT
    words = jnp.round(values * (LARGEST / row_scale(code))).astype(jnp.int32)
    head = words[:, :128]
    lane = lax.broadcasted_iota(jnp.int32, head.shape, 1)
    bit = lax.shift_right_logical(jnp.broadcast_to(code, head.shape), jnp.minimum(lane, CODE_BITS)) & 1
    head = jnp.where(lane < CODE_BITS, (head & -2) | bit, head)
    if words.shape[1] > 128:
        head = jnp.concatenate([head, words[:, 128:]], axis=1)
    return head.astype(jnp.int16)


def bit_weights():
    lane = lax.broadcasted_iota(jnp.int32, (128, 128), 0)
    weight = jnp.where(lane < CODE_BITS, lax.shift_left(jnp.ones_like(lane), jnp.minimum(lane, CODE_BITS)), 0)
    return weight.astype(jnp.float32).astype(jnp.bfloat16)


def from_words(words, weights):
    words = words.astype(jnp.int32)
    bits = (words[:, :128] & 1).astype(jnp.float32).astype(jnp.bfloat16)
    code = jnp.dot(bits, weights, preferred_element_type=jnp.float32)
    scale = jnp.exp2((code - SHIFT) * (1.0 / STEPS_PER_OCTAVE)) * (1.0 / LARGEST)
    if words.shape[1] > 128:
        scale = jnp.concatenate([scale] * (words.shape[1] // 128), axis=1)
    return words.astype(jnp.float32) * scale


def pack_kernel(source_ref, *refs):
    out_ref = refs[-1]
    count, wide, _ = source_ref.shape
    dests = out_ref.shape[0]
    few_rows = wide // dests
    for d in range(dests):
        for v in range(count):
            out_ref[d, v * few_rows : (v + 1) * few_rows, :] = source_ref[v, d * few_rows : (d + 1) * few_rows, :]
        if len(refs) == 2:
            out_ref[d, count * few_rows :, :] = refs[0][...]


def pack(ci_vectors, heads, first, count, ring):
    _, rows, strip = ci_vectors.shape
    few_rows = rows // ring
    depth = count * few_rows + (0 if heads is None else TILE)
    each = 4
    in_specs = [pl.BlockSpec((count, each * few_rows, strip), lambda d: (first // count, d, 0))]
    args = [ci_vectors]
    if heads is not None:
        in_specs.append(pl.BlockSpec((TILE, strip), lambda d: (0, 0)))
        args.append(heads)
    return pl.pallas_call(
        pack_kernel,
        grid=(ring // each,),
        in_specs=in_specs,
        out_specs=pl.BlockSpec((each, depth, strip), lambda d: (d, 0, 0)),
        out_shape=jax.ShapeDtypeStruct((ring, depth, strip), jnp.bfloat16),
        compiler_params=pltpu.CompilerParams(vmem_limit_bytes=VMEM),
        cost_estimate=pl.CostEstimate(flops=0, bytes_accessed=4 * ring * depth * strip, transcendentals=0),
        name="pack_pieces",
    )(*args)


def turn_kernel(place_ref, blocks_ref, out_ref):
    _, count, block, _ = blocks_ref.shape
    for k in range(count):
        out_ref[k * block : (k + 1) * block, :] = blocks_ref[0, k].T


def turn_half(place, stored):
    _, count, block, _ = stored.shape
    return pl.pallas_call(
        turn_kernel,
        grid_spec=pltpu.PrefetchScalarGridSpec(
            num_scalar_prefetch=1,
            grid=(1,),
            in_specs=[pl.BlockSpec((1, count, block, block), lambda g, place_ref: (place_ref[2], 0, 0, 0))],
            out_specs=pl.BlockSpec((count * block, block), lambda g, place_ref: (0, 0)),
        ),
        out_shape=jax.ShapeDtypeStruct((count * block, block), jnp.bfloat16),
        compiler_params=pltpu.CompilerParams(vmem_limit_bytes=VMEM),
        cost_estimate=pl.CostEstimate(flops=0, bytes_accessed=4 * count * block * block, transcendentals=0),
        name="turn_blocks",
    )(place, stored)


def row_tile(rows):
    return max(t for t in range(TILE, 513, TILE) if rows % t == 0)


def beta_kernel(slots, xs, cols_ref, place_ref, *refs):
    sources_of_rows = refs[:2]
    message_refs = refs[2:-5]
    out_ref, picked_ref, blocks_ref, picked_sem, blocks_sem = refs[-5:]
    block = blocks_ref.shape[-1]
    sources = sources_of_rows[0].shape[0]
    per_strip = sources_of_rows[0].shape[2] // block
    size = out_ref.shape[1]
    tiles = picked_ref.shape[0]
    half = blocks_ref.shape[1] // 2
    outer = message_refs[0].shape[0]
    tile, dest = pl.program_id(0), pl.program_id(1)
    core, x_here, parity = place_ref[0], place_ref[1], place_ref[2]

    def fetch_rows(t):
        ref, at = sources_of_rows[t // (tiles // CORES)], t % (tiles // CORES) * size
        for src in range(sources):
            for s in range(per_strip):
                pltpu.make_async_copy(
                    ref.at[src, pl.ds(at, size), pl.ds(s * block, block)],
                    picked_ref.at[t, src * per_strip + s],
                    picked_sem.at[t],
                ).start()

    @pl.when((tile == 0) & (dest == 0))
    def _():
        fetch_rows(0)
        for z in range(outer):
            for q in range(xs):
                for r in range(2):
                    d = z * xs + (x_here ^ q)
                    at = pl.multiple_of((parity ^ r) * half, half)
                    pltpu.make_async_copy(
                        message_refs[q * 2 + r].at[z], blocks_ref.at[d, pl.ds(at, half)], blocks_sem.at[d]
                    ).start()
        for t in range(1, tiles):
            fetch_rows(t)

    @pl.when(dest == 0)
    def _():
        pltpu.make_async_copy(picked_ref.at[tile], picked_ref.at[tile], picked_sem.at[tile]).wait()

    @pl.when(tile == 0)
    def _():
        pltpu.make_async_copy(blocks_ref.at[dest], blocks_ref.at[dest], blocks_sem.at[dest]).wait()

    strip = dest * CORES + core
    parts = []
    for n in range(per_strip):
        wide = jnp.concatenate(
            [picked_ref[tile, cols_ref[(strip * per_strip + n) * slots + k]] for k in range(slots)], axis=1
        )
        tall = blocks_ref[dest, n * slots * block : (n + 1) * slots * block, :]
        parts.append(jnp.dot(wide, tall, preferred_element_type=jnp.float32))
    term = jnp.concatenate(parts, axis=1) if per_strip > 1 else parts[0]
    out_ref[0] = to_words(term)


def beta_term(slots, xs, columns, place, own, twin, messages, rows, hint):
    sources, _, strip = own.shape
    outer, half, block = messages[0].shape
    dests = outer * xs
    both = rows * CORES
    size = row_tile(rows)
    per_core = rows // size
    tiles = CORES * per_core
    count = sources * strip // block

    def out_at(t, d, cols_ref, place_ref):
        return d, (place_ref[0] ^ (t // per_core)) * per_core + t % per_core, 0

    return pl.pallas_call(
        functools.partial(beta_kernel, slots, xs),
        grid_spec=pltpu.PrefetchScalarGridSpec(
            num_scalar_prefetch=2,
            grid=(tiles, dests),
            in_specs=[ANYWHERE] * (2 + len(messages)),
            out_specs=pl.BlockSpec((1, size, strip), out_at),
            scratch_shapes=[
                pltpu.VMEM((tiles, count, size, block), jnp.bfloat16),
                pltpu.VMEM((dests, 2 * half, block), jnp.bfloat16),
                pltpu.SemaphoreType.DMA((tiles,)),
                pltpu.SemaphoreType.DMA((dests,)),
            ],
        ),
        out_shape=jax.ShapeDtypeStruct((dests, both, strip), jnp.int16),
        compiler_params=pltpu.CompilerParams(vmem_limit_bytes=VMEM),
        cost_estimate=pl.CostEstimate(
            flops=hint * dests * both * strip * slots * block,
            bytes_accessed=8 * half * block * dests + 4 * count * both * block,
            transcendentals=0,
        ),
        name="beta_term",
    )(columns, place, own, twin, *messages)


def alpha_kernel(pieces, cols_ref, place_ref, *refs):
    blocks_ref, diag_ref = refs[pieces : pieces + 2]
    out_ref, whole_ref = refs[-2:]
    own_ref = refs[0]
    owned, slots, block, _ = blocks_ref.shape
    rows = own_ref.shape[1]
    for s in range(pieces):
        at = pl.multiple_of(lax.rem(place_ref[3] + s, pieces) * rows, rows)
        whole_ref[pl.ds(at, rows), :] = refs[s][0]

    @pl.loop(0, owned)
    def _(r):
        picked = []
        for k in range(slots):
            at = pl.multiple_of(cols_ref[r * slots + k] * block, block)
            picked.append(whole_ref[pl.ds(at, block), :])
        tall = jnp.concatenate(picked, axis=0)
        wide = jnp.concatenate([blocks_ref[r, k] for k in range(slots)], axis=1)
        term = jnp.dot(wide, tall, preferred_element_type=jnp.float32)
        here = pl.ds(pl.multiple_of(r * block, block), block)
        out_ref[0, here, :] = term + diag_ref[here, :] * own_ref[0, here, :].astype(jnp.float32)


def alpha_term(columns, place, own, others, blocks, diagonal, first, count, before):
    vectors, rows, strip = own.shape
    owned, slots, block, _ = blocks.shape
    pieces = 1 + len(others)
    once = pl.Buffered(1)
    mine = pl.BlockSpec((1, rows, strip), lambda v, *_: (first + v, 0, 0))
    in_specs = (
        [mine]
        + [pl.BlockSpec((1, rows, strip), lambda v, *_: (v, 0, 0))] * len(others)
        + [
            pl.BlockSpec(blocks.shape, lambda v, *_: (0, 0, 0, 0), pipeline_mode=once),
            pl.BlockSpec(diagonal.shape, lambda v, *_: (0, 0), pipeline_mode=once),
        ]
    )
    args = [columns, place, own, *others, blocks, diagonal]
    aliases = {}
    if before is not None:
        aliases = {len(args): 0}
        args.append(before)
        in_specs.append(ANYWHERE)
    return pl.pallas_call(
        functools.partial(alpha_kernel, pieces),
        grid_spec=pltpu.PrefetchScalarGridSpec(
            num_scalar_prefetch=2,
            grid=(count,),
            in_specs=in_specs,
            out_specs=mine,
            scratch_shapes=[pltpu.VMEM((pieces * rows, strip), jnp.bfloat16)],
        ),
        out_shape=jax.ShapeDtypeStruct((vectors, rows, strip), jnp.float32),
        input_output_aliases=aliases,
        compiler_params=pltpu.CompilerParams(vmem_limit_bytes=VMEM),
        cost_estimate=pl.CostEstimate(
            flops=6 * count * rows * strip * slots * block,
            bytes_accessed=count * rows * strip * (2 * pieces + 4) + blocks.size * 2 + diagonal.size * 4,
            transcendentals=0,
        ),
        name="alpha_term",
    )(*args)


def join_kernel(few_rows, acc_ref, words_ref, *rest):
    out_ref = rest[-1]
    weights = bit_weights()
    for j in range(words_ref.shape[0]):
        for c in range(CORES):
            here = pl.ds((j * CORES + c) * few_rows, few_rows)
            out_ref[0, here, :] = (acc_ref[0, here, :] + from_words(words_ref[j, c, 0], weights)).astype(jnp.bfloat16)


def join(acc, words, first, vectors, before):
    _, rows, strip = acc.shape
    sources = words.shape[0]
    few_rows = rows // (sources * CORES)
    words = words.reshape(sources, CORES, -1, few_rows, strip)
    count = words.shape[2]
    cut = 2
    here = pl.BlockSpec((1, rows // cut, strip), lambda v, h: (first + v, h, 0))
    in_specs = [here, pl.BlockSpec((sources // cut, CORES, 1, few_rows, strip), lambda v, h: (h, 0, v, 0, 0))]
    args = [acc, words]
    aliases = {}
    if before is not None:
        in_specs.append(ANYWHERE)
        args.append(before)
        aliases = {2: 0}
    return pl.pallas_call(
        functools.partial(join_kernel, few_rows),
        grid=(count, cut),
        in_specs=in_specs,
        out_specs=here,
        out_shape=jax.ShapeDtypeStruct((vectors, rows, strip), jnp.bfloat16),
        input_output_aliases=aliases,
        compiler_params=pltpu.CompilerParams(vmem_limit_bytes=VMEM),
        cost_estimate=pl.CostEstimate(
            flops=8 * count * rows * strip, bytes_accessed=8 * count * rows * strip, transcendentals=0
        ),
        name="join_terms",
    )(*args)


def after(value, earlier):
    return lax.optimization_barrier((value, earlier))[0]


def shards(ring, ring_a, ci_vectors, alpha_blocks, alpha_cols, beta_blocks, beta_cols, diagonal):
    vectors, rows, strip = ci_vectors.shape
    few_rows = rows // ring
    owned, slots, block, _ = beta_blocks.shape
    outer = 4
    inner = ring // outer
    xs = inner // CORES
    at_a, at_b = lax.axis_index("alpha"), lax.axis_index("beta")
    parity = lax.rem(at_a, 2)
    place = jnp.stack([lax.rem(at_b, CORES), lax.rem(lax.div(at_b, CORES), xs), parity, at_a]).astype(jnp.int32)
    few = vectors // 4
    cuts = [(vectors - few, few), (0, vectors - few)]
    early = (3 * vectors) // 8
    shares = [(0, early), (early, vectors // 2 - early), (vectors // 2, vectors - vectors // 2)]
    sent = [ci_vectors[first : first + count] for first, count in shares]

    def swap(value, bit):
        return lax.ppermute(value, "beta", [(i, i ^ bit) for i in range(ring)])

    def across(value):
        return lax.ppermute(value, "alpha", [(i, i ^ 1) for i in range(ring_a)])

    def exchange(value):
        return [
            lax.ppermute(value, "alpha", [((i + s) % ring_a, i) for i in range(ring_a)]) for s in range(1, ring_a)
        ]

    mine = turn_half(place, beta_blocks.reshape(2, owned * slots // 2, block, block))
    far = [[o * inner + i for o in range(outer)] for i in range(inner)]
    gathered = lax.all_gather(mine, "beta", axis=0, tiled=False, axis_index_groups=far)

    heads = jnp.pad(beta_cols.reshape(1, -1).astype(jnp.bfloat16), ((0, TILE - 1), (0, strip - owned * slots)))
    pieces = [pack(ci_vectors, heads if i == 0 else None, *cut, ring) for i, cut in enumerate(cuts)]
    pieces[0] = after(pieces[0], mine)

    others = [exchange(after(sent[0], (pieces[1], *sent[1:])))]

    carried = [gathered]
    bit = CORES
    while bit < inner:
        carried = carried + [swap(m, bit) for m in carried]
        bit *= 2

    turned = []
    for i, piece in enumerate(pieces):
        if i > 0:
            piece = after(piece, (turned[i - 1], gathered, others[0][-1]))
        turned.append(lax.all_to_all(piece, "beta", split_axis=0, concat_axis=0, tiled=True))
    columns = turned[0][:, cuts[0][1] * few_rows, : owned * slots].reshape(-1).astype(jnp.int32)
    twins = [swap(turned[0], 1)]

    messages = []
    for m in carried:
        if messages:
            m = after(m, (messages[-1], twins[0]))
        messages += [m, across(m)]
    for value in sent[1:]:
        others.append(exchange(after(value, messages[-1])))

    acc = None
    for (first, count), others_now in zip(shares, others):
        acc = alpha_term(
            alpha_cols.reshape(-1), place, ci_vectors, others_now, alpha_blocks, diagonal, first, count, acc
        )

    near = [[j * CORES + c for j in range(ring // CORES)] for c in range(CORES)]
    total = None
    last = turned[-1]
    for i, (first, count) in enumerate(cuts):
        if i > 0:
            twins.append(swap(after(turned[i], term), 1))
        term = beta_term(slots, xs, columns, place, turned[i], twins[i], messages, count * few_rows, HINTS[i])
        term = after(term, last if i == 0 else (last, others[1][-1]))
        words = lax.all_to_all(term, "beta", split_axis=0, concat_axis=0, tiled=True, axis_index_groups=near)
        last = words
        total = join(acc, words, first, vectors, total)
    return total


def solution(mesh):
    placed = (
        P(None, "alpha", "beta"),
        P("alpha", None, None, None),
        P("alpha", None),
        P("beta", None, None, None),
        P("beta", None),
        P("alpha", "beta"),
    )
    return jax.shard_map(
        functools.partial(shards, mesh.shape["beta"], mesh.shape["alpha"]),
        mesh=mesh,
        in_specs=placed,
        out_specs=P(None, "alpha", "beta"),
        check_vma=False,
    )
```

```python
import functools
import math

import jax
import jax.numpy as jnp
from jax import lax
from jax.experimental import pallas as pl
from jax.experimental.pallas import tpu as pltpu
from jax.sharding import PartitionSpec as P

MIB = 1 << 20
STEPS_PER_OCTAVE = 8
SHIFT = 1000
CODE_BITS = 11
LARGEST = 32767.0
TILE = 16
HINTS = (4, 4)
VMEM = 60 * MIB
CORES = 2
ANYWHERE = pl.BlockSpec(memory_space=pl.ANY)


def row_scale(code):
    return jnp.exp2((code - SHIFT).astype(jnp.float32) * (1.0 / STEPS_PER_OCTAVE))


def to_words(values):
    top = jnp.maximum(jnp.max(jnp.abs(values), axis=1, keepdims=True), 2.0 ** -100)
    code = jnp.ceil(jnp.log2(top) * STEPS_PER_OCTAVE + 0.01).astype(jnp.int32) + SHIFT
    words = jnp.round(values * (LARGEST / row_scale(code))).astype(jnp.int32)
    head = words[:, :128]
    lane = lax.broadcasted_iota(jnp.int32, head.shape, 1)
    bit = lax.shift_right_logical(jnp.broadcast_to(code, head.shape), jnp.minimum(lane, CODE_BITS)) & 1
    head = jnp.where(lane < CODE_BITS, (head & -2) | bit, head)
    if words.shape[1] > 128:
        head = jnp.concatenate([head, words[:, 128:]], axis=1)
    return head.astype(jnp.int16)


def bit_weights():
    lane = lax.broadcasted_iota(jnp.int32, (128, 128), 0)
    weight = jnp.where(lane < CODE_BITS, lax.shift_left(jnp.ones_like(lane), jnp.minimum(lane, CODE_BITS)), 0)
    return weight.astype(jnp.float32).astype(jnp.bfloat16)


def from_words(words, weights):
    words = words.astype(jnp.int32)
    bits = (words[:, :128] & 1).astype(jnp.float32).astype(jnp.bfloat16)
    code = jnp.dot(bits, weights, preferred_element_type=jnp.float32)
    scale = jnp.exp2((code - SHIFT) * (1.0 / STEPS_PER_OCTAVE)) * (1.0 / LARGEST)
    if words.shape[1] > 128:
        scale = jnp.concatenate([scale] * (words.shape[1] // 128), axis=1)
    return words.astype(jnp.float32) * scale


def pack_kernel(source_ref, *refs):
    out_ref = refs[-1]
    count, wide, _ = source_ref.shape
    dests = out_ref.shape[0]
    few_rows = wide // dests
    for d in range(dests):
        for v in range(count):
            out_ref[d, v * few_rows : (v + 1) * few_rows, :] = source_ref[v, d * few_rows : (d + 1) * few_rows, :]
        if len(refs) == 2:
            out_ref[d, count * few_rows :, :] = refs[0][...]


def pack(ci_vectors, heads, first, count, ring):
    _, rows, strip = ci_vectors.shape
    few_rows = rows // ring
    depth = count * few_rows + (0 if heads is None else TILE)
    each = 4
    in_specs = [pl.BlockSpec((count, each * few_rows, strip), lambda d: (first // count, d, 0))]
    args = [ci_vectors]
    if heads is not None:
        in_specs.append(pl.BlockSpec((TILE, strip), lambda d: (0, 0)))
        args.append(heads)
    return pl.pallas_call(
        pack_kernel,
        grid=(ring // each,),
        in_specs=in_specs,
        out_specs=pl.BlockSpec((each, depth, strip), lambda d: (d, 0, 0)),
        out_shape=jax.ShapeDtypeStruct((ring, depth, strip), jnp.bfloat16),
        compiler_params=pltpu.CompilerParams(vmem_limit_bytes=VMEM),
        cost_estimate=pl.CostEstimate(flops=0, bytes_accessed=4 * ring * depth * strip, transcendentals=0),
        name="pack_pieces",
    )(*args)


def turn_kernel(place_ref, blocks_ref, out_ref):
    _, count, block, _ = blocks_ref.shape
    for k in range(count):
        out_ref[k * block : (k + 1) * block, :] = blocks_ref[0, k].T


def turn_half(place, stored):
    _, count, block, _ = stored.shape
    return pl.pallas_call(
        turn_kernel,
        grid_spec=pltpu.PrefetchScalarGridSpec(
            num_scalar_prefetch=1,
            grid=(1,),
            in_specs=[pl.BlockSpec((1, count, block, block), lambda g, place_ref: (place_ref[2], 0, 0, 0))],
            out_specs=pl.BlockSpec((count * block, block), lambda g, place_ref: (0, 0)),
        ),
        out_shape=jax.ShapeDtypeStruct((count * block, block), jnp.bfloat16),
        compiler_params=pltpu.CompilerParams(vmem_limit_bytes=VMEM),
        cost_estimate=pl.CostEstimate(flops=0, bytes_accessed=4 * count * block * block, transcendentals=0),
        name="turn_blocks",
    )(place, stored)


def beta_kernel(slots, xs, segments, pieces, cols_ref, place_ref, *refs):
    x_refs = refs[: 2 * len(segments)]
    message_refs = refs[2 * len(segments) : -5]
    out_ref, picked_ref, blocks_ref, picked_sem, blocks_sem = refs[-5:]
    block = blocks_ref.shape[-1]
    sources = x_refs[0].shape[0]
    per_strip = x_refs[0].shape[2] // block
    tiles, _, size, _ = picked_ref.shape
    rows = size * tiles // CORES
    quarter = blocks_ref.shape[1] // (2 * pieces)
    outer = message_refs[0].shape[0]
    tile, dest = pl.program_id(0), pl.program_id(1)
    core, x_here, parity = place_ref[0], place_ref[1], place_ref[2]

    def fetch_rows(t):
        for w in range(CORES // tiles):
            which = t * (CORES // tiles) + w
            base = 0 if tiles == CORES else (core ^ which) * rows
            for i, (start, count) in enumerate(segments):
                at = pl.multiple_of(base + sum(n for _, n in segments[:i]), TILE)
                for src in range(sources):
                    for s in range(per_strip):
                        pltpu.make_async_copy(
                            x_refs[2 * i + which].at[src, pl.ds(start, count), pl.ds(s * block, block)],
                            picked_ref.at[t, src * per_strip + s, pl.ds(at, count)],
                            picked_sem.at[t],
                        ).start()

    @pl.when((tile == 0) & (dest == 0))
    def _():
        fetch_rows(0)
        for z in range(outer):
            for q in range(xs):
                for p in range(pieces):
                    for r in range(2):
                        d = z * xs + (x_here ^ q)
                        at = pl.multiple_of(((parity ^ r) * pieces + p) * quarter, quarter)
                        pltpu.make_async_copy(
                            message_refs[(p * xs + q) * 2 + r].at[z],
                            blocks_ref.at[d, pl.ds(at, quarter)],
                            blocks_sem.at[d],
                        ).start()
        for t in range(1, tiles):
            fetch_rows(t)

    @pl.when(dest == 0)
    def _():
        pltpu.make_async_copy(picked_ref.at[tile], picked_ref.at[tile], picked_sem.at[tile]).wait()

    @pl.when(tile == 0)
    def _():
        pltpu.make_async_copy(blocks_ref.at[dest], blocks_ref.at[dest], blocks_sem.at[dest]).wait()

    strip = dest * CORES + core
    parts = []
    for n in range(per_strip):
        wide = jnp.concatenate(
            [picked_ref[tile, cols_ref[(strip * per_strip + n) * slots + k]] for k in range(slots)], axis=1
        )
        tall = blocks_ref[dest, n * slots * block : (n + 1) * slots * block, :]
        parts.append(jnp.dot(wide, tall, preferred_element_type=jnp.float32))
    term = jnp.concatenate(parts, axis=1) if per_strip > 1 else parts[0]
    out_ref[0] = to_words(term)


def beta_term(slots, xs, columns, place, parts, messages, pieces, hint):
    sources, _, strip = parts[0][0].shape
    outer, quarter, block = messages[0].shape
    dests = outer * xs
    segments = [(start, count) for _, _, start, count in parts]
    rows = sum(count for _, count in segments)
    tiles = CORES if rows >= 512 else 1
    size = rows * CORES // tiles
    count = sources * strip // block
    depth = 2 * pieces * quarter
    arrays = [a for own, twin, _, _ in parts for a in (own, twin)] + list(messages)

    def out_at(t, d, cols_ref, place_ref):
        return d, place_ref[0] ^ t if tiles == CORES else 0, 0

    return pl.pallas_call(
        functools.partial(beta_kernel, slots, xs, segments, pieces),
        grid_spec=pltpu.PrefetchScalarGridSpec(
            num_scalar_prefetch=2,
            grid=(tiles, dests),
            in_specs=[ANYWHERE] * len(arrays),
            out_specs=pl.BlockSpec((1, size, strip), out_at),
            scratch_shapes=[
                pltpu.VMEM((tiles, count, size, block), jnp.bfloat16),
                pltpu.VMEM((dests, depth, block), jnp.bfloat16),
                pltpu.SemaphoreType.DMA((tiles,)),
                pltpu.SemaphoreType.DMA((dests,)),
            ],
        ),
        out_shape=jax.ShapeDtypeStruct((dests, rows * CORES, strip), jnp.int16),
        compiler_params=pltpu.CompilerParams(vmem_limit_bytes=VMEM),
        cost_estimate=pl.CostEstimate(
            flops=hint * dests * rows * CORES * strip * slots * block,
            bytes_accessed=2 * depth * block * dests + 4 * count * rows * CORES * block,
            transcendentals=0,
        ),
        name="beta_term",
    )(columns, place, *arrays)


def alpha_kernel(pieces, cols_ref, place_ref, *refs):
    blocks_ref, diag_ref = refs[pieces : pieces + 2]
    out_ref, whole_ref = refs[-2:]
    own_ref = refs[0]
    owned, slots, block, _ = blocks_ref.shape
    rows = own_ref.shape[1]
    for s in range(pieces):
        at = pl.multiple_of(lax.rem(place_ref[3] + s, pieces) * rows, rows)
        whole_ref[pl.ds(at, rows), :] = refs[s][0]

    @pl.loop(0, owned)
    def _(r):
        picked = []
        for k in range(slots):
            at = pl.multiple_of(cols_ref[r * slots + k] * block, block)
            picked.append(whole_ref[pl.ds(at, block), :])
        tall = jnp.concatenate(picked, axis=0)
        wide = jnp.concatenate([blocks_ref[r, k] for k in range(slots)], axis=1)
        term = jnp.dot(wide, tall, preferred_element_type=jnp.float32)
        here = pl.ds(pl.multiple_of(r * block, block), block)
        out_ref[0, here, :] = term + diag_ref[here, :] * own_ref[0, here, :].astype(jnp.float32)


def alpha_term(columns, place, own, others, blocks, diagonal, first, count, base, total, before):
    _, rows, strip = own.shape
    owned, slots, block, _ = blocks.shape
    pieces = 1 + len(others)
    once = pl.Buffered(1)
    mine = pl.BlockSpec((1, rows, strip), lambda v, *_: (first + v, 0, 0))
    in_specs = (
        [mine]
        + [pl.BlockSpec((1, rows, strip), lambda v, *_: (v, 0, 0))] * len(others)
        + [
            pl.BlockSpec(blocks.shape, lambda v, *_: (0, 0, 0, 0), pipeline_mode=once),
            pl.BlockSpec(diagonal.shape, lambda v, *_: (0, 0), pipeline_mode=once),
        ]
    )
    args = [columns, place, own, *others, blocks, diagonal]
    aliases = {}
    if before is not None:
        aliases = {len(args): 0}
        args.append(before)
        in_specs.append(ANYWHERE)
    return pl.pallas_call(
        functools.partial(alpha_kernel, pieces),
        grid_spec=pltpu.PrefetchScalarGridSpec(
            num_scalar_prefetch=2,
            grid=(count,),
            in_specs=in_specs,
            out_specs=pl.BlockSpec((1, rows, strip), lambda v, *_: (first - base + v, 0, 0)),
            scratch_shapes=[pltpu.VMEM((pieces * rows, strip), jnp.bfloat16)],
        ),
        out_shape=jax.ShapeDtypeStruct((total, rows, strip), jnp.float32),
        input_output_aliases=aliases,
        compiler_params=pltpu.CompilerParams(vmem_limit_bytes=VMEM),
        cost_estimate=pl.CostEstimate(
            flops=6 * count * rows * strip * slots * block,
            bytes_accessed=count * rows * strip * (2 * pieces + 4) + blocks.size * 2 + diagonal.size * 4,
            transcendentals=0,
        ),
        name="alpha_term",
    )(*args)


def join_kernel(few_rows, acc_ref, words_ref, *rest):
    out_ref = rest[-1]
    weights = bit_weights()
    for j in range(words_ref.shape[0]):
        for c in range(CORES):
            here = pl.ds((j * CORES + c) * few_rows, few_rows)
            out_ref[0, here, :] = (acc_ref[0, here, :] + from_words(words_ref[j, c, 0], weights)).astype(jnp.bfloat16)


def join(acc, words, first, vectors, before):
    count, rows, strip = acc.shape
    sources = words.shape[0]
    few_rows = rows // (sources * CORES)
    words = words.reshape(sources, CORES, count, few_rows, strip)
    in_specs = [
        pl.BlockSpec((1, rows, strip), lambda v: (v, 0, 0)),
        pl.BlockSpec((sources, CORES, 1, few_rows, strip), lambda v: (0, 0, v, 0, 0)),
    ]
    args = [acc, words]
    aliases = {}
    if before is not None:
        in_specs.append(ANYWHERE)
        args.append(before)
        aliases = {2: 0}
    return pl.pallas_call(
        functools.partial(join_kernel, few_rows),
        grid=(count,),
        in_specs=in_specs,
        out_specs=pl.BlockSpec((1, rows, strip), lambda v: (first + v, 0, 0)),
        out_shape=jax.ShapeDtypeStruct((vectors, rows, strip), jnp.bfloat16),
        input_output_aliases=aliases,
        compiler_params=pltpu.CompilerParams(vmem_limit_bytes=24 * MIB),
        cost_estimate=pl.CostEstimate(
            flops=8 * count * rows * strip, bytes_accessed=8 * count * rows * strip, transcendentals=0
        ),
        name="join_terms",
    )(*args)


def after(value, earlier):
    return lax.optimization_barrier((value, earlier))[0]


def shards(ring, ring_a, ci_vectors, alpha_blocks, alpha_cols, beta_blocks, beta_cols, diagonal):
    vectors, rows, strip = ci_vectors.shape
    few_rows = rows // ring
    owned, slots, block, _ = beta_blocks.shape
    outer = 4
    inner = ring // outer
    xs = inner // CORES
    at_a, at_b = lax.axis_index("alpha"), lax.axis_index("beta")
    parity = lax.rem(at_a, 2)
    place = jnp.stack([lax.rem(at_b, CORES), lax.rem(lax.div(at_b, CORES), xs), parity, at_a]).astype(jnp.int32)
    few = vectors // 4
    cuts = [(0, vectors - few), (vectors - few, few)]
    back = [(0, few), (few, vectors - few)]
    shares = [(0, few), (few, few), (2 * few, vectors - 2 * few)]
    sent = [ci_vectors[first : first + count] for first, count in shares]
    pieces = 2

    def swap(value, bit):
        return lax.ppermute(value, "beta", [(i, i ^ bit) for i in range(ring)])

    def across(value):
        return lax.ppermute(value, "alpha", [(i, i ^ 1) for i in range(ring_a)])

    def exchange(value):
        return [
            lax.ppermute(value, "alpha", [((i + s) % ring_a, i) for i in range(ring_a)]) for s in range(1, ring_a)
        ]

    mine = turn_half(place, beta_blocks.reshape(2, owned * slots // 2, block, block))
    far = [[o * inner + i for o in range(outer)] for i in range(inner)]
    gathered = [
        lax.all_gather(m, "beta", axis=0, tiled=False, axis_index_groups=far) for m in jnp.split(mine, pieces)
    ]

    heads = jnp.pad(beta_cols.reshape(1, -1).astype(jnp.bfloat16), ((0, TILE - 1), (0, strip - owned * slots)))
    packed = [pack(ci_vectors, heads if i == 0 else None, *cut, ring) for i, cut in enumerate(cuts)]
    packed[0] = after(packed[0], mine)

    others = [exchange(after(sent[0], (packed[1], *sent[1:])))]

    messages = []
    for g in gathered:
        carried = [after(g, messages[-2] if messages else others[0][-1])]
        bit = CORES
        while bit < inner:
            carried = carried + [swap(m, bit) for m in carried]
            bit *= 2
        for m in carried:
            messages += [m, across(m)]

    turned = [lax.all_to_all(packed[0], "beta", split_axis=0, concat_axis=0, tiled=True)]
    ahead = tuple(messages[1:-1])
    second = after(packed[1], (turned[0], *ahead))
    turned.append(lax.all_to_all(second, "beta", split_axis=0, concat_axis=0, tiled=True))
    columns = turned[0][:, cuts[0][1] * few_rows, : owned * slots].reshape(-1).astype(jnp.int32)
    twins = [swap(after(turned[0], ahead), 1)]
    for value in sent[1:]:
        others.append(exchange(after(value, messages[-1])))

    def alpha(i, base, total, before):
        return alpha_term(
            alpha_cols.reshape(-1), place, ci_vectors, others[i], alpha_blocks, diagonal, *shares[i], base, total, before
        )

    acc = [alpha(0, 0, few, None), alpha(2, few, vectors - few, alpha(1, few, vectors - few, None))]

    near = [[j * CORES + c for j in range(ring // CORES)] for c in range(CORES)]

    def send_back(term):
        return lax.all_to_all(term, "beta", split_axis=0, concat_axis=0, tiled=True, axis_index_groups=near)

    rest = cuts[0][1] - few
    parts = [(turned[0], twins[0], 0, few * few_rows)]
    term = beta_term(slots, xs, columns, place, parts, messages, pieces, HINTS[0])
    twins.append(swap(after(turned[1], term), 1))
    words = [send_back(after(term, turned[1]))]
    parts = [
        (turned[0], twins[0], few * few_rows, rest * few_rows),
        (turned[1], twins[1], 0, few * few_rows),
    ]
    term = beta_term(slots, xs, columns, place, parts, messages, pieces, HINTS[1])
    words.append(send_back(after(term, (words[0], others[1][-1]))))

    total = None
    for i, (first, _) in enumerate(back):
        total = join(acc[i], words[i], first, vectors, total)
    return total


def solution(mesh):
    placed = (
        P(None, "alpha", "beta"),
        P("alpha", None, None, None),
        P("alpha", None),
        P("beta", None, None, None),
        P("beta", None),
        P("alpha", "beta"),
    )
    return jax.shard_map(
        functools.partial(shards, mesh.shape["beta"], mesh.shape["alpha"]),
        mesh=mesh,
        in_specs=placed,
        out_specs=P(None, "alpha", "beta"),
        check_vma=False,
    )
```

```python
import functools
import math

import jax
import jax.numpy as jnp
from jax import lax
from jax.experimental import pallas as pl
from jax.experimental.pallas import tpu as pltpu
from jax.sharding import PartitionSpec as P

MIB = 1 << 20
STEPS_PER_OCTAVE = 8
SHIFT = 1000
CODE_BITS = 11
LARGEST = 32767.0
TILE = 16
HINTS = (4, 4)
VMEM = 60 * MIB
CORES = 2
ANYWHERE = pl.BlockSpec(memory_space=pl.ANY)


def row_scale(code):
    return jnp.exp2((code - SHIFT).astype(jnp.float32) * (1.0 / STEPS_PER_OCTAVE))


def to_words(values):
    top = jnp.maximum(jnp.max(jnp.abs(values), axis=1, keepdims=True), 2.0 ** -100)
    code = jnp.ceil(jnp.log2(top) * STEPS_PER_OCTAVE + 0.01).astype(jnp.int32) + SHIFT
    words = jnp.round(values * (LARGEST / row_scale(code))).astype(jnp.int32)
    head = words[:, :128]
    lane = lax.broadcasted_iota(jnp.int32, head.shape, 1)
    bit = lax.shift_right_logical(jnp.broadcast_to(code, head.shape), jnp.minimum(lane, CODE_BITS)) & 1
    head = jnp.where(lane < CODE_BITS, (head & -2) | bit, head)
    if words.shape[1] > 128:
        head = jnp.concatenate([head, words[:, 128:]], axis=1)
    return head.astype(jnp.int16)


def bit_weights():
    lane = lax.broadcasted_iota(jnp.int32, (128, 128), 0)
    weight = jnp.where(lane < CODE_BITS, lax.shift_left(jnp.ones_like(lane), jnp.minimum(lane, CODE_BITS)), 0)
    return weight.astype(jnp.float32).astype(jnp.bfloat16)


def from_words(words, weights):
    words = words.astype(jnp.int32)
    bits = (words[:, :128] & 1).astype(jnp.float32).astype(jnp.bfloat16)
    code = jnp.dot(bits, weights, preferred_element_type=jnp.float32)
    scale = jnp.exp2((code - SHIFT) * (1.0 / STEPS_PER_OCTAVE)) * (1.0 / LARGEST)
    if words.shape[1] > 128:
        scale = jnp.concatenate([scale] * (words.shape[1] // 128), axis=1)
    return words.astype(jnp.float32) * scale


def pack_kernel(source_ref, *refs):
    out_ref = refs[-1]
    count, wide, _ = source_ref.shape
    dests = out_ref.shape[0]
    few_rows = wide // dests
    for d in range(dests):
        for v in range(count):
            out_ref[d, v * few_rows : (v + 1) * few_rows, :] = source_ref[v, d * few_rows : (d + 1) * few_rows, :]
        if len(refs) == 2:
            out_ref[d, count * few_rows :, :] = refs[0][...]


def pack(ci_vectors, heads, first, count, ring):
    _, rows, strip = ci_vectors.shape
    few_rows = rows // ring
    depth = count * few_rows + (0 if heads is None else TILE)
    each = 4
    in_specs = [pl.BlockSpec((count, each * few_rows, strip), lambda d: (first // count, d, 0))]
    args = [ci_vectors]
    if heads is not None:
        in_specs.append(pl.BlockSpec((TILE, strip), lambda d: (0, 0)))
        args.append(heads)
    return pl.pallas_call(
        pack_kernel,
        grid=(ring // each,),
        in_specs=in_specs,
        out_specs=pl.BlockSpec((each, depth, strip), lambda d: (d, 0, 0)),
        out_shape=jax.ShapeDtypeStruct((ring, depth, strip), jnp.bfloat16),
        compiler_params=pltpu.CompilerParams(vmem_limit_bytes=VMEM),
        cost_estimate=pl.CostEstimate(flops=0, bytes_accessed=4 * ring * depth * strip, transcendentals=0),
        name="pack_pieces",
    )(*args)


def turn_kernel(place_ref, blocks_ref, out_ref):
    _, count, block, _ = blocks_ref.shape
    for k in range(count):
        out_ref[k * block : (k + 1) * block, :] = blocks_ref[0, k].T


def turn_half(place, stored):
    _, count, block, _ = stored.shape
    return pl.pallas_call(
        turn_kernel,
        grid_spec=pltpu.PrefetchScalarGridSpec(
            num_scalar_prefetch=1,
            grid=(1,),
            in_specs=[pl.BlockSpec((1, count, block, block), lambda g, place_ref: (place_ref[2], 0, 0, 0))],
            out_specs=pl.BlockSpec((count * block, block), lambda g, place_ref: (0, 0)),
        ),
        out_shape=jax.ShapeDtypeStruct((count * block, block), jnp.bfloat16),
        compiler_params=pltpu.CompilerParams(vmem_limit_bytes=VMEM),
        cost_estimate=pl.CostEstimate(flops=0, bytes_accessed=4 * count * block * block, transcendentals=0),
        name="turn_blocks",
    )(place, stored)


def beta_kernel(slots, xs, segments, pieces, cols_ref, place_ref, *refs):
    x_refs = refs[: 2 * len(segments)]
    message_refs = refs[2 * len(segments) : -5]
    out_ref, picked_ref, blocks_ref, picked_sem, blocks_sem = refs[-5:]
    block = blocks_ref.shape[-1]
    sources = x_refs[0].shape[0]
    per_strip = x_refs[0].shape[2] // block
    tiles, _, size, _ = picked_ref.shape
    rows = size * tiles // CORES
    half = blocks_ref.shape[1] // 2
    outer = message_refs[0].shape[0]
    tile, dest = pl.program_id(0), pl.program_id(1)
    core, x_here, parity = place_ref[0], place_ref[1], place_ref[2]

    def fetch_rows(t):
        for w in range(CORES // tiles):
            which = t * (CORES // tiles) + w
            base = 0 if tiles == CORES else (core ^ which) * rows
            for i, (start, count) in enumerate(segments):
                at = pl.multiple_of(base + sum(n for _, n in segments[:i]), TILE)
                for src in range(sources):
                    for s in range(per_strip):
                        pltpu.make_async_copy(
                            x_refs[2 * i + which].at[src, pl.ds(start, count), pl.ds(s * block, block)],
                            picked_ref.at[t, src * per_strip + s, pl.ds(at, count)],
                            picked_sem.at[t],
                        ).start()

    @pl.when((tile == 0) & (dest == 0))
    def _():
        fetch_rows(0)
        for p in range(pieces):
            for z in range(outer):
                for q in range(xs):
                    for r in range(2):
                        d = (p * outer + z) * xs + (x_here ^ q)
                        at = pl.multiple_of((parity ^ r) * half, half)
                        pltpu.make_async_copy(
                            message_refs[(p * xs + q) * 2 + r].at[z],
                            blocks_ref.at[d, pl.ds(at, half)],
                            blocks_sem.at[d],
                        ).start()
        for t in range(1, tiles):
            fetch_rows(t)

    @pl.when(dest == 0)
    def _():
        pltpu.make_async_copy(picked_ref.at[tile], picked_ref.at[tile], picked_sem.at[tile]).wait()

    @pl.when(tile == 0)
    def _():
        pltpu.make_async_copy(blocks_ref.at[dest], blocks_ref.at[dest], blocks_sem.at[dest]).wait()

    strip = dest * CORES + core
    parts = []
    for n in range(per_strip):
        wide = jnp.concatenate(
            [picked_ref[tile, cols_ref[(strip * per_strip + n) * slots + k]] for k in range(slots)], axis=1
        )
        tall = blocks_ref[dest, n * slots * block : (n + 1) * slots * block, :]
        parts.append(jnp.dot(wide, tall, preferred_element_type=jnp.float32))
    term = jnp.concatenate(parts, axis=1) if per_strip > 1 else parts[0]
    out_ref[0] = to_words(term)


def beta_term(slots, xs, columns, place, parts, messages, pieces, hint):
    sources, _, strip = parts[0][0].shape
    outer, half, block = messages[0].shape
    dests = pieces * outer * xs
    segments = [(start, count) for _, _, start, count in parts]
    rows = sum(count for _, count in segments)
    tiles = CORES if rows >= 512 else 1
    size = rows * CORES // tiles
    count = sources * strip // block
    depth = 2 * half
    arrays = [a for own, twin, _, _ in parts for a in (own, twin)] + list(messages)

    def out_at(t, d, cols_ref, place_ref):
        return d, place_ref[0] ^ t if tiles == CORES else 0, 0

    return pl.pallas_call(
        functools.partial(beta_kernel, slots, xs, segments, pieces),
        grid_spec=pltpu.PrefetchScalarGridSpec(
            num_scalar_prefetch=2,
            grid=(tiles, dests),
            in_specs=[ANYWHERE] * len(arrays),
            out_specs=pl.BlockSpec((1, size, strip), out_at),
            scratch_shapes=[
                pltpu.VMEM((tiles, count, size, block), jnp.bfloat16),
                pltpu.VMEM((dests, depth, block), jnp.bfloat16),
                pltpu.SemaphoreType.DMA((tiles,)),
                pltpu.SemaphoreType.DMA((dests,)),
            ],
        ),
        out_shape=jax.ShapeDtypeStruct((dests, rows * CORES, strip), jnp.int16),
        compiler_params=pltpu.CompilerParams(vmem_limit_bytes=VMEM),
        cost_estimate=pl.CostEstimate(
            flops=hint * dests * rows * CORES * strip * slots * block,
            bytes_accessed=2 * depth * block * dests + 4 * count * rows * CORES * block,
            transcendentals=0,
        ),
        name="beta_term",
    )(columns, place, *arrays)


def alpha_kernel(pieces, cols_ref, place_ref, *refs):
    blocks_ref, diag_ref = refs[pieces : pieces + 2]
    out_ref, whole_ref = refs[-2:]
    own_ref = refs[0]
    owned, slots, block, _ = blocks_ref.shape
    rows = own_ref.shape[1]
    for s in range(pieces):
        at = pl.multiple_of(lax.rem(place_ref[3] + s, pieces) * rows, rows)
        whole_ref[pl.ds(at, rows), :] = refs[s][0]

    @pl.loop(0, owned)
    def _(r):
        picked = []
        for k in range(slots):
            at = pl.multiple_of(cols_ref[r * slots + k] * block, block)
            picked.append(whole_ref[pl.ds(at, block), :])
        tall = jnp.concatenate(picked, axis=0)
        wide = jnp.concatenate([blocks_ref[r, k] for k in range(slots)], axis=1)
        term = jnp.dot(wide, tall, preferred_element_type=jnp.float32)
        here = pl.ds(pl.multiple_of(r * block, block), block)
        out_ref[0, here, :] = term + diag_ref[here, :] * own_ref[0, here, :].astype(jnp.float32)


def alpha_term(columns, place, own, others, blocks, diagonal, first, count, base, total, before):
    _, rows, strip = own.shape
    owned, slots, block, _ = blocks.shape
    pieces = 1 + len(others)
    once = pl.Buffered(1)
    mine = pl.BlockSpec((1, rows, strip), lambda v, *_: (first + v, 0, 0))
    in_specs = (
        [mine]
        + [pl.BlockSpec((1, rows, strip), lambda v, *_: (v, 0, 0))] * len(others)
        + [
            pl.BlockSpec(blocks.shape, lambda v, *_: (0, 0, 0, 0), pipeline_mode=once),
            pl.BlockSpec(diagonal.shape, lambda v, *_: (0, 0), pipeline_mode=once),
        ]
    )
    args = [columns, place, own, *others, blocks, diagonal]
    aliases = {}
    if before is not None:
        aliases = {len(args): 0}
        args.append(before)
        in_specs.append(ANYWHERE)
    return pl.pallas_call(
        functools.partial(alpha_kernel, pieces),
        grid_spec=pltpu.PrefetchScalarGridSpec(
            num_scalar_prefetch=2,
            grid=(count,),
            in_specs=in_specs,
            out_specs=pl.BlockSpec((1, rows, strip), lambda v, *_: (first - base + v, 0, 0)),
            scratch_shapes=[pltpu.VMEM((pieces * rows, strip), jnp.bfloat16)],
        ),
        out_shape=jax.ShapeDtypeStruct((total, rows, strip), jnp.float32),
        input_output_aliases=aliases,
        compiler_params=pltpu.CompilerParams(vmem_limit_bytes=VMEM),
        cost_estimate=pl.CostEstimate(
            flops=6 * count * rows * strip * slots * block,
            bytes_accessed=count * rows * strip * (2 * pieces + 4) + blocks.size * 2 + diagonal.size * 4,
            transcendentals=0,
        ),
        name="alpha_term",
    )(*args)


def join_kernel(few_rows, acc_ref, words_ref, *rest):
    out_ref = rest[-1]
    weights = bit_weights()
    for j in range(words_ref.shape[0]):
        for c in range(CORES):
            here = pl.ds((j * CORES + c) * few_rows, few_rows)
            out_ref[0, here, :] = (acc_ref[0, here, :] + from_words(words_ref[j, c, 0], weights)).astype(jnp.bfloat16)


def join(acc, words, first, vectors, before):
    count, rows, strip = acc.shape
    sources = words.shape[0]
    few_rows = rows // (sources * CORES)
    words = words.reshape(sources, CORES, count, few_rows, strip)
    in_specs = [
        pl.BlockSpec((1, rows, strip), lambda v: (v, 0, 0)),
        pl.BlockSpec((sources, CORES, 1, few_rows, strip), lambda v: (0, 0, v, 0, 0)),
    ]
    args = [acc, words]
    aliases = {}
    if before is not None:
        in_specs.append(ANYWHERE)
        args.append(before)
        aliases = {2: 0}
    return pl.pallas_call(
        functools.partial(join_kernel, few_rows),
        grid=(count,),
        in_specs=in_specs,
        out_specs=pl.BlockSpec((1, rows, strip), lambda v: (first + v, 0, 0)),
        out_shape=jax.ShapeDtypeStruct((vectors, rows, strip), jnp.bfloat16),
        input_output_aliases=aliases,
        compiler_params=pltpu.CompilerParams(vmem_limit_bytes=VMEM),
        cost_estimate=pl.CostEstimate(
            flops=8 * count * rows * strip, bytes_accessed=8 * count * rows * strip, transcendentals=0
        ),
        name="join_terms",
    )(*args)


def after(value, earlier):
    return lax.optimization_barrier((value, earlier))[0]


def shards(ring, ring_a, ci_vectors, alpha_blocks, alpha_cols, beta_blocks, beta_cols, diagonal):
    vectors, rows, strip = ci_vectors.shape
    few_rows = rows // ring
    owned, slots, block, _ = beta_blocks.shape
    outer = 4
    inner = ring // outer
    xs = inner // CORES
    at_a, at_b = lax.axis_index("alpha"), lax.axis_index("beta")
    parity = lax.rem(at_a, 2)
    place = jnp.stack([lax.rem(at_b, CORES), lax.rem(lax.div(at_b, CORES), xs), parity, at_a]).astype(jnp.int32)
    few = vectors // 4
    cuts = [(0, vectors - few), (vectors - few, few)]
    back = [(0, few), (few, vectors - few)]
    shares = [(0, few), (few, few), (2 * few, vectors - 2 * few)]
    sent = [ci_vectors[first : first + count] for first, count in shares]
    pieces = 2

    def swap(value, bit):
        return lax.ppermute(value, "beta", [(i, i ^ bit) for i in range(ring)])

    def across(value):
        return lax.ppermute(value, "alpha", [(i, i ^ 1) for i in range(ring_a)])

    def exchange(value):
        return [
            lax.ppermute(value, "alpha", [((i + s) % ring_a, i) for i in range(ring_a)]) for s in range(1, ring_a)
        ]

    mine = turn_half(place, beta_blocks.reshape(2, owned * slots // 2, block, block))
    far = [[o * inner + i for o in range(outer)] for i in range(inner)]
    gathered = lax.all_gather(mine, "beta", axis=0, tiled=False, axis_index_groups=far)

    heads = jnp.pad(beta_cols.reshape(1, -1).astype(jnp.bfloat16), ((0, TILE - 1), (0, strip - owned * slots)))
    packed = [pack(ci_vectors, heads if i == 0 else None, *cut, ring) for i, cut in enumerate(cuts)]
    packed[0] = after(packed[0], mine)

    others = [exchange(after(sent[0], (packed[1], *sent[1:])))]

    messages = []
    for g in jnp.split(gathered, pieces):
        carried = [after(g, messages[-2]) if messages else g]
        bit = CORES
        while bit < inner:
            carried = carried + [swap(m, bit) for m in carried]
            bit *= 2
        for m in carried:
            messages += [m, across(m if messages else after(m, others[0][-1]))]

    turned = [lax.all_to_all(packed[0], "beta", split_axis=0, concat_axis=0, tiled=True)]
    ahead = tuple(messages[1:-1])
    second = after(packed[1], (turned[0], *ahead))
    turned.append(lax.all_to_all(second, "beta", split_axis=0, concat_axis=0, tiled=True))
    columns = turned[0][:, cuts[0][1] * few_rows, : owned * slots].reshape(-1).astype(jnp.int32)
    twins = [swap(after(turned[0], ahead), 1)]
    for value in sent[1:]:
        others.append(exchange(after(value, messages[-1])))

    def alpha(i, base, total, before):
        return alpha_term(
            alpha_cols.reshape(-1), place, ci_vectors, others[i], alpha_blocks, diagonal, *shares[i], base, total, before
        )

    acc = [alpha(0, 0, few, None), alpha(2, few, vectors - few, alpha(1, few, vectors - few, None))]

    near = [[j * CORES + c for j in range(ring // CORES)] for c in range(CORES)]

    def send_back(term):
        return lax.all_to_all(term, "beta", split_axis=0, concat_axis=0, tiled=True, axis_index_groups=near)

    rest = cuts[0][1] - few
    parts = [(turned[0], twins[0], 0, few * few_rows)]
    term = beta_term(slots, xs, columns, place, parts, messages, pieces, HINTS[0])
    twins.append(swap(after(turned[1], term), 1))
    words = [send_back(after(term, turned[1]))]
    parts = [
        (turned[0], twins[0], few * few_rows, rest * few_rows),
        (turned[1], twins[1], 0, few * few_rows),
    ]
    term = beta_term(slots, xs, columns, place, parts, messages, pieces, HINTS[1])
    words.append(send_back(after(term, (words[0], others[1][-1]))))

    total = None
    for i, (first, _) in enumerate(back):
        total = join(acc[i], words[i], first, vectors, total)
    return total


def solution(mesh):
    placed = (
        P(None, "alpha", "beta"),
        P("alpha", None, None, None),
        P("alpha", None),
        P("beta", None, None, None),
        P("beta", None),
        P("alpha", "beta"),
    )
    return jax.shard_map(
        functools.partial(shards, mesh.shape["beta"], mesh.shape["alpha"]),
        mesh=mesh,
        in_specs=placed,
        out_specs=P(None, "alpha", "beta"),
        check_vma=False,
    )
```

```python
import functools
import math

import jax
import jax.numpy as jnp
from jax import lax
from jax.experimental import pallas as pl
from jax.experimental.pallas import tpu as pltpu
from jax.sharding import PartitionSpec as P

MIB = 1 << 20
STEPS_PER_OCTAVE = 8
SHIFT = 1000
CODE_BITS = 11
LARGEST = 32767.0
TILE = 16
HINTS = (26, 4)
VMEM = 60 * MIB
CORES = 2
ANYWHERE = pl.BlockSpec(memory_space=pl.ANY)


def row_scale(code):
    return jnp.exp2((code - SHIFT).astype(jnp.float32) * (1.0 / STEPS_PER_OCTAVE))


def to_words(values):
    top = jnp.maximum(jnp.max(jnp.abs(values), axis=1, keepdims=True), 2.0 ** -100)
    code = jnp.ceil(jnp.log2(top) * STEPS_PER_OCTAVE + 0.01).astype(jnp.int32) + SHIFT
    words = jnp.round(values * (LARGEST / row_scale(code))).astype(jnp.int32)
    head = words[:, :128]
    lane = lax.broadcasted_iota(jnp.int32, head.shape, 1)
    bit = lax.shift_right_logical(jnp.broadcast_to(code, head.shape), jnp.minimum(lane, CODE_BITS)) & 1
    head = jnp.where(lane < CODE_BITS, (head & -2) | bit, head)
    if words.shape[1] > 128:
        head = jnp.concatenate([head, words[:, 128:]], axis=1)
    return head.astype(jnp.int16)


def bit_weights():
    lane = lax.broadcasted_iota(jnp.int32, (128, 128), 0)
    weight = jnp.where(lane < CODE_BITS, lax.shift_left(jnp.ones_like(lane), jnp.minimum(lane, CODE_BITS)), 0)
    return weight.astype(jnp.float32).astype(jnp.bfloat16)


def from_words(words, weights):
    words = words.astype(jnp.int32)
    bits = (words[:, :128] & 1).astype(jnp.float32).astype(jnp.bfloat16)
    code = jnp.dot(bits, weights, preferred_element_type=jnp.float32)
    scale = jnp.exp2((code - SHIFT) * (1.0 / STEPS_PER_OCTAVE)) * (1.0 / LARGEST)
    if words.shape[1] > 128:
        scale = jnp.concatenate([scale] * (words.shape[1] // 128), axis=1)
    return words.astype(jnp.float32) * scale


def pack_kernel(skip, count, source_ref, *refs):
    out_ref = refs[-1]
    dests = out_ref.shape[0]
    few_rows = source_ref.shape[1] // dests
    for d in range(dests):
        rows = slice(d * few_rows, (d + 1) * few_rows)
        for v in range(count):
            out_ref[d, v * few_rows : (v + 1) * few_rows, :] = source_ref[skip + v, rows, :]
        if len(refs) == 2:
            out_ref[d, count * few_rows :, :] = refs[0][...]


def pack(ci_vectors, heads, first, count, ring):
    vectors, rows, strip = ci_vectors.shape
    few_rows = rows // ring
    taken, at = (count, first // count) if first % count == 0 else (vectors, 0)
    depth = count * few_rows + (0 if heads is None else TILE)
    each = 4
    in_specs = [pl.BlockSpec((taken, each * few_rows, strip), lambda d: (at, d, 0))]
    args = [ci_vectors]
    if heads is not None:
        in_specs.append(pl.BlockSpec((TILE, strip), lambda d: (0, 0)))
        args.append(heads)
    return pl.pallas_call(
        functools.partial(pack_kernel, first - at * taken, count),
        grid=(ring // each,),
        in_specs=in_specs,
        out_specs=pl.BlockSpec((each, depth, strip), lambda d: (d, 0, 0)),
        out_shape=jax.ShapeDtypeStruct((ring, depth, strip), jnp.bfloat16),
        compiler_params=pltpu.CompilerParams(vmem_limit_bytes=VMEM),
        cost_estimate=pl.CostEstimate(flops=0, bytes_accessed=4 * ring * depth * strip, transcendentals=0),
        name="pack_pieces",
    )(*args)


def turn_kernel(place_ref, blocks_ref, out_ref):
    _, count, block, _ = blocks_ref.shape
    for k in range(count):
        out_ref[k * block : (k + 1) * block, :] = blocks_ref[0, k].T


def turn_half(place, stored):
    _, count, block, _ = stored.shape
    return pl.pallas_call(
        turn_kernel,
        grid_spec=pltpu.PrefetchScalarGridSpec(
            num_scalar_prefetch=1,
            grid=(1,),
            in_specs=[pl.BlockSpec((1, count, block, block), lambda g, place_ref: (place_ref[2], 0, 0, 0))],
            out_specs=pl.BlockSpec((count * block, block), lambda g, place_ref: (0, 0)),
        ),
        out_shape=jax.ShapeDtypeStruct((count * block, block), jnp.bfloat16),
        compiler_params=pltpu.CompilerParams(vmem_limit_bytes=VMEM),
        cost_estimate=pl.CostEstimate(flops=0, bytes_accessed=4 * count * block * block, transcendentals=0),
        name="turn_blocks",
    )(place, stored)


def beta_kernel(slots, xs, segments, pieces, cols_ref, place_ref, *refs):
    x_refs = refs[: 2 * len(segments)]
    message_refs = refs[2 * len(segments) : -5]
    out_ref, picked_ref, blocks_ref, picked_sem, blocks_sem = refs[-5:]
    block = blocks_ref.shape[-1]
    sources = x_refs[0].shape[0]
    per_strip = x_refs[0].shape[2] // block
    tiles, _, size, _ = picked_ref.shape
    rows = size * tiles // CORES
    half = blocks_ref.shape[1] // 2
    outer = message_refs[0].shape[0]
    tile, dest = pl.program_id(0), pl.program_id(1)
    core, x_here, parity = place_ref[0], place_ref[1], place_ref[2]

    def fetch_rows(t):
        for w in range(CORES // tiles):
            which = t * (CORES // tiles) + w
            base = 0 if tiles == CORES else (core ^ which) * rows
            for i, (start, count) in enumerate(segments):
                at = pl.multiple_of(base + sum(n for _, n in segments[:i]), TILE)
                for src in range(sources):
                    for s in range(per_strip):
                        pltpu.make_async_copy(
                            x_refs[2 * i + which].at[src, pl.ds(start, count), pl.ds(s * block, block)],
                            picked_ref.at[t, src * per_strip + s, pl.ds(at, count)],
                            picked_sem.at[t],
                        ).start()

    @pl.when((tile == 0) & (dest == 0))
    def _():
        fetch_rows(0)
        for p in range(pieces):
            for z in range(outer):
                for q in range(xs):
                    for r in range(2):
                        d = (p * outer + z) * xs + (x_here ^ q)
                        at = pl.multiple_of((parity ^ r) * half, half)
                        pltpu.make_async_copy(
                            message_refs[(p * xs + q) * 2 + r].at[z],
                            blocks_ref.at[d, pl.ds(at, half)],
                            blocks_sem.at[d],
                        ).start()
        for t in range(1, tiles):
            fetch_rows(t)

    @pl.when(dest == 0)
    def _():
        pltpu.make_async_copy(picked_ref.at[tile], picked_ref.at[tile], picked_sem.at[tile]).wait()

    @pl.when(tile == 0)
    def _():
        pltpu.make_async_copy(blocks_ref.at[dest], blocks_ref.at[dest], blocks_sem.at[dest]).wait()

    strip = dest * CORES + core
    parts = []
    for n in range(per_strip):
        wide = jnp.concatenate(
            [picked_ref[tile, cols_ref[(strip * per_strip + n) * slots + k]] for k in range(slots)], axis=1
        )
        tall = blocks_ref[dest, n * slots * block : (n + 1) * slots * block, :]
        parts.append(jnp.dot(wide, tall, preferred_element_type=jnp.float32))
    term = jnp.concatenate(parts, axis=1) if per_strip > 1 else parts[0]
    out_ref[0] = to_words(term)


def beta_term(slots, xs, columns, place, parts, messages, pieces, hint):
    sources, _, strip = parts[0][0].shape
    outer, half, block = messages[0].shape
    dests = pieces * outer * xs
    segments = [(start, count) for _, _, start, count in parts]
    rows = sum(count for _, count in segments)
    tiles = CORES if rows >= 512 else 1
    size = rows * CORES // tiles
    count = sources * strip // block
    depth = 2 * half
    arrays = [a for own, twin, _, _ in parts for a in (own, twin)] + list(messages)

    def out_at(t, d, cols_ref, place_ref):
        return d, place_ref[0] ^ t if tiles == CORES else 0, 0

    return pl.pallas_call(
        functools.partial(beta_kernel, slots, xs, segments, pieces),
        grid_spec=pltpu.PrefetchScalarGridSpec(
            num_scalar_prefetch=2,
            grid=(tiles, dests),
            in_specs=[ANYWHERE] * len(arrays),
            out_specs=pl.BlockSpec((1, size, strip), out_at),
            scratch_shapes=[
                pltpu.VMEM((tiles, count, size, block), jnp.bfloat16),
                pltpu.VMEM((dests, depth, block), jnp.bfloat16),
                pltpu.SemaphoreType.DMA((tiles,)),
                pltpu.SemaphoreType.DMA((dests,)),
            ],
        ),
        out_shape=jax.ShapeDtypeStruct((dests, rows * CORES, strip), jnp.int16),
        compiler_params=pltpu.CompilerParams(vmem_limit_bytes=VMEM),
        cost_estimate=pl.CostEstimate(
            flops=hint * dests * rows * CORES * strip * slots * block,
            bytes_accessed=2 * depth * block * dests + 4 * count * rows * CORES * block,
            transcendentals=0,
        ),
        name="beta_term",
    )(columns, place, *arrays)


def alpha_kernel(pieces, cols_ref, place_ref, *refs):
    blocks_ref, diag_ref = refs[pieces : pieces + 2]
    out_ref, whole_ref = refs[-2:]
    own_ref = refs[0]
    owned, slots, block, _ = blocks_ref.shape
    rows = own_ref.shape[1]
    for s in range(pieces):
        at = pl.multiple_of(lax.rem(place_ref[3] + s, pieces) * rows, rows)
        whole_ref[pl.ds(at, rows), :] = refs[s][0]

    @pl.loop(0, owned)
    def _(r):
        picked = []
        for k in range(slots):
            at = pl.multiple_of(cols_ref[r * slots + k] * block, block)
            picked.append(whole_ref[pl.ds(at, block), :])
        tall = jnp.concatenate(picked, axis=0)
        wide = jnp.concatenate([blocks_ref[r, k] for k in range(slots)], axis=1)
        term = jnp.dot(wide, tall, preferred_element_type=jnp.float32)
        here = pl.ds(pl.multiple_of(r * block, block), block)
        out_ref[0, here, :] = term + diag_ref[here, :] * own_ref[0, here, :].astype(jnp.float32)


def alpha_term(columns, place, own, others, blocks, diagonal, first, count, base, total, before):
    _, rows, strip = own.shape
    owned, slots, block, _ = blocks.shape
    pieces = 1 + len(others)
    once = pl.Buffered(1)
    mine = pl.BlockSpec((1, rows, strip), lambda v, *_: (first + v, 0, 0))
    in_specs = (
        [mine]
        + [pl.BlockSpec((1, rows, strip), lambda v, *_: (v, 0, 0))] * len(others)
        + [
            pl.BlockSpec(blocks.shape, lambda v, *_: (0, 0, 0, 0), pipeline_mode=once),
            pl.BlockSpec(diagonal.shape, lambda v, *_: (0, 0), pipeline_mode=once),
        ]
    )
    args = [columns, place, own, *others, blocks, diagonal]
    aliases = {}
    if before is not None:
        aliases = {len(args): 0}
        args.append(before)
        in_specs.append(ANYWHERE)
    return pl.pallas_call(
        functools.partial(alpha_kernel, pieces),
        grid_spec=pltpu.PrefetchScalarGridSpec(
            num_scalar_prefetch=2,
            grid=(count,),
            in_specs=in_specs,
            out_specs=pl.BlockSpec((1, rows, strip), lambda v, *_: (first - base + v, 0, 0)),
            scratch_shapes=[pltpu.VMEM((pieces * rows, strip), jnp.bfloat16)],
        ),
        out_shape=jax.ShapeDtypeStruct((total, rows, strip), jnp.float32),
        input_output_aliases=aliases,
        compiler_params=pltpu.CompilerParams(vmem_limit_bytes=VMEM),
        cost_estimate=pl.CostEstimate(
            flops=6 * count * rows * strip * slots * block,
            bytes_accessed=count * rows * strip * (2 * pieces + 4) + blocks.size * 2 + diagonal.size * 4,
            transcendentals=0,
        ),
        name="alpha_term",
    )(*args)


def join_kernel(few_rows, acc_ref, words_ref, *rest):
    out_ref = rest[-1]
    weights = bit_weights()
    for j in range(words_ref.shape[0]):
        for c in range(CORES):
            here = pl.ds((j * CORES + c) * few_rows, few_rows)
            out_ref[0, here, :] = (acc_ref[0, here, :] + from_words(words_ref[j, c, 0], weights)).astype(jnp.bfloat16)


def join(acc, words, first, vectors, before):
    count, rows, strip = acc.shape
    sources = words.shape[0]
    few_rows = rows // (sources * CORES)
    words = words.reshape(sources, CORES, count, few_rows, strip)
    in_specs = [
        pl.BlockSpec((1, rows, strip), lambda v: (v, 0, 0)),
        pl.BlockSpec((sources, CORES, 1, few_rows, strip), lambda v: (0, 0, v, 0, 0)),
    ]
    args = [acc, words]
    aliases = {}
    if before is not None:
        in_specs.append(ANYWHERE)
        args.append(before)
        aliases = {2: 0}
    return pl.pallas_call(
        functools.partial(join_kernel, few_rows),
        grid=(count,),
        in_specs=in_specs,
        out_specs=pl.BlockSpec((1, rows, strip), lambda v: (first + v, 0, 0)),
        out_shape=jax.ShapeDtypeStruct((vectors, rows, strip), jnp.bfloat16),
        input_output_aliases=aliases,
        compiler_params=pltpu.CompilerParams(vmem_limit_bytes=VMEM),
        cost_estimate=pl.CostEstimate(
            flops=8 * count * rows * strip, bytes_accessed=8 * count * rows * strip, transcendentals=0
        ),
        name="join_terms",
    )(*args)


def after(value, earlier):
    return lax.optimization_barrier((value, earlier))[0]


def shards(ring, ring_a, ci_vectors, alpha_blocks, alpha_cols, beta_blocks, beta_cols, diagonal):
    vectors, rows, strip = ci_vectors.shape
    few_rows = rows // ring
    owned, slots, block, _ = beta_blocks.shape
    outer = 4
    inner = ring // outer
    xs = inner // CORES
    at_a, at_b = lax.axis_index("alpha"), lax.axis_index("beta")
    parity = lax.rem(at_a, 2)
    place = jnp.stack([lax.rem(at_b, CORES), lax.rem(lax.div(at_b, CORES), xs), parity, at_a]).astype(jnp.int32)
    few = vectors // 4
    lead = 3 * vectors // 8
    cuts = [(0, lead), (lead, vectors - lead)]
    back = [(0, few), (few, vectors - few)]
    shares = [(0, few), (few, few), (2 * few, vectors - 2 * few)]
    sent = [ci_vectors[first : first + count] for first, count in shares]
    pieces = 2

    def swap(value, bit):
        return lax.ppermute(value, "beta", [(i, i ^ bit) for i in range(ring)])

    def across(value):
        return lax.ppermute(value, "alpha", [(i, i ^ 1) for i in range(ring_a)])

    def exchange(value):
        return [
            lax.ppermute(value, "alpha", [((i + s) % ring_a, i) for i in range(ring_a)]) for s in range(1, ring_a)
        ]

    mine = turn_half(place, beta_blocks.reshape(2, owned * slots // 2, block, block))
    far = [[o * inner + i for o in range(outer)] for i in range(inner)]
    gathered = lax.all_gather(mine, "beta", axis=0, tiled=False, axis_index_groups=far)

    heads = jnp.pad(beta_cols.reshape(1, -1).astype(jnp.bfloat16), ((0, TILE - 1), (0, strip - owned * slots)))
    packed = [pack(ci_vectors, heads if i == 0 else None, *cut, ring) for i, cut in enumerate(cuts)]

    others = [exchange(after(sent[0], (packed[1], *sent[1:])))]

    messages = []
    for g in jnp.split(gathered, pieces):
        carried = [after(g, messages[-2]) if messages else g]
        bit = CORES
        while bit < inner:
            carried = carried + [swap(m, bit) for m in carried]
            bit *= 2
        for m in carried:
            messages += [m, across(m)]

    turned = [lax.all_to_all(packed[0], "beta", split_axis=0, concat_axis=0, tiled=True)]
    second = after(packed[1], (turned[0], messages[0], others[0][-1]))
    turned.append(lax.all_to_all(second, "beta", split_axis=0, concat_axis=0, tiled=True))
    columns = turned[0][:, cuts[0][1] * few_rows, : owned * slots].reshape(-1).astype(jnp.int32)
    twins = [swap(after(turned[0], tuple(messages[1:-1])), 1)]
    for value in sent[1:]:
        others.append(exchange(after(value, messages[-1])))

    def alpha(i, base, total, before):
        return alpha_term(
            alpha_cols.reshape(-1), place, ci_vectors, others[i], alpha_blocks, diagonal, *shares[i], base, total, before
        )

    acc = [alpha(0, 0, few, None), alpha(2, few, vectors - few, alpha(1, few, vectors - few, None))]

    near = [[j * CORES + c for j in range(ring // CORES)] for c in range(CORES)]

    def send_back(term):
        return lax.all_to_all(term, "beta", split_axis=0, concat_axis=0, tiled=True, axis_index_groups=near)

    rest = cuts[0][1] - few
    parts = [(turned[0], twins[0], 0, few * few_rows)]
    term = beta_term(slots, xs, columns, place, parts, messages, pieces, HINTS[0])
    twins.append(swap(after(turned[1], term), 1))
    words = [send_back(after(term, turned[1]))]
    parts = [
        (turned[0], twins[0], few * few_rows, rest * few_rows),
        (turned[1], twins[1], 0, cuts[1][1] * few_rows),
    ]
    term = beta_term(slots, xs, columns, place, parts, messages, pieces, HINTS[1])
    words.append(send_back(after(term, (words[0], others[1][-1]))))

    total = None
    for i, (first, _) in enumerate(back):
        total = join(acc[i], words[i], first, vectors, total)
    return total


def solution(mesh):
    placed = (
        P(None, "alpha", "beta"),
        P("alpha", None, None, None),
        P("alpha", None),
        P("beta", None, None, None),
        P("beta", None),
        P("alpha", "beta"),
    )
    return jax.shard_map(
        functools.partial(shards, mesh.shape["beta"], mesh.shape["alpha"]),
        mesh=mesh,
        in_specs=placed,
        out_specs=P(None, "alpha", "beta"),
        check_vma=False,
    )
```

```python
import functools
import math

import jax
import jax.numpy as jnp
from jax import lax
from jax.experimental import pallas as pl
from jax.experimental.pallas import tpu as pltpu
from jax.sharding import PartitionSpec as P

MIB = 1 << 20
STEPS_PER_OCTAVE = 8
SHIFT = 1000
CODE_BITS = 11
LARGEST = 32767.0
TILE = 16
HINTS = (42, 4)
VMEM = 60 * MIB
CORES = 2
ANYWHERE = pl.BlockSpec(memory_space=pl.ANY)


def row_scale(code):
    return jnp.exp2((code - SHIFT).astype(jnp.float32) * (1.0 / STEPS_PER_OCTAVE))


def to_words(values):
    top = jnp.maximum(jnp.max(jnp.abs(values), axis=1, keepdims=True), 2.0 ** -100)
    code = jnp.ceil(jnp.log2(top) * STEPS_PER_OCTAVE + 0.01).astype(jnp.int32) + SHIFT
    words = jnp.round(values * (LARGEST / row_scale(code))).astype(jnp.int32)
    head = words[:, :128]
    lane = lax.broadcasted_iota(jnp.int32, head.shape, 1)
    bit = lax.shift_right_logical(jnp.broadcast_to(code, head.shape), jnp.minimum(lane, CODE_BITS)) & 1
    head = jnp.where(lane < CODE_BITS, (head & -2) | bit, head)
    if words.shape[1] > 128:
        head = jnp.concatenate([head, words[:, 128:]], axis=1)
    return head.astype(jnp.int16)


def bit_weights():
    lane = lax.broadcasted_iota(jnp.int32, (128, 128), 0)
    weight = jnp.where(lane < CODE_BITS, lax.shift_left(jnp.ones_like(lane), jnp.minimum(lane, CODE_BITS)), 0)
    return weight.astype(jnp.float32).astype(jnp.bfloat16)


def from_words(words, weights):
    words = words.astype(jnp.int32)
    bits = (words[:, :128] & 1).astype(jnp.float32).astype(jnp.bfloat16)
    code = jnp.dot(bits, weights, preferred_element_type=jnp.float32)
    scale = jnp.exp2((code - SHIFT) * (1.0 / STEPS_PER_OCTAVE)) * (1.0 / LARGEST)
    if words.shape[1] > 128:
        scale = jnp.concatenate([scale] * (words.shape[1] // 128), axis=1)
    return words.astype(jnp.float32) * scale


def pack_kernel(skip, count, source_ref, *refs):
    out_ref = refs[-1]
    dests = out_ref.shape[0]
    few_rows = source_ref.shape[1] // dests
    for d in range(dests):
        rows = slice(d * few_rows, (d + 1) * few_rows)
        for v in range(count):
            out_ref[d, v * few_rows : (v + 1) * few_rows, :] = source_ref[skip + v, rows, :]
        if len(refs) == 2:
            out_ref[d, count * few_rows :, :] = refs[0][...]


def pack(ci_vectors, heads, first, count, ring):
    vectors, rows, strip = ci_vectors.shape
    few_rows = rows // ring
    taken, at = (count, first // count) if first % count == 0 else (vectors, 0)
    depth = count * few_rows + (0 if heads is None else TILE)
    each = 4
    in_specs = [pl.BlockSpec((taken, each * few_rows, strip), lambda d: (at, d, 0))]
    args = [ci_vectors]
    if heads is not None:
        in_specs.append(pl.BlockSpec((TILE, strip), lambda d: (0, 0)))
        args.append(heads)
    return pl.pallas_call(
        functools.partial(pack_kernel, first - at * taken, count),
        grid=(ring // each,),
        in_specs=in_specs,
        out_specs=pl.BlockSpec((each, depth, strip), lambda d: (d, 0, 0)),
        out_shape=jax.ShapeDtypeStruct((ring, depth, strip), jnp.bfloat16),
        compiler_params=pltpu.CompilerParams(vmem_limit_bytes=VMEM),
        cost_estimate=pl.CostEstimate(flops=0, bytes_accessed=4 * ring * depth * strip, transcendentals=0),
        name="pack_pieces",
    )(*args)


def turn_kernel(place_ref, blocks_ref, out_ref):
    _, count, block, _ = blocks_ref.shape
    for k in range(count):
        out_ref[k * block : (k + 1) * block, :] = blocks_ref[0, k].T


def turn_half(place, stored):
    _, count, block, _ = stored.shape
    return pl.pallas_call(
        turn_kernel,
        grid_spec=pltpu.PrefetchScalarGridSpec(
            num_scalar_prefetch=1,
            grid=(1,),
            in_specs=[pl.BlockSpec((1, count, block, block), lambda g, place_ref: (place_ref[2], 0, 0, 0))],
            out_specs=pl.BlockSpec((count * block, block), lambda g, place_ref: (0, 0)),
        ),
        out_shape=jax.ShapeDtypeStruct((count * block, block), jnp.bfloat16),
        compiler_params=pltpu.CompilerParams(vmem_limit_bytes=VMEM),
        cost_estimate=pl.CostEstimate(flops=0, bytes_accessed=4 * count * block * block, transcendentals=0),
        name="turn_blocks",
    )(place, stored)


def beta_kernel(slots, xs, segments, pieces, cols_ref, place_ref, *refs):
    x_refs = refs[: 2 * len(segments)]
    message_refs = refs[2 * len(segments) : -5]
    out_ref, picked_ref, blocks_ref, picked_sem, blocks_sem = refs[-5:]
    block = blocks_ref.shape[-1]
    sources = x_refs[0].shape[0]
    per_strip = x_refs[0].shape[2] // block
    tiles, _, size, _ = picked_ref.shape
    rows = size * tiles // CORES
    half = blocks_ref.shape[1] // 2
    outer = message_refs[0].shape[0]
    tile, dest = pl.program_id(0), pl.program_id(1)
    core, x_here, parity = place_ref[0], place_ref[1], place_ref[2]

    def fetch_rows(t):
        for w in range(CORES // tiles):
            which = t * (CORES // tiles) + w
            base = 0 if tiles == CORES else (core ^ which) * rows
            for i, (start, count) in enumerate(segments):
                at = pl.multiple_of(base + sum(n for _, n in segments[:i]), TILE)
                for src in range(sources):
                    for s in range(per_strip):
                        pltpu.make_async_copy(
                            x_refs[2 * i + which].at[src, pl.ds(start, count), pl.ds(s * block, block)],
                            picked_ref.at[t, src * per_strip + s, pl.ds(at, count)],
                            picked_sem.at[t],
                        ).start()

    @pl.when((tile == 0) & (dest == 0))
    def _():
        fetch_rows(0)
        for p in range(pieces):
            for z in range(outer):
                for q in range(xs):
                    for r in range(2):
                        d = (p * outer + z) * xs + (x_here ^ q)
                        at = pl.multiple_of((parity ^ r) * half, half)
                        pltpu.make_async_copy(
                            message_refs[(p * xs + q) * 2 + r].at[z],
                            blocks_ref.at[d, pl.ds(at, half)],
                            blocks_sem.at[d],
                        ).start()
        for t in range(1, tiles):
            fetch_rows(t)

    @pl.when(dest == 0)
    def _():
        pltpu.make_async_copy(picked_ref.at[tile], picked_ref.at[tile], picked_sem.at[tile]).wait()

    @pl.when(tile == 0)
    def _():
        pltpu.make_async_copy(blocks_ref.at[dest], blocks_ref.at[dest], blocks_sem.at[dest]).wait()

    strip = dest * CORES + core
    parts = []
    for n in range(per_strip):
        wide = jnp.concatenate(
            [picked_ref[tile, cols_ref[(strip * per_strip + n) * slots + k]] for k in range(slots)], axis=1
        )
        tall = blocks_ref[dest, n * slots * block : (n + 1) * slots * block, :]
        parts.append(jnp.dot(wide, tall, preferred_element_type=jnp.float32))
    term = jnp.concatenate(parts, axis=1) if per_strip > 1 else parts[0]
    out_ref[0] = to_words(term)


def beta_term(slots, xs, columns, place, parts, messages, pieces, hint):
    sources, _, strip = parts[0][0].shape
    outer, half, block = messages[0].shape
    dests = pieces * outer * xs
    segments = [(start, count) for _, _, start, count in parts]
    rows = sum(count for _, count in segments)
    tiles = CORES if rows >= 512 else 1
    size = rows * CORES // tiles
    count = sources * strip // block
    depth = 2 * half
    arrays = [a for own, twin, _, _ in parts for a in (own, twin)] + list(messages)

    def out_at(t, d, cols_ref, place_ref):
        return d, place_ref[0] ^ t if tiles == CORES else 0, 0

    return pl.pallas_call(
        functools.partial(beta_kernel, slots, xs, segments, pieces),
        grid_spec=pltpu.PrefetchScalarGridSpec(
            num_scalar_prefetch=2,
            grid=(tiles, dests),
            in_specs=[ANYWHERE] * len(arrays),
            out_specs=pl.BlockSpec((1, size, strip), out_at),
            scratch_shapes=[
                pltpu.VMEM((tiles, count, size, block), jnp.bfloat16),
                pltpu.VMEM((dests, depth, block), jnp.bfloat16),
                pltpu.SemaphoreType.DMA((tiles,)),
                pltpu.SemaphoreType.DMA((dests,)),
            ],
        ),
        out_shape=jax.ShapeDtypeStruct((dests, rows * CORES, strip), jnp.int16),
        compiler_params=pltpu.CompilerParams(vmem_limit_bytes=VMEM),
        cost_estimate=pl.CostEstimate(
            flops=hint * dests * rows * CORES * strip * slots * block,
            bytes_accessed=2 * depth * block * dests + 4 * count * rows * CORES * block,
            transcendentals=0,
        ),
        name="beta_term",
    )(columns, place, *arrays)


def alpha_kernel(pieces, cols_ref, place_ref, *refs):
    blocks_ref, diag_ref = refs[pieces : pieces + 2]
    out_ref, whole_ref = refs[-2:]
    own_ref = refs[0]
    owned, slots, block, _ = blocks_ref.shape
    rows = own_ref.shape[1]
    for s in range(pieces):
        at = pl.multiple_of(lax.rem(place_ref[3] + s, pieces) * rows, rows)
        whole_ref[pl.ds(at, rows), :] = refs[s][0]

    @pl.loop(0, owned)
    def _(r):
        picked = []
        for k in range(slots):
            at = pl.multiple_of(cols_ref[r * slots + k] * block, block)
            picked.append(whole_ref[pl.ds(at, block), :])
        tall = jnp.concatenate(picked, axis=0)
        wide = jnp.concatenate([blocks_ref[r, k] for k in range(slots)], axis=1)
        term = jnp.dot(wide, tall, preferred_element_type=jnp.float32)
        here = pl.ds(pl.multiple_of(r * block, block), block)
        out_ref[0, here, :] = term + diag_ref[here, :] * own_ref[0, here, :].astype(jnp.float32)


def alpha_term(columns, place, own, others, blocks, diagonal, first, count, base, total, before):
    _, rows, strip = own.shape
    owned, slots, block, _ = blocks.shape
    pieces = 1 + len(others)
    once = pl.Buffered(1)
    mine = pl.BlockSpec((1, rows, strip), lambda v, *_: (first + v, 0, 0))
    in_specs = (
        [mine]
        + [pl.BlockSpec((1, rows, strip), lambda v, *_: (v, 0, 0))] * len(others)
        + [
            pl.BlockSpec(blocks.shape, lambda v, *_: (0, 0, 0, 0), pipeline_mode=once),
            pl.BlockSpec(diagonal.shape, lambda v, *_: (0, 0), pipeline_mode=once),
        ]
    )
    args = [columns, place, own, *others, blocks, diagonal]
    aliases = {}
    if before is not None:
        aliases = {len(args): 0}
        args.append(before)
        in_specs.append(ANYWHERE)
    return pl.pallas_call(
        functools.partial(alpha_kernel, pieces),
        grid_spec=pltpu.PrefetchScalarGridSpec(
            num_scalar_prefetch=2,
            grid=(count,),
            in_specs=in_specs,
            out_specs=pl.BlockSpec((1, rows, strip), lambda v, *_: (first - base + v, 0, 0)),
            scratch_shapes=[pltpu.VMEM((pieces * rows, strip), jnp.bfloat16)],
        ),
        out_shape=jax.ShapeDtypeStruct((total, rows, strip), jnp.float32),
        input_output_aliases=aliases,
        compiler_params=pltpu.CompilerParams(vmem_limit_bytes=VMEM),
        cost_estimate=pl.CostEstimate(
            flops=6 * count * rows * strip * slots * block,
            bytes_accessed=count * rows * strip * (2 * pieces + 4) + blocks.size * 2 + diagonal.size * 4,
            transcendentals=0,
        ),
        name="alpha_term",
    )(*args)


def join_kernel(few_rows, acc_ref, words_ref, *rest):
    out_ref = rest[-1]
    weights = bit_weights()
    for j in range(words_ref.shape[0]):
        for c in range(CORES):
            here = pl.ds((j * CORES + c) * few_rows, few_rows)
            out_ref[0, here, :] = (acc_ref[0, here, :] + from_words(words_ref[j, c, 0], weights)).astype(jnp.bfloat16)


def join(acc, words, first, vectors, before):
    _, rows, strip = acc.shape
    sources = words.shape[0]
    few_rows = rows // (sources * CORES)
    words = words.reshape(sources, CORES, -1, few_rows, strip)
    count = words.shape[2]
    in_specs = [
        pl.BlockSpec((1, rows, strip), lambda v: (first + v, 0, 0)),
        pl.BlockSpec((sources, CORES, 1, few_rows, strip), lambda v: (0, 0, v, 0, 0)),
    ]
    args = [acc, words]
    aliases = {}
    if before is not None:
        in_specs.append(ANYWHERE)
        args.append(before)
        aliases = {2: 0}
    return pl.pallas_call(
        functools.partial(join_kernel, few_rows),
        grid=(count,),
        in_specs=in_specs,
        out_specs=pl.BlockSpec((1, rows, strip), lambda v: (first + v, 0, 0)),
        out_shape=jax.ShapeDtypeStruct((vectors, rows, strip), jnp.bfloat16),
        input_output_aliases=aliases,
        compiler_params=pltpu.CompilerParams(vmem_limit_bytes=VMEM),
        cost_estimate=pl.CostEstimate(
            flops=8 * count * rows * strip, bytes_accessed=8 * count * rows * strip, transcendentals=0
        ),
        name="join_terms",
    )(*args)


def after(value, earlier):
    return lax.optimization_barrier((value, earlier))[0]


def shards(ring, ring_a, ci_vectors, alpha_blocks, alpha_cols, beta_blocks, beta_cols, diagonal):
    vectors, rows, strip = ci_vectors.shape
    few_rows = rows // ring
    owned, slots, block, _ = beta_blocks.shape
    outer = 4
    inner = ring // outer
    xs = inner // CORES
    at_a, at_b = lax.axis_index("alpha"), lax.axis_index("beta")
    parity = lax.rem(at_a, 2)
    place = jnp.stack([lax.rem(at_b, CORES), lax.rem(lax.div(at_b, CORES), xs), parity, at_a]).astype(jnp.int32)
    few = vectors // 4
    cuts = [(vectors - few, few), (0, vectors - few)]
    early = 3 * vectors // 8
    shares = [(0, early), (early, vectors // 2 - early), (vectors // 2, vectors - vectors // 2)]
    sent = [ci_vectors[first : first + count] for first, count in shares]
    pieces = 1

    def swap(value, bit):
        return lax.ppermute(value, "beta", [(i, i ^ bit) for i in range(ring)])

    def across(value):
        return lax.ppermute(value, "alpha", [(i, i ^ 1) for i in range(ring_a)])

    def exchange(value):
        return [
            lax.ppermute(value, "alpha", [((i + s) % ring_a, i) for i in range(ring_a)]) for s in range(1, ring_a)
        ]

    mine = turn_half(place, beta_blocks.reshape(2, owned * slots // 2, block, block))
    far = [[o * inner + i for o in range(outer)] for i in range(inner)]
    gathered = lax.all_gather(mine, "beta", axis=0, tiled=False, axis_index_groups=far)

    heads = jnp.pad(beta_cols.reshape(1, -1).astype(jnp.bfloat16), ((0, TILE - 1), (0, strip - owned * slots)))
    packed = [pack(ci_vectors, heads if i == 0 else None, *cut, ring) for i, cut in enumerate(cuts)]

    others = [exchange(after(sent[0], (packed[1], *sent[1:])))]

    carried = []
    for g in jnp.split(gathered, pieces):
        group, bit = [g], CORES
        while bit < inner:
            group = group + [swap(m, bit) for m in group]
            bit *= 2
        carried += group

    turned = [lax.all_to_all(packed[0], "beta", split_axis=0, concat_axis=0, tiled=True)]
    second = after(packed[1], (turned[0], gathered, others[0][-1]))
    turned.append(lax.all_to_all(second, "beta", split_axis=0, concat_axis=0, tiled=True))
    columns = turned[0][:, cuts[0][1] * few_rows, : owned * slots].reshape(-1).astype(jnp.int32)
    twins = [swap(turned[0], 1)]

    messages = []
    for i, m in enumerate(carried):
        if i == len(carried) - 1:
            m = after(m, (*messages[1::2], twins[0]))
        messages += [m, across(m)]
    for value in sent[1:]:
        others.append(exchange(after(value, messages[-1])))

    acc = None
    for i, share in enumerate(shares):
        acc = alpha_term(
            alpha_cols.reshape(-1), place, ci_vectors, others[i], alpha_blocks, diagonal, *share, 0, vectors, acc
        )

    near = [[j * CORES + c for j in range(ring // CORES)] for c in range(CORES)]

    def send_back(term):
        return lax.all_to_all(term, "beta", split_axis=0, concat_axis=0, tiled=True, axis_index_groups=near)

    def term_of(i):
        parts = [(turned[i], twins[i], 0, cuts[i][1] * few_rows)]
        return beta_term(slots, xs, columns, place, parts, messages, pieces, HINTS[i])

    term = term_of(0)
    twins.append(swap(after(turned[1], term), 1))
    words = [send_back(after(term, turned[1]))]
    words.append(send_back(after(term_of(1), (words[0], others[1][-1]))))

    total = None
    for i, (first, _) in enumerate(cuts):
        total = join(acc, words[i], first, vectors, total)
    return total


def solution(mesh):
    placed = (
        P(None, "alpha", "beta"),
        P("alpha", None, None, None),
        P("alpha", None),
        P("beta", None, None, None),
        P("beta", None),
        P("alpha", "beta"),
    )
    return jax.shard_map(
        functools.partial(shards, mesh.shape["beta"], mesh.shape["alpha"]),
        mesh=mesh,
        in_specs=placed,
        out_specs=P(None, "alpha", "beta"),
        check_vma=False,
    )
```

```python
import functools
import math

import jax
import jax.numpy as jnp
from jax import lax
from jax.experimental import pallas as pl
from jax.experimental.pallas import tpu as pltpu
from jax.sharding import PartitionSpec as P

MIB = 1 << 20
STEPS_PER_OCTAVE = 8
SHIFT = 1000
CODE_BITS = 11
LARGEST = 32767.0
TILE = 16
HINTS = (42, 4)
VMEM = 60 * MIB
CORES = 2
ANYWHERE = pl.BlockSpec(memory_space=pl.ANY)


def row_scale(code):
    return jnp.exp2((code - SHIFT).astype(jnp.float32) * (1.0 / STEPS_PER_OCTAVE))


def to_words(values):
    top = jnp.maximum(jnp.max(jnp.abs(values), axis=1, keepdims=True), 2.0 ** -100)
    code = jnp.ceil(jnp.log2(top) * STEPS_PER_OCTAVE + 0.01).astype(jnp.int32) + SHIFT
    words = jnp.round(values * (LARGEST / row_scale(code))).astype(jnp.int32)
    head = words[:, :128]
    lane = lax.broadcasted_iota(jnp.int32, head.shape, 1)
    bit = lax.shift_right_logical(jnp.broadcast_to(code, head.shape), jnp.minimum(lane, CODE_BITS)) & 1
    head = jnp.where(lane < CODE_BITS, (head & -2) | bit, head)
    if words.shape[1] > 128:
        head = jnp.concatenate([head, words[:, 128:]], axis=1)
    return head.astype(jnp.int16)


def bit_weights():
    lane = lax.broadcasted_iota(jnp.int32, (128, 128), 0)
    weight = jnp.where(lane < CODE_BITS, lax.shift_left(jnp.ones_like(lane), jnp.minimum(lane, CODE_BITS)), 0)
    return weight.astype(jnp.float32).astype(jnp.bfloat16)


def from_words(words, weights):
    words = words.astype(jnp.int32)
    bits = (words[:, :128] & 1).astype(jnp.float32).astype(jnp.bfloat16)
    code = jnp.dot(bits, weights, preferred_element_type=jnp.float32)
    scale = jnp.exp2((code - SHIFT) * (1.0 / STEPS_PER_OCTAVE)) * (1.0 / LARGEST)
    if words.shape[1] > 128:
        scale = jnp.concatenate([scale] * (words.shape[1] // 128), axis=1)
    return words.astype(jnp.float32) * scale


def pack_kernel(skip, count, source_ref, *refs):
    out_ref = refs[-1]
    dests = out_ref.shape[0]
    few_rows = source_ref.shape[1] // dests
    for d in range(dests):
        rows = slice(d * few_rows, (d + 1) * few_rows)
        for v in range(count):
            out_ref[d, v * few_rows : (v + 1) * few_rows, :] = source_ref[skip + v, rows, :]
        if len(refs) == 2:
            out_ref[d, count * few_rows :, :] = refs[0][...]


def pack(ci_vectors, heads, first, count, ring):
    vectors, rows, strip = ci_vectors.shape
    few_rows = rows // ring
    taken, at = (count, first // count) if first % count == 0 else (vectors, 0)
    depth = count * few_rows + (0 if heads is None else TILE)
    each = 4
    in_specs = [pl.BlockSpec((taken, each * few_rows, strip), lambda d: (at, d, 0))]
    args = [ci_vectors]
    if heads is not None:
        in_specs.append(pl.BlockSpec((TILE, strip), lambda d: (0, 0)))
        args.append(heads)
    return pl.pallas_call(
        functools.partial(pack_kernel, first - at * taken, count),
        grid=(ring // each,),
        in_specs=in_specs,
        out_specs=pl.BlockSpec((each, depth, strip), lambda d: (d, 0, 0)),
        out_shape=jax.ShapeDtypeStruct((ring, depth, strip), jnp.bfloat16),
        compiler_params=pltpu.CompilerParams(vmem_limit_bytes=VMEM),
        cost_estimate=pl.CostEstimate(flops=0, bytes_accessed=4 * ring * depth * strip, transcendentals=0),
        name="pack_pieces",
    )(*args)


def turn_kernel(place_ref, blocks_ref, out_ref):
    _, count, block, _ = blocks_ref.shape
    for k in range(count):
        out_ref[k * block : (k + 1) * block, :] = blocks_ref[0, k].T


def turn_half(place, stored):
    _, count, block, _ = stored.shape
    return pl.pallas_call(
        turn_kernel,
        grid_spec=pltpu.PrefetchScalarGridSpec(
            num_scalar_prefetch=1,
            grid=(1,),
            in_specs=[pl.BlockSpec((1, count, block, block), lambda g, place_ref: (place_ref[2], 0, 0, 0))],
            out_specs=pl.BlockSpec((count * block, block), lambda g, place_ref: (0, 0)),
        ),
        out_shape=jax.ShapeDtypeStruct((count * block, block), jnp.bfloat16),
        compiler_params=pltpu.CompilerParams(vmem_limit_bytes=VMEM),
        cost_estimate=pl.CostEstimate(flops=0, bytes_accessed=4 * count * block * block, transcendentals=0),
        name="turn_blocks",
    )(place, stored)


def beta_kernel(slots, xs, segments, pieces, cols_ref, place_ref, *refs):
    x_refs = refs[: 2 * len(segments)]
    message_refs = refs[2 * len(segments) : -5]
    out_ref, picked_ref, blocks_ref, picked_sem, blocks_sem = refs[-5:]
    block = blocks_ref.shape[-1]
    sources = x_refs[0].shape[0]
    per_strip = x_refs[0].shape[2] // block
    tiles, _, size, _ = picked_ref.shape
    rows = size * tiles // CORES
    half = blocks_ref.shape[1] // 2
    outer = message_refs[0].shape[0]
    tile, dest = pl.program_id(0), pl.program_id(1)
    core, x_here, parity = place_ref[0], place_ref[1], place_ref[2]

    def fetch_rows(t):
        for w in range(CORES // tiles):
            which = t * (CORES // tiles) + w
            base = 0 if tiles == CORES else (core ^ which) * rows
            for i, (start, count) in enumerate(segments):
                at = pl.multiple_of(base + sum(n for _, n in segments[:i]), TILE)
                for src in range(sources):
                    for s in range(per_strip):
                        pltpu.make_async_copy(
                            x_refs[2 * i + which].at[src, pl.ds(start, count), pl.ds(s * block, block)],
                            picked_ref.at[t, src * per_strip + s, pl.ds(at, count)],
                            picked_sem.at[t],
                        ).start()

    @pl.when((tile == 0) & (dest == 0))
    def _():
        fetch_rows(0)
        for p in range(pieces):
            for z in range(outer):
                for q in range(xs):
                    for r in range(2):
                        d = (p * outer + z) * xs + (x_here ^ q)
                        at = pl.multiple_of((parity ^ r) * half, half)
                        pltpu.make_async_copy(
                            message_refs[(p * xs + q) * 2 + r].at[z],
                            blocks_ref.at[d, pl.ds(at, half)],
                            blocks_sem.at[d],
                        ).start()
        for t in range(1, tiles):
            fetch_rows(t)

    @pl.when(dest == 0)
    def _():
        pltpu.make_async_copy(picked_ref.at[tile], picked_ref.at[tile], picked_sem.at[tile]).wait()

    @pl.when(tile == 0)
    def _():
        pltpu.make_async_copy(blocks_ref.at[dest], blocks_ref.at[dest], blocks_sem.at[dest]).wait()

    strip = dest * CORES + core
    parts = []
    for n in range(per_strip):
        wide = jnp.concatenate(
            [picked_ref[tile, cols_ref[(strip * per_strip + n) * slots + k]] for k in range(slots)], axis=1
        )
        tall = blocks_ref[dest, n * slots * block : (n + 1) * slots * block, :]
        parts.append(jnp.dot(wide, tall, preferred_element_type=jnp.float32))
    term = jnp.concatenate(parts, axis=1) if per_strip > 1 else parts[0]
    out_ref[0] = to_words(term)


def beta_term(slots, xs, columns, place, parts, messages, pieces, hint):
    sources, _, strip = parts[0][0].shape
    outer, half, block = messages[0].shape
    dests = pieces * outer * xs
    segments = [(start, count) for _, _, start, count in parts]
    rows = sum(count for _, count in segments)
    tiles = CORES if rows >= 512 else 1
    size = rows * CORES // tiles
    count = sources * strip // block
    depth = 2 * half
    arrays = [a for own, twin, _, _ in parts for a in (own, twin)] + list(messages)

    def out_at(t, d, cols_ref, place_ref):
        return d, place_ref[0] ^ t if tiles == CORES else 0, 0

    return pl.pallas_call(
        functools.partial(beta_kernel, slots, xs, segments, pieces),
        grid_spec=pltpu.PrefetchScalarGridSpec(
            num_scalar_prefetch=2,
            grid=(tiles, dests),
            in_specs=[ANYWHERE] * len(arrays),
            out_specs=pl.BlockSpec((1, size, strip), out_at),
            scratch_shapes=[
                pltpu.VMEM((tiles, count, size, block), jnp.bfloat16),
                pltpu.VMEM((dests, depth, block), jnp.bfloat16),
                pltpu.SemaphoreType.DMA((tiles,)),
                pltpu.SemaphoreType.DMA((dests,)),
            ],
        ),
        out_shape=jax.ShapeDtypeStruct((dests, rows * CORES, strip), jnp.int16),
        compiler_params=pltpu.CompilerParams(vmem_limit_bytes=VMEM),
        cost_estimate=pl.CostEstimate(
            flops=hint * dests * rows * CORES * strip * slots * block,
            bytes_accessed=2 * depth * block * dests + 4 * count * rows * CORES * block,
            transcendentals=0,
        ),
        name="beta_term",
    )(columns, place, *arrays)


def alpha_kernel(pieces, cols_ref, place_ref, *refs):
    blocks_ref, diag_ref = refs[pieces : pieces + 2]
    out_ref, whole_ref = refs[-2:]
    own_ref = refs[0]
    owned, slots, block, _ = blocks_ref.shape
    rows = own_ref.shape[1]
    for s in range(pieces):
        at = pl.multiple_of(lax.rem(place_ref[3] + s, pieces) * rows, rows)
        whole_ref[pl.ds(at, rows), :] = refs[s][0]

    @pl.loop(0, owned)
    def _(r):
        picked = []
        for k in range(slots):
            at = pl.multiple_of(cols_ref[r * slots + k] * block, block)
            picked.append(whole_ref[pl.ds(at, block), :])
        tall = jnp.concatenate(picked, axis=0)
        wide = jnp.concatenate([blocks_ref[r, k] for k in range(slots)], axis=1)
        term = jnp.dot(wide, tall, preferred_element_type=jnp.float32)
        here = pl.ds(pl.multiple_of(r * block, block), block)
        out_ref[0, here, :] = term + diag_ref[here, :] * own_ref[0, here, :].astype(jnp.float32)


def alpha_term(columns, place, own, others, blocks, diagonal, first, count, base, total, before):
    _, rows, strip = own.shape
    owned, slots, block, _ = blocks.shape
    pieces = 1 + len(others)
    once = pl.Buffered(1)
    mine = pl.BlockSpec((1, rows, strip), lambda v, *_: (first + v, 0, 0))
    in_specs = (
        [mine]
        + [pl.BlockSpec((1, rows, strip), lambda v, *_: (v, 0, 0))] * len(others)
        + [
            pl.BlockSpec(blocks.shape, lambda v, *_: (0, 0, 0, 0), pipeline_mode=once),
            pl.BlockSpec(diagonal.shape, lambda v, *_: (0, 0), pipeline_mode=once),
        ]
    )
    args = [columns, place, own, *others, blocks, diagonal]
    aliases = {}
    if before is not None:
        aliases = {len(args): 0}
        args.append(before)
        in_specs.append(ANYWHERE)
    return pl.pallas_call(
        functools.partial(alpha_kernel, pieces),
        grid_spec=pltpu.PrefetchScalarGridSpec(
            num_scalar_prefetch=2,
            grid=(count,),
            in_specs=in_specs,
            out_specs=pl.BlockSpec((1, rows, strip), lambda v, *_: (first - base + v, 0, 0)),
            scratch_shapes=[pltpu.VMEM((pieces * rows, strip), jnp.bfloat16)],
        ),
        out_shape=jax.ShapeDtypeStruct((total, rows, strip), jnp.float32),
        input_output_aliases=aliases,
        compiler_params=pltpu.CompilerParams(vmem_limit_bytes=VMEM),
        cost_estimate=pl.CostEstimate(
            flops=6 * count * rows * strip * slots * block,
            bytes_accessed=count * rows * strip * (2 * pieces + 4) + blocks.size * 2 + diagonal.size * 4,
            transcendentals=0,
        ),
        name="alpha_term",
    )(*args)


def join_kernel(few_rows, acc_ref, words_ref, *rest):
    out_ref = rest[-1]
    weights = bit_weights()
    for j in range(words_ref.shape[0]):
        for c in range(CORES):
            here = pl.ds((j * CORES + c) * few_rows, few_rows)
            out_ref[0, here, :] = (acc_ref[0, here, :] + from_words(words_ref[j, c, 0], weights)).astype(jnp.bfloat16)


def join(acc, words, first, vectors, before):
    _, rows, strip = acc.shape
    sources = words.shape[0]
    few_rows = rows // (sources * CORES)
    words = words.reshape(sources, CORES, -1, few_rows, strip)
    count = words.shape[2]
    in_specs = [
        pl.BlockSpec((1, rows, strip), lambda v: (first + v, 0, 0)),
        pl.BlockSpec((sources, CORES, 1, few_rows, strip), lambda v: (0, 0, v, 0, 0)),
    ]
    args = [acc, words]
    aliases = {}
    if before is not None:
        in_specs.append(ANYWHERE)
        args.append(before)
        aliases = {2: 0}
    return pl.pallas_call(
        functools.partial(join_kernel, few_rows),
        grid=(count,),
        in_specs=in_specs,
        out_specs=pl.BlockSpec((1, rows, strip), lambda v: (first + v, 0, 0)),
        out_shape=jax.ShapeDtypeStruct((vectors, rows, strip), jnp.bfloat16),
        input_output_aliases=aliases,
        compiler_params=pltpu.CompilerParams(vmem_limit_bytes=VMEM),
        cost_estimate=pl.CostEstimate(
            flops=8 * count * rows * strip, bytes_accessed=8 * count * rows * strip, transcendentals=0
        ),
        name="join_terms",
    )(*args)


def after(value, earlier):
    return lax.optimization_barrier((value, earlier))[0]


def shards(ring, ring_a, ci_vectors, alpha_blocks, alpha_cols, beta_blocks, beta_cols, diagonal):
    vectors, rows, strip = ci_vectors.shape
    few_rows = rows // ring
    owned, slots, block, _ = beta_blocks.shape
    outer = 4
    inner = ring // outer
    xs = inner // CORES
    at_a, at_b = lax.axis_index("alpha"), lax.axis_index("beta")
    parity = lax.rem(at_a, 2)
    place = jnp.stack([lax.rem(at_b, CORES), lax.rem(lax.div(at_b, CORES), xs), parity, at_a]).astype(jnp.int32)
    few = vectors // 4
    cuts = [(vectors - few, few), (0, vectors - few)]
    early = 3 * vectors // 8
    shares = [(0, early), (early, vectors // 2 - early), (vectors // 2, vectors - vectors // 2)]
    sent = [ci_vectors[first : first + count] for first, count in shares]
    pieces = 1

    def swap(value, bit):
        return lax.ppermute(value, "beta", [(i, i ^ bit) for i in range(ring)])

    def across(value):
        return lax.ppermute(value, "alpha", [(i, i ^ 1) for i in range(ring_a)])

    def exchange(value):
        return [
            lax.ppermute(value, "alpha", [((i + s) % ring_a, i) for i in range(ring_a)]) for s in range(1, ring_a)
        ]

    mine = turn_half(place, beta_blocks.reshape(2, owned * slots // 2, block, block))
    far = [[o * inner + i for o in range(outer)] for i in range(inner)]
    gathered = lax.all_gather(mine, "beta", axis=0, tiled=False, axis_index_groups=far)

    heads = jnp.pad(beta_cols.reshape(1, -1).astype(jnp.bfloat16), ((0, TILE - 1), (0, strip - owned * slots)))
    packed = [pack(ci_vectors, heads if i == 0 else None, *cut, ring) for i, cut in enumerate(cuts)]

    others = [exchange(after(sent[0], packed[1]))]

    carried = []
    for g in jnp.split(gathered, pieces):
        group, bit = [g], CORES
        while bit < inner:
            group = group + [swap(m, bit) for m in group]
            bit *= 2
        carried += group

    turned = [lax.all_to_all(packed[0], "beta", split_axis=0, concat_axis=0, tiled=True)]
    second = after(packed[1], (turned[0], gathered, others[0][-1]))
    turned.append(lax.all_to_all(second, "beta", split_axis=0, concat_axis=0, tiled=True))
    columns = turned[0][:, cuts[0][1] * few_rows, : owned * slots].reshape(-1).astype(jnp.int32)
    twins = [swap(turned[0], 1)]

    messages = []
    for i, m in enumerate(carried):
        if i == len(carried) - 1:
            m = after(m, (*messages[1::2], twins[0]))
        messages += [m, across(m)]
    for value in sent[1:]:
        others.append(exchange(after(value, messages[-1])))

    acc = None
    for i, share in enumerate(shares):
        acc = alpha_term(
            alpha_cols.reshape(-1), place, ci_vectors, others[i], alpha_blocks, diagonal, *share, 0, vectors, acc
        )

    near = [[j * CORES + c for j in range(ring // CORES)] for c in range(CORES)]

    def send_back(term):
        return lax.all_to_all(term, "beta", split_axis=0, concat_axis=0, tiled=True, axis_index_groups=near)

    def term_of(i):
        parts = [(turned[i], twins[i], 0, cuts[i][1] * few_rows)]
        return beta_term(slots, xs, columns, place, parts, messages, pieces, HINTS[i])

    term = term_of(0)
    twins.append(swap(after(turned[1], term), 1))
    words = [send_back(after(term, turned[1]))]
    words.append(send_back(after(term_of(1), (words[0], others[1][-1]))))

    total = None
    for i, (first, _) in enumerate(cuts):
        total = join(acc, words[i], first, vectors, total)
    return total


def solution(mesh):
    placed = (
        P(None, "alpha", "beta"),
        P("alpha", None, None, None),
        P("alpha", None),
        P("beta", None, None, None),
        P("beta", None),
        P("alpha", "beta"),
    )
    return jax.shard_map(
        functools.partial(shards, mesh.shape["beta"], mesh.shape["alpha"]),
        mesh=mesh,
        in_specs=placed,
        out_specs=P(None, "alpha", "beta"),
        check_vma=False,
    )
```

```python
import functools
import math

import jax
import jax.numpy as jnp
from jax import lax
from jax.experimental import pallas as pl
from jax.experimental.pallas import tpu as pltpu
from jax.sharding import PartitionSpec as P

MIB = 1 << 20
STEPS_PER_OCTAVE = 8
SHIFT = 1000
CODE_BITS = 11
LARGEST = 32767.0
TILE = 16
HINTS = (42, 4)
VMEM = 60 * MIB
CORES = 2
ANYWHERE = pl.BlockSpec(memory_space=pl.ANY)


def row_scale(code):
    return jnp.exp2((code - SHIFT).astype(jnp.float32) * (1.0 / STEPS_PER_OCTAVE))


def to_words(values):
    top = jnp.maximum(jnp.max(jnp.abs(values), axis=1, keepdims=True), 2.0 ** -100)
    code = jnp.ceil(jnp.log2(top) * STEPS_PER_OCTAVE + 0.01).astype(jnp.int32) + SHIFT
    words = jnp.round(values * (LARGEST / row_scale(code))).astype(jnp.int32)
    head = words[:, :128]
    lane = lax.broadcasted_iota(jnp.int32, head.shape, 1)
    bit = lax.shift_right_logical(jnp.broadcast_to(code, head.shape), jnp.minimum(lane, CODE_BITS)) & 1
    head = jnp.where(lane < CODE_BITS, (head & -2) | bit, head)
    if words.shape[1] > 128:
        head = jnp.concatenate([head, words[:, 128:]], axis=1)
    return head.astype(jnp.int16)


def bit_weights():
    lane = lax.broadcasted_iota(jnp.int32, (128, 128), 0)
    weight = jnp.where(lane < CODE_BITS, lax.shift_left(jnp.ones_like(lane), jnp.minimum(lane, CODE_BITS)), 0)
    return weight.astype(jnp.float32).astype(jnp.bfloat16)


def from_words(words, weights):
    words = words.astype(jnp.int32)
    bits = (words[:, :128] & 1).astype(jnp.float32).astype(jnp.bfloat16)
    code = jnp.dot(bits, weights, preferred_element_type=jnp.float32)
    scale = jnp.exp2((code - SHIFT) * (1.0 / STEPS_PER_OCTAVE)) * (1.0 / LARGEST)
    if words.shape[1] > 128:
        scale = jnp.concatenate([scale] * (words.shape[1] // 128), axis=1)
    return words.astype(jnp.float32) * scale


def pack_kernel(skip, count, source_ref, *refs):
    out_ref = refs[-1]
    dests = out_ref.shape[0]
    few_rows = source_ref.shape[1] // dests
    for d in range(dests):
        rows = slice(d * few_rows, (d + 1) * few_rows)
        for v in range(count):
            out_ref[d, v * few_rows : (v + 1) * few_rows, :] = source_ref[skip + v, rows, :]
        if len(refs) == 2:
            out_ref[d, count * few_rows :, :] = refs[0][...]


def pack(ci_vectors, heads, first, count, ring):
    vectors, rows, strip = ci_vectors.shape
    few_rows = rows // ring
    taken, at = (count, first // count) if first % count == 0 else (vectors, 0)
    depth = count * few_rows + (0 if heads is None else TILE)
    each = 4
    in_specs = [pl.BlockSpec((taken, each * few_rows, strip), lambda d: (at, d, 0))]
    args = [ci_vectors]
    if heads is not None:
        in_specs.append(pl.BlockSpec((TILE, strip), lambda d: (0, 0)))
        args.append(heads)
    return pl.pallas_call(
        functools.partial(pack_kernel, first - at * taken, count),
        grid=(ring // each,),
        in_specs=in_specs,
        out_specs=pl.BlockSpec((each, depth, strip), lambda d: (d, 0, 0)),
        out_shape=jax.ShapeDtypeStruct((ring, depth, strip), jnp.bfloat16),
        compiler_params=pltpu.CompilerParams(vmem_limit_bytes=VMEM),
        cost_estimate=pl.CostEstimate(flops=0, bytes_accessed=4 * ring * depth * strip, transcendentals=0),
        name="pack_pieces",
    )(*args)


def turn_kernel(place_ref, blocks_ref, out_ref):
    _, count, block, _ = blocks_ref.shape
    for k in range(count):
        out_ref[k * block : (k + 1) * block, :] = blocks_ref[0, k].T


def turn_half(place, stored):
    _, count, block, _ = stored.shape
    return pl.pallas_call(
        turn_kernel,
        grid_spec=pltpu.PrefetchScalarGridSpec(
            num_scalar_prefetch=1,
            grid=(1,),
            in_specs=[pl.BlockSpec((1, count, block, block), lambda g, place_ref: (place_ref[2], 0, 0, 0))],
            out_specs=pl.BlockSpec((count * block, block), lambda g, place_ref: (0, 0)),
        ),
        out_shape=jax.ShapeDtypeStruct((count * block, block), jnp.bfloat16),
        compiler_params=pltpu.CompilerParams(vmem_limit_bytes=VMEM),
        cost_estimate=pl.CostEstimate(flops=0, bytes_accessed=4 * count * block * block, transcendentals=0),
        name="turn_blocks",
    )(place, stored)


def beta_kernel(slots, xs, segments, pieces, cols_ref, place_ref, *refs):
    x_refs = refs[: 2 * len(segments)]
    message_refs = refs[2 * len(segments) : -5]
    out_ref, picked_ref, blocks_ref, picked_sem, blocks_sem = refs[-5:]
    block = blocks_ref.shape[-1]
    sources = x_refs[0].shape[0]
    per_strip = x_refs[0].shape[2] // block
    tiles, _, size, _ = picked_ref.shape
    rows = size * tiles // CORES
    half = blocks_ref.shape[1] // 2
    outer = message_refs[0].shape[0]
    tile, dest = pl.program_id(0), pl.program_id(1)
    core, x_here, parity = place_ref[0], place_ref[1], place_ref[2]

    def fetch_rows(t):
        for w in range(CORES // tiles):
            which = t * (CORES // tiles) + w
            base = 0 if tiles == CORES else (core ^ which) * rows
            for i, (start, count) in enumerate(segments):
                at = pl.multiple_of(base + sum(n for _, n in segments[:i]), TILE)
                for src in range(sources):
                    for s in range(per_strip):
                        pltpu.make_async_copy(
                            x_refs[2 * i + which].at[src, pl.ds(start, count), pl.ds(s * block, block)],
                            picked_ref.at[t, src * per_strip + s, pl.ds(at, count)],
                            picked_sem.at[t],
                        ).start()

    @pl.when((tile == 0) & (dest == 0))
    def _():
        fetch_rows(0)
        for p in range(pieces):
            for z in range(outer):
                for q in range(xs):
                    for r in range(2):
                        d = (p * outer + z) * xs + (x_here ^ q)
                        at = pl.multiple_of((parity ^ r) * half, half)
                        pltpu.make_async_copy(
                            message_refs[(p * xs + q) * 2 + r].at[z],
                            blocks_ref.at[d, pl.ds(at, half)],
                            blocks_sem.at[d],
                        ).start()
        for t in range(1, tiles):
            fetch_rows(t)

    @pl.when(dest == 0)
    def _():
        pltpu.make_async_copy(picked_ref.at[tile], picked_ref.at[tile], picked_sem.at[tile]).wait()

    @pl.when(tile == 0)
    def _():
        pltpu.make_async_copy(blocks_ref.at[dest], blocks_ref.at[dest], blocks_sem.at[dest]).wait()

    strip = dest * CORES + core
    parts = []
    for n in range(per_strip):
        wide = jnp.concatenate(
            [picked_ref[tile, cols_ref[(strip * per_strip + n) * slots + k]] for k in range(slots)], axis=1
        )
        tall = blocks_ref[dest, n * slots * block : (n + 1) * slots * block, :]
        parts.append(jnp.dot(wide, tall, preferred_element_type=jnp.float32))
    term = jnp.concatenate(parts, axis=1) if per_strip > 1 else parts[0]
    out_ref[0] = to_words(term)


def beta_term(slots, xs, columns, place, parts, messages, pieces, hint):
    sources, _, strip = parts[0][0].shape
    outer, half, block = messages[0].shape
    dests = pieces * outer * xs
    segments = [(start, count) for _, _, start, count in parts]
    rows = sum(count for _, count in segments)
    tiles = CORES if rows >= 512 else 1
    size = rows * CORES // tiles
    count = sources * strip // block
    depth = 2 * half
    arrays = [a for own, twin, _, _ in parts for a in (own, twin)] + list(messages)

    def out_at(t, d, cols_ref, place_ref):
        return d, place_ref[0] ^ t if tiles == CORES else 0, 0

    return pl.pallas_call(
        functools.partial(beta_kernel, slots, xs, segments, pieces),
        grid_spec=pltpu.PrefetchScalarGridSpec(
            num_scalar_prefetch=2,
            grid=(tiles, dests),
            in_specs=[ANYWHERE] * len(arrays),
            out_specs=pl.BlockSpec((1, size, strip), out_at),
            scratch_shapes=[
                pltpu.VMEM((tiles, count, size, block), jnp.bfloat16),
                pltpu.VMEM((dests, depth, block), jnp.bfloat16),
                pltpu.SemaphoreType.DMA((tiles,)),
                pltpu.SemaphoreType.DMA((dests,)),
            ],
        ),
        out_shape=jax.ShapeDtypeStruct((dests, rows * CORES, strip), jnp.int16),
        compiler_params=pltpu.CompilerParams(vmem_limit_bytes=VMEM),
        cost_estimate=pl.CostEstimate(
            flops=hint * dests * rows * CORES * strip * slots * block,
            bytes_accessed=2 * depth * block * dests + 4 * count * rows * CORES * block,
            transcendentals=0,
        ),
        name="beta_term",
    )(columns, place, *arrays)


def alpha_kernel(pieces, cols_ref, place_ref, *refs):
    blocks_ref, diag_ref = refs[pieces : pieces + 2]
    out_ref, whole_ref = refs[-2:]
    own_ref = refs[0]
    owned, slots, block, _ = blocks_ref.shape
    rows = own_ref.shape[1]
    for s in range(pieces):
        at = pl.multiple_of(lax.rem(place_ref[3] + s, pieces) * rows, rows)
        whole_ref[pl.ds(at, rows), :] = refs[s][0]

    @pl.loop(0, owned)
    def _(r):
        picked = []
        for k in range(slots):
            at = pl.multiple_of(cols_ref[r * slots + k] * block, block)
            picked.append(whole_ref[pl.ds(at, block), :])
        tall = jnp.concatenate(picked, axis=0)
        wide = jnp.concatenate([blocks_ref[r, k] for k in range(slots)], axis=1)
        term = jnp.dot(wide, tall, preferred_element_type=jnp.float32)
        here = pl.ds(pl.multiple_of(r * block, block), block)
        out_ref[0, here, :] = term + diag_ref[here, :] * own_ref[0, here, :].astype(jnp.float32)


def alpha_term(columns, place, own, others, blocks, diagonal, first, count, base, total, before):
    _, rows, strip = own.shape
    owned, slots, block, _ = blocks.shape
    pieces = 1 + len(others)
    once = pl.Buffered(1)
    mine = pl.BlockSpec((1, rows, strip), lambda v, *_: (first + v, 0, 0))
    in_specs = (
        [mine]
        + [pl.BlockSpec((1, rows, strip), lambda v, *_: (v, 0, 0))] * len(others)
        + [
            pl.BlockSpec(blocks.shape, lambda v, *_: (0, 0, 0, 0), pipeline_mode=once),
            pl.BlockSpec(diagonal.shape, lambda v, *_: (0, 0), pipeline_mode=once),
        ]
    )
    args = [columns, place, own, *others, blocks, diagonal]
    aliases = {}
    if before is not None:
        aliases = {len(args): 0}
        args.append(before)
        in_specs.append(ANYWHERE)
    return pl.pallas_call(
        functools.partial(alpha_kernel, pieces),
        grid_spec=pltpu.PrefetchScalarGridSpec(
            num_scalar_prefetch=2,
            grid=(count,),
            in_specs=in_specs,
            out_specs=pl.BlockSpec((1, rows, strip), lambda v, *_: (first - base + v, 0, 0)),
            scratch_shapes=[pltpu.VMEM((pieces * rows, strip), jnp.bfloat16)],
        ),
        out_shape=jax.ShapeDtypeStruct((total, rows, strip), jnp.float32),
        input_output_aliases=aliases,
        compiler_params=pltpu.CompilerParams(vmem_limit_bytes=VMEM),
        cost_estimate=pl.CostEstimate(
            flops=6 * count * rows * strip * slots * block,
            bytes_accessed=count * rows * strip * (2 * pieces + 4) + blocks.size * 2 + diagonal.size * 4,
            transcendentals=0,
        ),
        name="alpha_term",
    )(*args)


def join_kernel(few_rows, acc_ref, words_ref, *rest):
    out_ref = rest[-1]
    weights = bit_weights()
    for j in range(words_ref.shape[0]):
        for c in range(CORES):
            here = pl.ds((j * CORES + c) * few_rows, few_rows)
            for v in range(out_ref.shape[0]):
                part = from_words(words_ref[j, c, v], weights)
                out_ref[v, here, :] = (acc_ref[v, here, :] + part).astype(jnp.bfloat16)


def join(acc, words, first, vectors, before):
    _, rows, strip = acc.shape
    sources = words.shape[0]
    few_rows = rows // (sources * CORES)
    words = words.reshape(sources, CORES, -1, few_rows, strip)
    count = words.shape[2]
    step = 2 if first % 2 == 0 and count % 2 == 0 else 1
    in_specs = [
        pl.BlockSpec((step, rows, strip), lambda v: (first // step + v, 0, 0)),
        pl.BlockSpec((sources, CORES, step, few_rows, strip), lambda v: (0, 0, v, 0, 0)),
    ]
    args = [acc, words]
    aliases = {}
    if before is not None:
        in_specs.append(ANYWHERE)
        args.append(before)
        aliases = {2: 0}
    return pl.pallas_call(
        functools.partial(join_kernel, few_rows),
        grid=(count // step,),
        in_specs=in_specs,
        out_specs=pl.BlockSpec((step, rows, strip), lambda v: (first // step + v, 0, 0)),
        out_shape=jax.ShapeDtypeStruct((vectors, rows, strip), jnp.bfloat16),
        input_output_aliases=aliases,
        compiler_params=pltpu.CompilerParams(vmem_limit_bytes=VMEM),
        cost_estimate=pl.CostEstimate(
            flops=8 * count * rows * strip, bytes_accessed=8 * count * rows * strip, transcendentals=0
        ),
        name="join_terms",
    )(*args)


def after(value, earlier):
    return lax.optimization_barrier((value, earlier))[0]


def shards(ring, ring_a, ci_vectors, alpha_blocks, alpha_cols, beta_blocks, beta_cols, diagonal):
    vectors, rows, strip = ci_vectors.shape
    few_rows = rows // ring
    owned, slots, block, _ = beta_blocks.shape
    outer = 4
    inner = ring // outer
    xs = inner // CORES
    at_a, at_b = lax.axis_index("alpha"), lax.axis_index("beta")
    parity = lax.rem(at_a, 2)
    place = jnp.stack([lax.rem(at_b, CORES), lax.rem(lax.div(at_b, CORES), xs), parity, at_a]).astype(jnp.int32)
    few = vectors // 4
    cuts = [(vectors - few, few), (0, vectors - few)]
    early = 3 * vectors // 8
    shares = [(0, early), (early, vectors // 2 - early), (vectors // 2, vectors - vectors // 2)]
    sent = [ci_vectors[first : first + count] for first, count in shares]
    pieces = 1

    def swap(value, bit):
        return lax.ppermute(value, "beta", [(i, i ^ bit) for i in range(ring)])

    def across(value):
        return lax.ppermute(value, "alpha", [(i, i ^ 1) for i in range(ring_a)])

    def exchange(value):
        return [
            lax.ppermute(value, "alpha", [((i + s) % ring_a, i) for i in range(ring_a)]) for s in range(1, ring_a)
        ]

    mine = turn_half(place, beta_blocks.reshape(2, owned * slots // 2, block, block))
    far = [[o * inner + i for o in range(outer)] for i in range(inner)]
    gathered = lax.all_gather(mine, "beta", axis=0, tiled=False, axis_index_groups=far)

    heads = jnp.pad(beta_cols.reshape(1, -1).astype(jnp.bfloat16), ((0, TILE - 1), (0, strip - owned * slots)))
    packed = [pack(ci_vectors, heads if i == 0 else None, *cut, ring) for i, cut in enumerate(cuts)]

    others = [exchange(after(sent[0], (packed[1], *sent[1:])))]

    carried = []
    for g in jnp.split(gathered, pieces):
        group, bit = [g], CORES
        while bit < inner:
            group = group + [swap(m, bit) for m in group]
            bit *= 2
        carried += group

    turned = [lax.all_to_all(packed[0], "beta", split_axis=0, concat_axis=0, tiled=True)]
    second = after(packed[1], (turned[0], gathered, others[0][-1]))
    turned.append(lax.all_to_all(second, "beta", split_axis=0, concat_axis=0, tiled=True))
    columns = turned[0][:, cuts[0][1] * few_rows, : owned * slots].reshape(-1).astype(jnp.int32)
    twins = [swap(turned[0], 1)]

    messages = []
    for i, m in enumerate(carried):
        if i == len(carried) - 1:
            m = after(m, (*messages[1::2], twins[0]))
        messages += [m, across(m)]
    for value in sent[1:]:
        others.append(exchange(after(value, messages[-1])))

    acc = None
    for i, share in enumerate(shares):
        acc = alpha_term(
            alpha_cols.reshape(-1), place, ci_vectors, others[i], alpha_blocks, diagonal, *share, 0, vectors, acc
        )

    near = [[j * CORES + c for j in range(ring // CORES)] for c in range(CORES)]

    def send_back(term):
        return lax.all_to_all(term, "beta", split_axis=0, concat_axis=0, tiled=True, axis_index_groups=near)

    def term_of(i):
        parts = [(turned[i], twins[i], 0, cuts[i][1] * few_rows)]
        return beta_term(slots, xs, columns, place, parts, messages, pieces, HINTS[i])

    term = term_of(0)
    twins.append(swap(after(turned[1], term), 1))
    words = [send_back(after(term, turned[1]))]
    words.append(send_back(after(term_of(1), (words[0], others[1][-1]))))

    total = None
    for i, (first, _) in enumerate(cuts):
        total = join(acc, words[i], first, vectors, total)
    return total


def solution(mesh):
    placed = (
        P(None, "alpha", "beta"),
        P("alpha", None, None, None),
        P("alpha", None),
        P("beta", None, None, None),
        P("beta", None),
        P("alpha", "beta"),
    )
    return jax.shard_map(
        functools.partial(shards, mesh.shape["beta"], mesh.shape["alpha"]),
        mesh=mesh,
        in_specs=placed,
        out_specs=P(None, "alpha", "beta"),
        check_vma=False,
    )
```
